32 devices in a mesh: batch: 4 (over x, core), seq: 8 (over z, y).
Axes of the slice: x: 2, y: 2, z: 4, core: 2. Of those that a mesh axis runs over, the one named last changes fastest.
Arguments:
- tokens: bfloat16 [4096, 2048], P(('batch', 'seq')), may hold values from -6 to 6
- ln1_gain: float32 [2048], replicated, may hold values from 0.5 to 1.5
- ln1_bias: float32 [2048], replicated, may hold values from -1 to 1
- w_qkv: bfloat16 [2048, 6144], P(('batch', 'seq')), may hold values from -0.125 to 0.125
- b_qkv: float32 [6144], replicated, may hold values from -1.5 to 1.5
- w_out: bfloat16 [2048, 2048], P(('batch', 'seq')), may hold values from -1 to 1
- b_out: float32 [2048], replicated, may hold values from -1 to 1
- ln2_gain: float32 [2048], replicated, may hold values from 0.5 to 1.5
- ln2_bias: float32 [2048], replicated, may hold values from -1 to 1
- w_gate: bfloat16 [2048, 5461], P(('batch', 'seq')), may hold values from -0.125 to 0.125
- b_gate: float32 [5461], replicated, may hold values from -1.5 to 1.5
- w_up: bfloat16 [2048, 5461], P(('batch', 'seq')), may hold values from -0.125 to 0.125
- b_up: float32 [5461], replicated, may hold values from -1.5 to 1.5
- w_down: bfloat16 [2048, 5461], P(('batch', 'seq')), may hold values from -0.078125 to 0.078125
- b_down: float32 [2048], replicated, may hold values from -1 to 1
- protein_lengths: int32 [4, 6], P('batch'), may hold values from 1 to 898, 1024 in all within a row
- prefix_lengths: int32 [4, 6], P('batch'), may hold values from 1 to 1024
- out_grad: bfloat16 [4096, 2048], P(('batch', 'seq')), may hold values from -6 to 6
Outputs:
- output: bfloat16 [4096, 2048], P(('batch', 'seq'))
- tokens_grad: bfloat16 [4096, 2048], P(('batch', 'seq'))
- ln1_gain_grad: float32 [2048], replicated
- ln1_bias_grad: float32 [2048], replicated
- w_qkv_grad: float32 [2048, 6144], P(('batch', 'seq'))
- b_qkv_grad: float32 [6144], replicated
- w_out_grad: float32 [2048, 2048], P(('batch', 'seq'))
- b_out_grad: float32 [2048], replicated
- ln2_gain_grad: float32 [2048], replicated
- ln2_bias_grad: float32 [2048], replicated
- w_gate_grad: float32 [2048, 5461], P(('batch', 'seq'))
- b_gate_grad: float32 [5461], replicated
- w_up_grad: float32 [2048, 5461], P(('batch', 'seq'))
- b_up_grad: float32 [5461], replicated
- w_down_grad: float32 [2048, 5461], P(('batch', 'seq'))
- b_down_grad: float32 [2048], replicated
The draws below stay inside these ranges and needn't reach their ends.
Inputs may be any that keep to these rules, and one draw needn't show every extreme that they name: `protein_lengths`: each row holds the lengths of the 6 proteins packed in order into one group; a row sums to 1024, and its longest protein has exactly 898 tokens.
All inputs are finite; a program needn't handle non-finite values.
Results may differ from the reference program's by a relative error of at most 0.014.
Values may be sent and summed in bfloat16 or wider, within the bound.
No kernel may reach another device: no remote copies, remote signals or barrier semaphores. Data moves between devices by JAX's collectives and lax.ppermute only.
A program may use at most 704 MiB of HBM per device.

```python
import math
import jax
import jax.numpy as jnp
import numpy as np
from jax import lax

D = 2048
HEADS = 16
HEAD = 128
FF = 5461
TOK_DEV = 128
PROTS = 6
GROUPS = 4
GROUP_TOK = 1024
TOKENS = 4096


def touch_ends(array, own_key, smallest, high):
    longest = array.shape.index(max(array.shape))
    spots = []
    for shift in (0, 1):
        where = [jax.random.randint(jax.random.fold_in(own_key, axis), (), 0, length) for axis, length in enumerate(array.shape)]
        where[longest] = (where[longest] + shift) % array.shape[longest]
        spots.append(tuple(where))
    return array.at[spots[0]].set(smallest).at[spots[1]].set(high)


def raised(entries, own_key, source, target, blocks, factor):
    def block_of(axis_at):
        return (jnp.arange(entries.shape[axis_at]) // (entries.shape[axis_at] // blocks)).reshape((-1,) + (1,) * (entries.ndim - 1 - axis_at))

    one_side = jax.random.permutation(own_key, blocks)[block_of(target)]
    far = (block_of(target) + blocks // 2) % blocks
    return jnp.where((block_of(source) == one_side) | (block_of(source) == far), factor * entries, entries)


def steps_of(key, dims, pieces, least, top_value):
    loudness, own = 1.0, jax.random.fold_in(key, 6)
    for axis_at, parts in pieces:
        steps = jnp.exp(jax.random.uniform(jax.random.fold_in(own, axis_at), (parts,), jnp.float32, least / len(pieces), top_value / len(pieces)))
        loudness = loudness * jnp.repeat(steps, dims[axis_at] // parts).reshape([-1 if axis == axis_at else 1 for axis in range(len(dims))])
    return loudness


def length_profile(number_of, total, reach, skew):
    portions = [(1 << 20) // math.isqrt(grade ** skew) + 1 for grade in range(2, number_of + 1)]
    spare, counts = total - reach - (number_of - 1), [1] * (number_of - 1)
    while spare > 0:
        candidates = [i for i in range(number_of - 1) if counts[i] < reach]
        whole, budget = sum([portions[i] for i in candidates]), spare
        for i in candidates:
            more = min(reach - counts[i], max(1, budget * portions[i] // whole), spare)
            counts[i] = counts[i] + more
            spare = spare - more
    return np.array([reach] + counts)


def ragged_sizes(stream_key, amount, total, reach, lean):
    if amount == 2:
        one = jax.random.randint(stream_key, (), max(1, total - reach), min(reach, total - 1) + 1)
        return jnp.stack([one, total - one])
    sizes = jnp.asarray(length_profile(amount, total, reach, lean), jnp.int32)
    pairs = (amount - 1) // 2
    giver, taker = sizes[1:1 + 2 * pairs:2], sizes[2:2 + 2 * pairs:2]
    margin = jnp.minimum(giver - 1, reach - taker)
    shifted = jax.random.randint(jax.random.fold_in(stream_key, 1), (pairs,), 0, 1 << 20) % (margin + 1)
    sizes = sizes.at[1:1 + 2 * pairs:2].set(giver - shifted).at[2:2 + 2 * pairs:2].set(taker + shifted)
    return sizes[jax.random.permutation(jax.random.fold_in(stream_key, 2), amount)]


def bell_draw(rng, dims, width, reach, cuts=(), kind=jnp.bfloat16):
    drawn = jax.random.normal(rng, dims, jnp.float32) * width
    if len(cuts) > 0:
        drawn = steps_of(rng, dims, cuts, -0.22, 0.18) * drawn
    return jnp.clip(drawn, min=-reach, max=reach).astype(kind)


def gaussian_with(own_key, shape, width, most, pieces, heavy, kind=jnp.bfloat16):
    values = width * jax.random.normal(own_key, shape, jnp.float32)
    if pieces:
        values = values * steps_of(own_key, shape, pieces, -0.22, 0.18)
    return jnp.clip(raised(values, jax.random.fold_in(own_key, 3), *heavy), -most, most).astype(kind)


def setup_inputs(seed: int = 0) -> dict:
    key_of = jax.random.split(jax.random.key(seed), 19)
    return {
        "tokens": bell_draw(key_of[0], (TOKENS, D), 1.0, 6.0, ((0, 32),)),
        "ln1_gain": jnp.clip(1.0 + 0.1 * jax.random.normal(key_of[1], (D,), jnp.float32), 0.5, 1.5),
        "ln1_bias": bell_draw(key_of[2], (D,), 0.2, 1.0, (), jnp.float32),
        "w_qkv": bell_draw(key_of[3], (D, 3 * D), D ** -0.5, 0.125, ((0, 32),)),
        "b_qkv": bell_draw(key_of[4], (3 * D,), 0.3, 1.5, (), jnp.float32),
        "w_out": bell_draw(key_of[5], (D, D), (D // 64) ** -0.5, 1.0, ((0, 32),)),
        "b_out": bell_draw(key_of[6], (D,), 0.2, 1.0, (), jnp.float32),
        "ln2_gain": jnp.clip(1.0 + 0.1 * jax.random.normal(key_of[7], (D,), jnp.float32), 0.5, 1.5),
        "ln2_bias": bell_draw(key_of[8], (D,), 0.2, 1.0, (), jnp.float32),
        "w_gate": bell_draw(key_of[9], (D, FF), D ** -0.5, 0.125, ((0, 32),)),
        "b_gate": bell_draw(key_of[10], (FF,), 0.3, 1.5, (), jnp.float32),
        "w_up": bell_draw(key_of[11], (D, FF), D ** -0.5, 0.125, ((0, 32),)),
        "b_up": bell_draw(key_of[12], (FF,), 0.3, 1.5, (), jnp.float32),
        "w_down": bell_draw(key_of[13], (D, FF), FF ** -0.5, 0.078125, ((0, 32),)),
        "b_down": bell_draw(key_of[14], (D,), 0.2, 1.0, (), jnp.float32),
        "protein_lengths": jax.vmap(lambda own: ragged_sizes(own, PROTS, GROUP_TOK, GROUP_TOK - TOK_DEV + 2, 2))(jax.random.split(key_of[15], GROUPS)).reshape((GROUPS, PROTS)).astype(jnp.int32),
        "prefix_lengths": touch_ends(jax.random.randint(key_of[16], (GROUPS, PROTS), 1, GROUP_TOK + 1), jax.random.fold_in(key_of[16], 1), 1, GROUP_TOK).astype(jnp.int32),
        "out_grad": gaussian_with(key_of[17], (TOKENS, D), 1.0, 6.0, ((0, 32),), (0, 1, 32, 2.75)),
    }


epsilon = 1e-05
masked_value = -1000000000.0
highest = lax.Precision.HIGHEST

@jax.custom_vjp
def low(v):
    return lax.optimization_barrier(v.astype(jnp.bfloat16)).astype(jnp.float32)

@jax.custom_vjp
def low_back(v):
    return v

def low_keep(v):
    return (low(v), None)

def low_pass(kept, grad):
    return (grad,)

def back_keep(v):
    return (v, None)

def back_low(kept, grad):
    return (low(grad),)
low.defvjp(low_keep, low_pass)
low_back.defvjp(back_keep, back_low)

def layer_norm(values, gain, bias):
    average = lax.optimization_barrier(jnp.mean(values, axis=-1, keepdims=True))
    centered = values - average
    spread = lax.optimization_barrier(jnp.mean(centered * centered, axis=-1, keepdims=True))
    return centered * lax.rsqrt(spread + epsilon) * gain + bias

def gelu_tanh(values):
    return 0.5 * values * (1.0 + jnp.tanh(0.7978845608028654 * (values + 0.044715 * values * values * values)))

def group_layout(lengths, prefixes, count):
    ends = jnp.cumsum(lengths).astype(jnp.int32)
    starts = (ends - lengths).astype(jnp.int32)
    places = jnp.arange(count, dtype=jnp.int32)
    member = ((places[:, None] >= starts[None, :]) & (places[:, None] < ends[None, :])).astype(jnp.int32)
    numbers = jnp.arange(lengths.shape[0], dtype=jnp.int32)
    segment = lax.optimization_barrier(jnp.sum(member * numbers[None, :], axis=1)).astype(jnp.int32)
    first = lax.optimization_barrier(jnp.sum(member * starts[None, :], axis=1)).astype(jnp.int32)
    limits = (starts + jnp.minimum(prefixes, lengths)).astype(jnp.int32)
    bound = lax.optimization_barrier(jnp.sum(member * limits[None, :], axis=1)).astype(jnp.int32)
    return (segment, bound, (places - first).astype(jnp.int32))

def rotary_tables(position):
    half_size = HEAD // 2
    rates = jnp.exp(jnp.arange(half_size, dtype=jnp.float32) * (-2.0 * math.log(10000.0) / HEAD))
    angles = position.astype(jnp.float32)[:, None] * rates[None, :]
    cosine = jnp.cos(angles)
    sine = jnp.sin(angles)
    return (jnp.concatenate([cosine, cosine], axis=1), jnp.concatenate([sine, sine], axis=1))

def rotate(values, cosine, sine):
    half_size = values.shape[-1] // 2
    turned = jnp.concatenate([-values[..., half_size:], values[..., :half_size]], axis=-1)
    return values * cosine[:, None, :] + turned * sine[:, None, :]

def allowed_keys(segment, bound, begin, block_rows):
    key_places = jnp.arange(segment.shape[0], dtype=jnp.int32)
    query_places = begin + jnp.arange(block_rows, dtype=jnp.int32)
    query_segment = lax.dynamic_slice_in_dim(segment, begin, block_rows, 0)
    query_bound = lax.dynamic_slice_in_dim(bound, begin, block_rows, 0)
    same = query_segment[:, None] == segment[None, :]
    return same & ((key_places[None, :] <= query_places[:, None]) | (key_places[None, :] < query_bound[:, None]))

def attend_group(queries, keys_all, values_all, segment, bound):
    count = queries.shape[0]
    block_rows = min(512, count)
    scale = HEAD ** (-0.5)

    def one_block(block_index):
        begin = (block_index * block_rows).astype(jnp.int32)
        query_block = lax.dynamic_slice_in_dim(queries, begin, block_rows, 0)
        scores = low_back(jnp.einsum('bhe,khe->hbk', query_block, keys_all, precision=highest) * scale)
        allowed = allowed_keys(segment, bound, begin, block_rows)
        scores = jnp.where(allowed[None], scores, masked_value)
        largest = lax.optimization_barrier(jnp.max(scores, axis=-1, keepdims=True))
        powers = jnp.exp(scores - largest)
        probs = low(powers / lax.optimization_barrier(jnp.sum(powers, axis=-1, keepdims=True)))
        return jnp.einsum('hbk,khe->bhe', probs, values_all, precision=highest)
    blocks = lax.map(jax.checkpoint(one_block), jnp.arange(count // block_rows, dtype=jnp.int32))
    return blocks.reshape(count, queries.shape[1], queries.shape[2])

def reference(tokens, ln1_gain, ln1_bias, w_qkv, b_qkv, w_out, b_out, ln2_gain, ln2_bias, w_gate, b_gate, w_up, b_up, w_down, b_down, protein_lengths, prefix_lengths, out_grad):
    segment, bound, position = jax.vmap(group_layout, in_axes=(0, 0, None))(protein_lengths, prefix_lengths, GROUP_TOK)
    cosine, sine = rotary_tables(position.reshape(-1))

    def attend_all(sent):
        grouped = sent.reshape(GROUPS, GROUP_TOK, 3, HEADS, HEAD)

        def one_group(item):
            packed, group_segment, group_bound = item
            return attend_group(packed[:, 0], packed[:, 1], packed[:, 2], group_segment, group_bound)
        return lax.map(one_group, (grouped, segment, bound)).reshape(TOKENS, D)

    def forward(inputs, gain_one, bias_one, qkv_weight, qkv_bias, out_weight, out_bias, gain_two, bias_two, gate_weight, gate_bias, up_weight, up_bias, down_weight, down_bias):
        normed = low(layer_norm(inputs, gain_one, bias_one))
        raw = low_back(jnp.dot(normed, qkv_weight, precision=highest) + qkv_bias).reshape(TOKENS, 3, HEADS, HEAD)
        turned = jnp.stack([rotate(raw[:, 0], cosine, sine), rotate(raw[:, 1], cosine, sine), raw[:, 2]], axis=1)
        sent = low_back(low(turned))
        attended = low_back(low(attend_all(sent)))
        attn = low_back(jnp.dot(attended, out_weight, precision=highest) + out_bias)
        hidden_in = inputs + attn
        normed_two = low(layer_norm(hidden_in, gain_two, bias_two))
        gate = low_back(jnp.dot(normed_two, gate_weight, precision=highest) + gate_bias)
        upper = low_back(jnp.dot(normed_two, up_weight, precision=highest) + up_bias)
        act = low(gelu_tanh(gate) * upper)
        ffn = low_back(jnp.dot(act, down_weight.T, precision=highest) + down_bias)
        return hidden_in + ffn
    primals = [a.astype(jnp.float32) for a in (tokens, ln1_gain, ln1_bias, w_qkv, b_qkv, w_out, b_out, ln2_gain, ln2_bias, w_gate, b_gate, w_up, b_up, w_down, b_down)]
    result, pullback = jax.vjp(forward, *primals)
    grads = pullback(out_grad.astype(jnp.float32))
    return (result.astype(jnp.bfloat16), grads[0].astype(jnp.bfloat16), grads[1], grads[2], grads[3], grads[4], grads[5], grads[6], grads[7], grads[8], grads[9], grads[10], grads[11], grads[12], grads[13], grads[14])
```

```python
import math

import jax
import jax.numpy as jnp
from jax import lax
from jax.sharding import PartitionSpec as P

HEADS = 16
HEAD = 128
LANES = 128

epsilon = 1e-05
masked_value = -1000000000.0
bf16 = jnp.bfloat16
f32 = jnp.float32


def norm_parts(values):
    average = jnp.mean(values, axis=-1, keepdims=True)
    centered = values - average
    spread = jnp.mean(centered * centered, axis=-1, keepdims=True)
    inverse = lax.rsqrt(spread + epsilon)
    return (centered * inverse, inverse)


def layer_norm(values, gain, bias):
    unit, _ = norm_parts(values)
    return unit * gain + bias


def layer_norm_back(unit, inverse, gain, grad):
    scaled = grad * gain
    first = jnp.mean(scaled, axis=-1, keepdims=True)
    second = jnp.mean(scaled * unit, axis=-1, keepdims=True)
    return inverse * (scaled - first - unit * second)


def gelu_tanh(values):
    return (
        0.5
        * values
        * (1.0 + jnp.tanh(0.7978845608028654 * (values + 0.044715 * values * values * values)))
    )


def geglu(gate, upper):
    return gelu_tanh(gate) * upper


def group_layout(lengths, prefixes, count):
    ends = jnp.cumsum(lengths)
    starts = ends - lengths
    places = jnp.arange(count, dtype=jnp.int32)
    member = ((places[:, None] >= starts[None, :]) & (places[:, None] < ends[None, :])).astype(
        jnp.int32
    )
    numbers = jnp.arange(lengths.shape[0], dtype=jnp.int32)
    segment = jnp.sum(member * numbers[None, :], axis=1)
    first = jnp.sum(member * starts[None, :], axis=1)
    limits = starts + jnp.minimum(prefixes, lengths)
    bound = jnp.sum(member * limits[None, :], axis=1)
    return (segment, bound, places - first)


def rotary_tables(position):
    half_size = HEAD // 2
    rates = jnp.exp(jnp.arange(half_size, dtype=f32) * (-2.0 * math.log(10000.0) / HEAD))
    angles = position.astype(f32)[:, None] * rates[None, :]
    cosine = jnp.cos(angles)
    sine = jnp.sin(angles)
    return (jnp.concatenate([cosine, cosine], axis=1), jnp.concatenate([sine, sine], axis=1))


def rotate(values, cosine, sine):
    half_size = values.shape[-1] // 2
    turned = jnp.concatenate([-values[..., half_size:], values[..., :half_size]], axis=-1)
    return values * cosine[:, None, :] + turned * sine[:, None, :]


def rotate_back(values, cosine, sine):
    half_size = values.shape[-1] // 2
    wave = values * sine[:, None, :]
    turned = jnp.concatenate([wave[..., half_size:], -wave[..., :half_size]], axis=-1)
    return values * cosine[:, None, :] + turned


def dot_nn(left, right):
    return lax.dot_general(left, right, (((1,), (0,)), ((), ())), preferred_element_type=f32)


def dot_nt(left, right):
    return lax.dot_general(left, right, (((1,), (1,)), ((), ())), preferred_element_type=f32)


def dot_tn(left, right):
    return lax.dot_general(left, right, (((0,), (0,)), ((), ())), preferred_element_type=f32)


class Ring:
    def __init__(self, count):
        self.count = count
        rows = 4 if count % 4 == 0 else count
        columns = count // rows
        if columns == 2:
            order = [2 * z for z in range(rows)] + [2 * z + 1 for z in reversed(range(rows))]
        else:
            order = list(range(count))
        self.forward = [(order[i], order[(i + 1) % count]) for i in range(count)]
        self.backward = [(b, a) for a, b in self.forward]
        me = lax.axis_index("seq")
        if columns == 2:
            z, y = me // 2, me % 2
            place = jnp.where(y == 0, z, count - 1 - z)
        else:
            place = me
        self.me = me
        self.at = []
        for k in range(count):
            spot = lax.rem(place + k, count)
            if columns == 2:
                spot = jnp.where(spot < rows, 2 * spot, 2 * (count - 1 - spot) + 1)
            self.at.append(spot)

    def ahead(self, k):
        return self.at[k % self.count]

    def send(self, values, forward):
        return lax.ppermute(values, "seq", self.forward if forward else self.backward)

    def gather(self, block, axis=0):
        count, half_way = self.count, self.count // 2
        size = block.shape[axis]
        shape = list(block.shape)
        shape[axis] = size * count
        total = jnp.zeros(shape, block.dtype)
        half = block.shape[0] // 2

        def put(total, piece, owner, shift=0):
            start = [jnp.int32(0), jnp.int32(0)]
            start[axis] = owner * size
            if shift:
                start[0] = start[0] + shift
            return lax.dynamic_update_slice(total, piece, start)

        total = put(total, block, self.me)
        ahead = behind = block
        for k in range(1, half_way):
            behind = self.send(behind, True)
            ahead = self.send(ahead, False)
            total = put(total, behind, self.ahead(-k))
            total = put(total, ahead, self.ahead(k))
        behind = self.send(behind[:half], True)
        ahead = self.send(ahead[half:], False)
        total = put(total, behind, self.ahead(-half_way))
        total = put(total, ahead, self.ahead(half_way), half)
        return total

    def scatter(self, parts):
        count, half_way = self.count, self.count // 2
        rows, width = parts.shape[0] // count, parts.shape[1]
        half = rows // 2

        def piece(owner, start=0, size=rows):
            return lax.dynamic_slice(
                parts, (owner * rows + start, jnp.int32(0)), (size, width)
            ).astype(f32)

        low, high = piece(self.ahead(half_way), 0, half), piece(self.ahead(half_way), half, half)
        low = self.send(low.astype(bf16), True).astype(f32)
        high = self.send(high.astype(bf16), False).astype(f32)
        nothing = jnp.zeros_like(low)
        forward = jnp.concatenate([low, nothing], axis=0)
        backward = jnp.concatenate([nothing, high], axis=0)
        for k in range(half_way - 1, 0, -1):
            forward = forward + piece(self.ahead(k))
            backward = backward + piece(self.ahead(-k))
            forward = self.send(forward.astype(bf16), True).astype(f32)
            backward = self.send(backward.astype(bf16), False).astype(f32)
        return forward + backward + piece(self.me)


class Mates:
    def __init__(self, count):
        self.count = count
        self.chips = count // 2
        self.me = lax.axis_index("batch")
        self.chip, self.core = self.me // 2, self.me % 2
        self.swap = [(i, i ^ 1) for i in range(count)]

    def gather(self, block):
        rows, width = block.shape
        total = jnp.zeros((self.chips, 2, rows, width), block.dtype)
        zero = jnp.int32(0)

        def put(total, piece, chip, core):
            return lax.dynamic_update_slice(
                total, piece.reshape(1, 1, rows, width), (chip, core, zero, zero)
            )

        mine = [block]
        for step in range(1, self.chips):
            shift = [(i, (i + 2 * step) % self.count) for i in range(self.count)]
            mine.append(lax.ppermute(block, "batch", shift))
        for step, piece in enumerate(mine):
            chip = lax.rem(self.chip - step + self.chips, self.chips)
            total = put(total, piece, chip, self.core)
            total = put(total, lax.ppermute(piece, "batch", self.swap), chip, 1 - self.core)
        return total.reshape(self.count * rows, width)

    def scatter(self, parts):
        rows, width = parts.shape[0] // self.count, parts.shape[1]
        view = parts.reshape(self.chips, 2, rows, width)
        other = lax.dynamic_index_in_dim(view, 1 - self.core, 1, False).astype(bf16)
        kept = lax.dynamic_index_in_dim(view, self.core, 1, False).astype(f32)
        kept = kept + lax.ppermute(other, "batch", self.swap).astype(f32)
        total = lax.dynamic_index_in_dim(kept, self.chip, 0, False)
        for step in range(1, self.chips):
            shift = [(i, (i + 2 * step) % self.count) for i in range(self.count)]
            to = lax.rem(self.chip + step, self.chips)
            sent = lax.dynamic_index_in_dim(kept, to, 0, False).astype(bf16)
            total = total + lax.ppermute(sent, "batch", shift).astype(f32)
        return total


def sum_everywhere(values, batch_count, seq_count):
    for axis, count in (("batch", batch_count), ("seq", seq_count)):
        if count & (count - 1):
            values = lax.psum(values, axis)
            continue
        step = 1
        while step < count:
            values = values + lax.ppermute(values, axis, [(i, i ^ step) for i in range(count)])
            step *= 2
    return values


def allowed_keys(segment, bound):
    places = jnp.arange(segment.shape[0], dtype=jnp.int32)
    same = segment[:, None] == segment[None, :]
    return same & (
        (places[None, :] <= places[:, None]) | (places[None, :] < bound[:, None])
    )


def attend_forward(queries, keys, values, allowed):
    scores = jnp.einsum("qhe,khe->hqk", queries, keys, preferred_element_type=f32) * HEAD ** (-0.5)
    scores = jnp.where(allowed[None], scores, masked_value)
    largest = jnp.max(scores, axis=-1, keepdims=True)
    powers = jnp.exp(scores - largest)
    totals = jnp.sum(powers, axis=-1, keepdims=True)
    probs = (powers / totals).astype(bf16)
    result = jnp.einsum("hqk,khe->qhe", probs, values, preferred_element_type=f32)
    return (result.astype(bf16), largest + jnp.log(totals))


def attend_backward(queries, keys, values, grads, log_sums, allowed):
    scale = HEAD ** (-0.5)
    scores = jnp.einsum("qhe,khe->hqk", queries, keys, preferred_element_type=f32) * scale
    scores = jnp.where(allowed[None], scores, masked_value)
    probs = jnp.exp(scores - log_sums)
    low_probs = probs.astype(bf16)
    grad_probs = jnp.einsum("qhe,khe->hqk", grads, values, preferred_element_type=f32)
    delta = jnp.sum(probs * grad_probs, axis=-1, keepdims=True)
    grad_scores = (probs * (grad_probs - delta)).astype(bf16)
    query_grad = jnp.einsum("hqk,khe->qhe", grad_scores, keys, preferred_element_type=f32) * scale
    key_grad = jnp.einsum("hqk,qhe->khe", grad_scores, queries, preferred_element_type=f32) * scale
    value_grad = jnp.einsum("hqk,qhe->khe", low_probs, grads, preferred_element_type=f32)
    return (query_grad.astype(bf16), key_grad.astype(bf16), value_grad.astype(bf16))


def tile_split(width, count):
    tiles = -(-width // LANES)
    least, extra = divmod(tiles, count)
    sizes = [least + (1 if i < extra else 0) for i in range(count)]
    starts = [sum(sizes[:i]) for i in range(count)]
    return (starts, sizes, max(sizes))


def per_device(
    tokens,
    ln1_gain,
    ln1_bias,
    w_qkv,
    b_qkv,
    w_out,
    b_out,
    ln2_gain,
    ln2_bias,
    w_gate,
    b_gate,
    w_up,
    b_up,
    w_down,
    b_down,
    protein_lengths,
    prefix_lengths,
    out_grad,
):
    seq_count = lax.axis_size("seq")
    batch_count = lax.axis_size("batch")
    own_rows, width = tokens.shape
    weight_rows = w_qkv.shape[0]
    ffn_width = w_gate.shape[1]
    count = own_rows * seq_count
    own_heads = HEADS // seq_count
    own_width = own_heads * HEAD
    ring = Ring(seq_count)
    mates = Mates(batch_count)
    me = ring.me
    zero = jnp.int32(0)

    segment, bound, position = group_layout(protein_lengths[0], prefix_lengths[0], count)
    cosine, sine = rotary_tables(position)
    allowed = allowed_keys(segment, bound)

    def to_columns(blocks):
        moved = lax.all_to_all(blocks, "seq", split_axis=0, concat_axis=0, tiled=True)
        return moved.reshape(seq_count * weight_rows, blocks.shape[2])

    def to_rows(columns):
        blocks = columns.reshape(seq_count, weight_rows, columns.shape[1])
        return lax.all_to_all(blocks, "seq", split_axis=0, concat_axis=0, tiled=True)

    qkv_blocks = (
        w_qkv.reshape(weight_rows, 3, seq_count, own_width)
        .transpose(2, 0, 1, 3)
        .reshape(seq_count, weight_rows, 3 * own_width)
    )
    qkv_own = mates.gather(to_columns(qkv_blocks))
    tokens_all = ring.gather(tokens)
    out_all = mates.gather(ring.gather(w_out))

    starts, sizes, most = tile_split(ffn_width, seq_count)
    own_ffn = most * LANES
    padded = (starts[-1] + most) * LANES

    def ffn_blocks(weight, mask):
        whole = jnp.pad(weight, ((0, 0), (0, padded - ffn_width)))
        pieces = []
        for start, size in zip(starts, sizes):
            piece = whole[:, start * LANES : (start + most) * LANES]
            if mask and size < most:
                piece = jnp.pad(piece[:, : size * LANES], ((0, 0), (0, (most - size) * LANES)))
            pieces.append(piece)
        return jnp.stack(pieces)

    ffn_sent = jnp.concatenate(
        [ffn_blocks(w_gate, False), ffn_blocks(w_up, False), ffn_blocks(w_down, True)], axis=2
    )
    ffn_own = mates.gather(to_columns(ffn_sent))
    gate_up_own = ffn_own[:, : 2 * own_ffn]
    down_own = ffn_own[:, 2 * own_ffn :]
    first_tile = jnp.asarray(starts, jnp.int32)[me] * LANES

    def ffn_bias(bias):
        return lax.dynamic_slice(jnp.pad(bias, (0, padded - ffn_width)), (first_tile,), (own_ffn,))

    inputs = tokens_all.astype(f32)
    normed = layer_norm(inputs, ln1_gain, ln1_bias).astype(bf16)
    qkv_bias = lax.dynamic_slice(
        b_qkv.reshape(3, width), (zero, me * own_width), (3, own_width)
    ).reshape(3 * own_width)
    raw = (dot_nn(normed, qkv_own) + qkv_bias).reshape(count, 3, own_heads, HEAD)
    queries = rotate(raw[:, 0], cosine, sine).astype(bf16)
    keys = rotate(raw[:, 1], cosine, sine).astype(bf16)
    values = raw[:, 2].astype(bf16)
    head_result, log_sums = attend_forward(queries, keys, values, allowed)
    attended = ring.gather(head_result.reshape(count, own_width), axis=1)
    hidden_in = inputs + dot_nn(attended, out_all) + b_out
    hidden_own = lax.dynamic_slice(hidden_in, (me * own_rows, zero), (own_rows, width))

    normed_two = layer_norm(hidden_in, ln2_gain, ln2_bias).astype(bf16)
    gate_up = dot_nn(normed_two, gate_up_own)
    gate = gate_up[:, :own_ffn] + ffn_bias(b_gate)
    upper = gate_up[:, own_ffn:] + ffn_bias(b_up)
    act = geglu(gate, upper).astype(bf16)
    grad_out_all = ring.gather(out_grad)
    grad_act = dot_nn(grad_out_all, down_own)
    _, geglu_pull = jax.vjp(geglu, gate, upper)
    grad_gate, grad_up = geglu_pull(grad_act)
    grad_gate_up = jnp.concatenate([grad_gate.astype(bf16), grad_up.astype(bf16)], axis=1)
    grad_normed_two = ring.scatter(dot_nt(grad_gate_up, gate_up_own).astype(bf16))

    unit_two, inverse_two = norm_parts(hidden_own)
    cotangent = out_grad.astype(f32)
    grad_hidden = cotangent + layer_norm_back(unit_two, inverse_two, ln2_gain, grad_normed_two)
    gain_two_grad = jnp.sum(grad_normed_two * unit_two, axis=0)
    bias_two_grad = jnp.sum(grad_normed_two, axis=0)
    grad_attn = grad_hidden.astype(bf16)
    grad_attn_all = ring.gather(grad_attn)

    out_heads = lax.dynamic_slice(out_all, (me * own_width, zero), (own_width, width))
    grad_attended = dot_nt(grad_attn_all, out_heads).astype(bf16).reshape(count, own_heads, HEAD)
    grad_queries, grad_keys, grad_values = attend_backward(
        queries, keys, values, grad_attended, log_sums, allowed
    )
    grad_raw = jnp.stack(
        [
            rotate_back(grad_queries.astype(f32), cosine, sine).astype(bf16),
            rotate_back(grad_keys.astype(f32), cosine, sine).astype(bf16),
            grad_values,
        ],
        axis=1,
    ).reshape(count, 3 * own_width)
    grad_normed = ring.scatter(dot_nt(grad_raw, qkv_own).astype(bf16))
    unit_one, inverse_one = norm_parts(tokens.astype(f32))
    tokens_grad = (
        grad_hidden + layer_norm_back(unit_one, inverse_one, ln1_gain, grad_normed)
    ).astype(bf16)
    gain_one_grad = jnp.sum(grad_normed * unit_one, axis=0)
    bias_one_grad = jnp.sum(grad_normed, axis=0)

    ffn = ring.scatter(dot_nt(act, down_own).astype(bf16))
    output = (hidden_own + ffn + b_down).astype(bf16)

    ffn_share = mates.scatter(
        jnp.concatenate(
            [
                dot_tn(normed_two, grad_gate_up).astype(bf16),
                dot_tn(grad_out_all, act).astype(bf16),
            ],
            axis=1,
        )
    )
    ffn_rows = to_rows(ffn_share.astype(bf16))

    def ffn_grad(which):
        pieces = [
            ffn_rows[i, :, which * own_ffn : which * own_ffn + sizes[i] * LANES]
            for i in range(seq_count)
        ]
        return jnp.concatenate(pieces, axis=1)[:, :ffn_width].astype(f32)

    out_rows = jnp.concatenate(
        [
            lax.dynamic_slice(
                attended, (zero, (i * seq_count + me) * weight_rows), (count, weight_rows)
            )
            for i in range(batch_count)
        ],
        axis=1,
    )
    out_weight_grad = mates.scatter(dot_tn(out_rows, grad_attn_all).astype(bf16))
    qkv_share = mates.scatter(dot_tn(normed, grad_raw).astype(bf16))
    qkv_rows = to_rows(qkv_share.astype(bf16))
    qkv_weight_grad = (
        qkv_rows.reshape(seq_count, weight_rows, 3, own_width)
        .transpose(1, 2, 0, 3)
        .reshape(weight_rows, 3 * width)
        .astype(f32)
    )

    def spread(values, start, size):
        return lax.dynamic_update_slice(jnp.zeros((size,), f32), values, (start,))

    bias_gate_up = jnp.sum(grad_gate_up.astype(f32), axis=0)
    early = jnp.concatenate(
        [
            jnp.sum(cotangent, axis=0),
            jnp.sum(grad_attn.astype(f32), axis=0),
            gain_two_grad,
            bias_two_grad,
            spread(bias_gate_up[:own_ffn], first_tile, padded),
            spread(bias_gate_up[own_ffn:], first_tile, padded),
        ]
    )
    early = sum_everywhere(early, batch_count, seq_count)
    grad_bias_qkv = jnp.sum(grad_raw.astype(f32), axis=0)
    late = jnp.concatenate(
        [gain_one_grad, bias_one_grad]
        + [
            spread(grad_bias_qkv[i * own_width : (i + 1) * own_width], me * own_width, width)
            for i in range(3)
        ]
    )
    late = sum_everywhere(late, batch_count, seq_count)
    b_down_grad, b_out_grad, gain_two, bias_two = (
        early[i * width : (i + 1) * width] for i in range(4)
    )
    b_gate_grad = early[4 * width : 4 * width + ffn_width]
    b_up_grad = early[4 * width + padded : 4 * width + padded + ffn_width]
    return (
        output,
        tokens_grad,
        late[:width],
        late[width : 2 * width],
        qkv_weight_grad,
        late[2 * width :],
        out_weight_grad,
        b_out_grad,
        gain_two,
        bias_two,
        ffn_grad(0),
        b_gate_grad,
        ffn_grad(1),
        b_up_grad,
        ffn_grad(2),
        b_down_grad,
    )


def solution(mesh):
    rows = P(("batch", "seq"), None)
    in_specs = (
        rows, P(), P(), rows, P(), rows, P(), P(), P(), rows, P(), rows, P(), rows, P(),
        P("batch", None), P("batch", None), rows,
    )
    out_specs = (
        rows, rows, P(), P(), rows, P(), rows, P(), P(), P(), rows, P(), rows, P(), rows, P(),
    )
    return jax.shard_map(
        per_device, mesh=mesh, in_specs=in_specs, out_specs=out_specs, check_vma=False
    )
```

```python
import math

import jax
import jax.numpy as jnp
from jax import lax
from jax.experimental import pallas as pl
from jax.experimental.pallas import tpu as pltpu
from jax.sharding import Mesh
from jax.sharding import PartitionSpec as P

HEADS = 16
HEAD = 128
LANES = 128

epsilon = 1e-05
masked_value = -1000000000.0
log2_e = math.log2(math.e)
bf16 = jnp.bfloat16
f32 = jnp.float32

EVERY = ("x", "core", "z", "y")
GROUP = ("z", "y")
TEAM = ("core", "z")


def norm_parts(values):
    average = jnp.mean(values, axis=-1, keepdims=True)
    centered = values - average
    spread = jnp.mean(centered * centered, axis=-1, keepdims=True)
    inverse = lax.rsqrt(spread + epsilon)
    return (centered * inverse, inverse)


def layer_norm(values, gain, bias):
    unit, _ = norm_parts(values)
    return unit * gain + bias


def layer_norm_back(unit, inverse, gain, grad):
    scaled = grad * gain
    first = jnp.mean(scaled, axis=-1, keepdims=True)
    second = jnp.mean(scaled * unit, axis=-1, keepdims=True)
    return inverse * (scaled - first - unit * second)


def gelu_tanh(values):
    return (
        0.5
        * values
        * (1.0 + jnp.tanh(0.7978845608028654 * (values + 0.044715 * values * values * values)))
    )


def geglu(gate, upper):
    return gelu_tanh(gate) * upper


def group_layout(lengths, prefixes, count):
    ends = jnp.cumsum(lengths)
    starts = ends - lengths
    places = jnp.arange(count, dtype=jnp.int32)
    member = ((places[:, None] >= starts[None, :]) & (places[:, None] < ends[None, :])).astype(
        jnp.int32
    )
    first = jnp.sum(member * starts[None, :], axis=1)
    limits = starts + jnp.minimum(prefixes, lengths)
    bound = jnp.sum(member * limits[None, :], axis=1)
    return (places - first, first, jnp.maximum(places + 1, bound))


def rotary_tables(position):
    half_size = HEAD // 2
    rates = jnp.exp(jnp.arange(half_size, dtype=f32) * (-2.0 * math.log(10000.0) / HEAD))
    angles = position.astype(f32)[:, None] * rates[None, :]
    cosine = jnp.cos(angles)
    sine = jnp.sin(angles)
    return (jnp.concatenate([cosine, cosine], axis=1), jnp.concatenate([-sine, sine], axis=1))


def swap_halves(values):
    half_size = HEAD // 2
    return jnp.concatenate([values[:, half_size:], values[:, :half_size]], axis=1)


def rotate(values, cosine, sine):
    return values * cosine + swap_halves(values) * sine


def rotate_back(values, cosine, sine):
    return values * cosine + swap_halves(values * sine)


def dot_nn(left, right):
    return lax.dot_general(left, right, (((1,), (0,)), ((), ())), preferred_element_type=f32)


def dot_nt(left, right):
    return lax.dot_general(left, right, (((1,), (1,)), ((), ())), preferred_element_type=f32)


def dot_tn(left, right):
    return lax.dot_general(left, right, (((0,), (0,)), ((), ())), preferred_element_type=f32)


def put(total, piece, where):
    return lax.dynamic_update_slice(total, piece, [jnp.int32(i) for i in where])


def cut(values, where, sizes):
    return lax.dynamic_slice(values, [jnp.int32(i) for i in where], sizes)


class Clock:
    def __init__(self):
        self.last = None

    def hold(self, *values):
        if self.last is None:
            return values if len(values) > 1 else values[0]
        held = lax.optimization_barrier((*values, self.last))[:-1]
        return held if len(values) > 1 else held[0]

    def run(self, step, *values):
        held = self.hold(*values)
        out = step(*held) if len(values) > 1 else step(held)
        return self(*out) if isinstance(out, (tuple, list)) else self(out)

    def __call__(self, *values):
        given = values if self.last is None else (*values, self.last)
        out = lax.optimization_barrier(given)
        self.last = out[0]
        out = out[: len(values)]
        return out if len(values) > 1 else out[0]


class Task:
    def __init__(self, name, steps):
        self.name, self.steps = name, steps
        self.result = None
        self.step()

    def step(self):
        with jax.named_scope(self.name):
            try:
                next(self.steps)
            except StopIteration as end:
                self.steps, self.result = None, end.value
        return self

    def finish(self):
        while self.steps is not None:
            self.step()
        return self.result


class Ring:
    def __init__(self, rows, columns, clock):
        count = rows * columns
        self.count = count
        self.clock = clock
        if columns == 2:
            order = [2 * z for z in range(rows)] + [2 * z + 1 for z in reversed(range(rows))]
        else:
            order = list(range(count))
        self.forward = [(order[i], order[(i + 1) % count]) for i in range(count)]
        self.backward = [(b, a) for a, b in self.forward]
        me = lax.axis_index(GROUP)
        if columns == 2:
            place = jnp.where(me % 2 == 0, me // 2, count - 1 - me // 2)
        else:
            place = me
        self.me = me
        self.at = []
        for k in range(count):
            spot = lax.rem(place + k, count)
            if columns == 2:
                spot = jnp.where(spot < rows, 2 * spot, 2 * (count - 1 - spot) + 1)
            self.at.append(spot)

    def ahead(self, k):
        return self.at[k % self.count]

    def send(self, values, forward):
        return lax.ppermute(values, GROUP, self.forward if forward else self.backward)

    def gather(self, block):
        half_way = self.count // 2
        rows, width = block.shape
        half = rows // 2
        block = self.clock.hold(block)
        total = jnp.zeros((self.count * rows, width), block.dtype)
        total = put(total, block, (self.me * rows, 0))
        ahead = behind = block
        for k in range(1, half_way):
            behind, ahead = self.send(behind, True), self.send(ahead, False)
            yield
            behind, ahead = self.clock(behind, ahead)
            total = put(total, behind, (self.ahead(-k) * rows, 0))
            total = put(total, ahead, (self.ahead(k) * rows, 0))
        behind, ahead = self.send(behind[:half], True), self.send(ahead[half:], False)
        yield
        behind, ahead = self.clock(behind, ahead)
        total = put(total, behind, (self.ahead(half_way) * rows, 0))
        return put(total, ahead, (self.ahead(half_way) * rows + half, 0))

    def scatter(self, parts):
        half_way = self.count // 2
        rows, width = parts.shape[0] // self.count, parts.shape[1]
        half = rows // 2
        parts = self.clock.hold(parts)

        def piece(owner, start=0, size=rows):
            return cut(parts, (owner * rows + start, 0), (size, width)).astype(f32)

        low, high = piece(self.ahead(half_way), 0, half), piece(self.ahead(half_way), half, half)
        low, high = self.clock(low.astype(bf16), high.astype(bf16))
        low, high = self.send(low, True), self.send(high, False)
        yield
        low, high = self.clock(low, high)
        nothing = jnp.zeros_like(low)
        forward = jnp.concatenate([low, nothing], axis=0)
        backward = jnp.concatenate([nothing, high], axis=0)
        for k in range(half_way - 1, 0, -1):
            forward = (forward.astype(f32) + piece(self.ahead(k))).astype(bf16)
            backward = (backward.astype(f32) + piece(self.ahead(-k))).astype(bf16)
            forward, backward = self.clock(forward, backward)
            forward, backward = self.send(forward, True), self.send(backward, False)
            yield
            forward, backward = self.clock(forward, backward)
        return forward, backward, piece(self.me)


class Line:
    def __init__(self, count, clock):
        self.count = count
        self.clock = clock
        self.me = lax.axis_index("z")

    def up(self, values, low, high):
        return lax.ppermute(values, "z", [(i, i + 1) for i in range(low, high)])

    def down(self, values, low, high):
        return lax.ppermute(values, "z", [(i + 1, i) for i in range(low, high)])

    def gather(self, block, axis):
        last = self.count - 1
        size = block.shape[axis]
        shape = list(block.shape)
        shape[axis] = size * (self.count + 1)
        block = self.clock.hold(block)
        total = jnp.zeros(shape, block.dtype)

        def put_at(total, piece, owner):
            owner = jnp.where((owner < 0) | (owner > last), self.count, owner)
            return put(total, piece, [owner * size if d == axis else 0 for d in range(2)])

        total = put_at(total, block, self.me)
        below = above = block
        for k in range(last):
            below, above = self.up(below, k, last), self.down(above, 0, last - k)
            yield
            below, above = self.clock(below, above)
            total = put_at(total, below, self.me - k - 1)
            total = put_at(total, above, self.me + k + 1)
        return total

    def scatter(self, parts, before=None):
        last = self.count - 1
        rows, width = parts.shape[0] // self.count, parts.shape[1]
        parts = self.clock.hold(parts)

        def piece(owner):
            return cut(parts, (owner * rows, 0), (rows, width)).astype(f32)

        below = above = None
        for k in range(last, 0, -1):
            upward, downward = piece(self.me + k), piece(self.me - k)
            if below is not None:
                upward, downward = upward + below.astype(f32), downward + above.astype(f32)
            upward, downward = self.clock(upward.astype(bf16), downward.astype(bf16))
            below = self.up(upward, 0, last - k + 1)
            above = self.down(downward, k - 1, last)
            yield
            below, above = self.clock(below, above)
        return below, above, piece(self.me)


def shifts(count):
    return [[(i, (i + step) % count) for i in range(count)] for step in range(1, count)]


def from_axis(value, axis, count):
    me = lax.axis_index(axis)
    return [
        (lax.ppermute(value, axis, pairs), lax.rem(me - step + count, count))
        for step, pairs in enumerate(shifts(count), 1)
    ]


def to_axis(values, axis, count, dim):
    me = lax.axis_index(axis)
    return [
        lax.ppermute(
            lax.dynamic_index_in_dim(values, lax.rem(me + step, count), dim, False), axis, pairs
        )
        for step, pairs in enumerate(shifts(count), 1)
    ]


def in_order(found, axis, count, dim):
    me = lax.axis_index(axis)
    wide = jnp.stack((found[::-1] * 2)[:-1], axis=dim)
    where, sizes = [0] * wide.ndim, list(wide.shape)
    where[dim], sizes[dim] = count - 1 - me, count
    return cut(wide, where, sizes)


def exchange(values, axis, count, dim, clock):
    arrived = to_axis(values, axis, count, dim)
    yield
    found = [own_part(values, axis, dim)] + [clock(value) for value in arrived]
    return in_order(found, axis, count, dim)


def team_exchange(values, nz, clock):
    values = clock.hold(values).reshape(2, nz, *values.shape[1:])
    both = yield from exchange(values, "core", 2, 0, clock)
    out = yield from exchange(both, "z", nz, 1, clock)
    return out.reshape(2 * nz, *values.shape[2:])


def own_part(values, axis, dim):
    return lax.dynamic_index_in_dim(values, lax.axis_index(axis), dim, False)


def add_up(own, others):
    total = own.astype(f32)
    for other in others:
        total = total + other.astype(f32)
    return total.astype(bf16)


class Grid:
    def __init__(self, nx, ny, clock):
        self.nx, self.ny, self.clock = nx, ny, clock
        self.x, self.y = lax.axis_index("x"), lax.axis_index("y")

    def gather(self, block):
        half = block.shape[2] // 2 // LANES * LANES
        block = self.clock.hold(block)
        along_x, along_y = from_axis(block, "x", self.nx), from_axis(block, "y", self.ny)
        yield
        values = self.clock(*[v for v, _ in along_x + along_y])
        along_x, along_y = values[: self.nx - 1], values[self.nx - 1 :]
        left = [[w for w, _ in from_axis(v[..., :half], "y", self.ny)] for v in along_x]
        right = [[w for w, _ in from_axis(v[..., half:], "x", self.nx)] for v in along_y]
        own = in_order([block, *along_y], "y", self.ny, 1)
        yield
        found = [own]
        for i, value in enumerate(along_x):
            corners = [
                jnp.concatenate(self.clock(left[i][j], right[j][i]), axis=2)
                for j in range(self.ny - 1)
            ]
            found.append(in_order([value, *corners], "y", self.ny, 1))
        return [value.reshape(-1, value.shape[-1]) for value in found]

    def place(self, k):
        return lax.rem(self.x - k + self.nx, self.nx)

    def turn(self, values):
        half = values.shape[1] // self.nx
        wide = jnp.concatenate([values, values], axis=1)
        found = [
            cut(wide, (0, self.place(k) * half), (values.shape[0], half)) for k in range(self.nx)
        ]
        return jnp.concatenate(found, axis=1)

    def turn_back(self, values):
        return self.turn(values)

    def scatter(self, x_first, y_first, rows):
        nx, ny = self.nx, self.ny
        count = len(x_first)
        values = self.clock.hold(*x_first, *y_first)
        values = [v.reshape(nx, rows, ny, -1, v.shape[1]) for v in values]
        one, two = values[:count], values[count:]

        def send_x(values):
            return [
                lax.ppermute(values[k], "x", [(i, (i - k) % nx) for i in range(nx)])
                for k in range(1, nx)
            ]

        sent = [send_x(v) for v in one] + [to_axis(v, "y", ny, 2) for v in two]
        yield
        sent = [[self.clock(v) for v in group] for group in sent]
        one = [add_up(v[0], group) for v, group in zip(one, sent)]
        two = [add_up(own_part(v, "y", 2), group) for v, group in zip(two, sent[count:])]
        values = self.clock(*one, *two)
        one, two = values[:count], values[count:]
        sent = [to_axis(v, "y", ny, 1) for v in one] + [send_x(v) for v in two]
        yield
        sent = [[self.clock(v) for v in group] for group in sent]
        one = [add_up(own_part(v, "y", 1), group) for v, group in zip(one, sent)]
        two = [add_up(v[0], group) for v, group in zip(two, sent[count:])]
        return jnp.concatenate([*one, *two], axis=2)


def sum_everywhere(values, sizes, clock):
    values = clock.hold(values)
    for axis, count in sizes:
        if count & (count - 1):
            values = lax.psum(values, axis)
            continue
        step = 1
        while step < count:
            other = lax.ppermute(values, axis, [(i, i ^ step) for i in range(count)])
            yield
            values = values + clock(other)
            step *= 2
    return values


def allowed_keys(low_ref, high_ref, shape):
    places = lax.broadcasted_iota(jnp.int32, shape, 1)
    return (places >= low_ref[...]) & (places < high_ref[...])


def forward_kernel(q_ref, k_ref, v_ref, low_ref, high_ref, out_ref, lse_ref):
    scores = dot_nt(q_ref[...], k_ref[...]) * (HEAD**-0.5 * log2_e)
    allowed = allowed_keys(low_ref, high_ref, scores.shape)
    scores = jnp.where(allowed, scores, masked_value)
    largest = jnp.max(scores, axis=1, keepdims=True)
    powers = jnp.exp2(scores - largest)
    totals = jnp.sum(powers, axis=1, keepdims=True)
    probs = (powers * (1.0 / totals)).astype(bf16)
    out_ref[...] = dot_nn(probs, v_ref[...]).astype(bf16)
    lse_ref[0] = largest + jnp.log2(totals)


def backward_kernel(
    q_ref, k_ref, v_ref, g_ref, low_ref, high_ref, lse_ref, cos_ref, sin_ref, all_cos_ref, all_sin_ref,
    gq_ref, gk_ref, gv_ref, k_sum, v_sum,
):
    scale = HEAD**-0.5
    step = pl.program_id(1)

    @pl.when(step == 0)
    def _():
        k_sum[...] = jnp.zeros_like(k_sum)
        v_sum[...] = jnp.zeros_like(v_sum)

    scores = dot_nt(q_ref[...], k_ref[...]) * (scale * log2_e)
    allowed = allowed_keys(low_ref, high_ref, scores.shape)
    probs = jnp.where(allowed, jnp.exp2(scores - lse_ref[0]), 0.0)
    grad_probs = dot_nt(g_ref[...], v_ref[...])
    delta = jnp.sum(probs * grad_probs, axis=1, keepdims=True)
    grad_scores = (probs * (grad_probs - delta)).astype(bf16)
    grad_q = (dot_nn(grad_scores, k_ref[...]) * scale).astype(bf16).astype(f32)
    gq_ref[...] = rotate_back(grad_q, cos_ref[...], sin_ref[...]).astype(bf16)
    k_sum[...] += dot_tn(grad_scores, q_ref[...])
    v_sum[...] += dot_tn(probs.astype(bf16), g_ref[...])

    @pl.when(step == pl.num_programs(1) - 1)
    def _():
        grad_k = (k_sum[...] * scale).astype(bf16).astype(f32)
        gk_ref[...] = rotate_back(grad_k, all_cos_ref[...], all_sin_ref[...]).astype(bf16)
        gv_ref[...] = v_sum[...].astype(bf16)


params = pltpu.CompilerParams(vmem_limit_bytes=56 * 2**20)
cost = pl.CostEstimate(flops=0, bytes_accessed=0, transcendentals=0)


def attention_specs(count, heads, block):
    def one(column):
        return pl.BlockSpec((block, HEAD), lambda h, i: (i, column + h))

    def whole(column):
        return pl.BlockSpec((count, HEAD), lambda h, i: (0, column + h))

    edge = pl.BlockSpec((block, 1), lambda h, i: (i, 0))
    lse = pl.BlockSpec((1, block, 1), lambda h, i: (h, i, 0))
    return (one, whole, edge, lse)


def attend_forward(packed, low, high):
    count, heads = packed.shape[0], packed.shape[1] // (3 * HEAD)
    block = min(256, count)
    one, whole, edge, lse = attention_specs(count, heads, block)
    return pl.pallas_call(
        forward_kernel,
        grid=(heads, count // block),
        in_specs=[one(0), whole(heads), whole(2 * heads), edge, edge],
        out_specs=[one(0), lse],
        out_shape=[
            jax.ShapeDtypeStruct((count, heads * HEAD), bf16),
            jax.ShapeDtypeStruct((heads, count, 1), f32),
        ],
        compiler_params=params,
        cost_estimate=cost,
        name="attend_forward",
    )(packed, packed, packed, low, high)


def attend_backward(packed, grads, low, high, log_sums, cosine, sine):
    count, heads = packed.shape[0], packed.shape[1] // (3 * HEAD)
    block = min(256, count)
    one, whole, edge, lse = attention_specs(count, heads, block)
    shape = jax.ShapeDtypeStruct((count, heads * HEAD), bf16)
    turn = pl.BlockSpec((block, HEAD), lambda h, i: (i, 0))
    turn_all = pl.BlockSpec((count, HEAD), lambda h, i: (0, 0))
    return pl.pallas_call(
        backward_kernel,
        grid=(heads, count // block),
        in_specs=[one(0), whole(heads), whole(2 * heads), one(0), edge, edge, lse]
        + [turn, turn, turn_all, turn_all],
        out_specs=[one(0), whole(0), whole(0)],
        out_shape=[shape, shape, shape],
        scratch_shapes=[pltpu.VMEM((count, HEAD), f32), pltpu.VMEM((count, HEAD), f32)],
        compiler_params=params,
        cost_estimate=cost,
        name="attend_backward",
    )(packed, packed, packed, grads, low, high, log_sums, cosine, sine, cosine, sine)


def over_rows(name, body, block, rows, whole, outs, sums=(), places=None, scratch=()):
    count = rows[-1].shape[0]
    places = jnp.zeros((1,), jnp.int32) if places is None else places

    def kernel(places_ref, *refs):
        n, m, k = len(rows), len(rows) + len(whole), len(rows) + len(whole) + len(outs)
        if sums:

            @pl.when(pl.program_id(0) == 0)
            def _():
                for ref in refs[k : k + len(sums)]:
                    ref[...] = jnp.zeros_like(ref)

        body(refs[:n], refs[n:m], places_ref, refs[m:k], refs[k:])

    room = [pltpu.VMEM((block, width), kind) for width, kind in scratch]

    def by_row(i, places):
        return (i, 0)

    def fixed(i, places):
        return (0, 0)

    return pl.pallas_call(
        kernel,
        grid_spec=pltpu.PrefetchScalarGridSpec(
            num_scalar_prefetch=1,
            grid=(count // block,),
            in_specs=[
                pl.BlockSpec((block, a.shape[1]), by_row) for a in rows
            ]
            + [pl.BlockSpec(a.shape, fixed) for a in whole],
            out_specs=[pl.BlockSpec((block, width), by_row) for width, _ in outs]
            + [pl.BlockSpec((1, width), fixed) for width in sums],
            scratch_shapes=room,
        ),
        out_shape=[jax.ShapeDtypeStruct((count, width), kind) for width, kind in outs]
        + [jax.ShapeDtypeStruct((1, width), f32) for width in sums],
        compiler_params=params,
        cost_estimate=cost,
        name=name,
    )(places, *rows, *whole)


def columns_of(ref, place, width):
    return ref.at[:, pl.ds(pl.multiple_of(place * width, width), width)]


def project_pieces(left_ref, pieces, places_ref):
    total = None
    for i, piece in enumerate(pieces):
        depth = piece.shape[0]
        term = dot_nn(columns_of(left_ref, places_ref[i], depth)[...], piece[...])
        total = term if total is None else total + term
    return total


def transposed_sums(name, lefts, rights, block=256):
    rights = [r if isinstance(r, (tuple, list)) else [r] for r in rights]
    depth = lefts[0].shape[1]
    block = min(block, depth)
    width = sum(r.shape[1] for r in rights[0])
    flat = [r for group in rights for r in group]

    def kernel(*refs):
        left_refs, right_refs, out_ref = refs[: len(lefts)], refs[len(lefts) : -1], refs[-1]
        per = len(rights[0])
        start = 0
        for j in range(per):
            size = rights[0][j].shape[1]
            total = None
            for i, left in enumerate(left_refs):
                term = dot_tn(left[...], right_refs[i * per + j][...])
                total = term if total is None else total + term
            out_ref[:, start : start + size] = total.astype(bf16)
            start += size

    return pl.pallas_call(
        kernel,
        grid=(depth // block,),
        in_specs=[pl.BlockSpec((a.shape[0], block), lambda i: (0, i)) for a in lefts]
        + [pl.BlockSpec(a.shape, lambda i: (0, 0)) for a in flat],
        out_specs=pl.BlockSpec((block, width), lambda i: (i, 0)),
        out_shape=jax.ShapeDtypeStruct((depth, width), bf16),
        compiler_params=params,
        cost_estimate=cost,
        name=name,
    )(*lefts, *flat)


def times_transposed(name, left, pieces, places, width):
    def body(rows, whole, places_ref, outs, sums):
        for i, piece in enumerate(whole):
            part = dot_nt(rows[0][...], piece[...]).astype(bf16)
            columns_of(outs[0], places_ref[i], piece.shape[0])[...] = part

    (out,) = over_rows(
        name, body, min(256, left.shape[0]), [left], pieces, [(width, bf16)], places=places
    )
    return out


def tile_split(width, count):
    tiles = -(-width // LANES)
    least, extra = divmod(tiles, count)
    sizes = [least + (1 if i < extra else 0) for i in range(count)]
    starts = [sum(sizes[:i]) for i in range(count)]
    return (starts, sizes, max(sizes))


def per_device(
    tokens,
    ln1_gain,
    ln1_bias,
    w_qkv,
    b_qkv,
    w_out,
    b_out,
    ln2_gain,
    ln2_bias,
    w_gate,
    b_gate,
    w_up,
    b_up,
    w_down,
    b_down,
    protein_lengths,
    prefix_lengths,
    out_grad,
):
    nx, nz, ny = (lax.axis_size(axis) for axis in ("x", "z", "y"))
    x, core, z, y = (lax.axis_index(axis) for axis in EVERY)
    sizes_of = (("core", 2), ("x", nx), ("y", ny), ("z", nz))
    own_rows, width = tokens.shape
    weight_rows = w_qkv.shape[0]
    ffn_width = w_gate.shape[1]
    seq_count, team_count = nz * ny, 2 * nz
    count = own_rows * seq_count
    line_rows = nz * own_rows
    own_heads = HEADS // seq_count
    own_width = own_heads * HEAD
    clock = Clock()
    ring = Ring(nz, ny, clock)
    line = Line(nz, clock)
    grid = Grid(nx, ny, clock)
    me = ring.me

    def all_to_all(values, axes):
        return lax.all_to_all(values, axes, split_axis=0, concat_axis=0, tiled=True)

    def other_core(values):
        return lax.ppermute(values, "core", [(0, 1), (1, 0)])

    token_task = Task("tokens", ring.gather(tokens))
    qkv_blocks = (
        w_qkv.reshape(weight_rows, 3, seq_count, own_width)
        .transpose(2, 0, 1, 3)
        .reshape(seq_count, weight_rows, 3 * own_width)
    )
    qkv_moved = all_to_all(qkv_blocks, GROUP)

    starts, sizes, most = tile_split(ffn_width, team_count)
    own_ffn = most * LANES
    padded = (starts[-1] + most) * LANES
    first_tile = jnp.asarray(starts, jnp.int32)[core * nz + z] * LANES

    def ffn_blocks(weight, mask):
        whole = jnp.pad(weight, ((0, 0), (0, padded - ffn_width)))
        pieces = []
        for start, size in zip(starts, sizes):
            piece = whole[:, start * LANES : (start + most) * LANES]
            if mask and size < most:
                piece = jnp.pad(piece[:, : size * LANES], ((0, 0), (0, (most - size) * LANES)))
            pieces.append(piece)
        return jnp.stack(pieces)

    def ffn_bias(bias):
        return cut(jnp.pad(bias, (0, padded - ffn_width)), (first_tile,), (own_ffn,))

    half_places = jnp.stack([lax.rem(x - k + nx, nx) for k in range(nx)])
    places = jnp.concatenate([half_places * 2 + core, half_places * 2 + 1 - core])

    row = lambda values: values.reshape(1, -1)
    token_task.step()
    gate_up_blocks = clock.run(
        lambda gate, up: jnp.concatenate([ffn_blocks(gate, False), ffn_blocks(up, False)], axis=2),
        w_gate,
        w_up,
    )
    token_task.step()
    down_blocks = clock.run(lambda down: ffn_blocks(down, True), w_down)
    qkv_rows = clock(qkv_moved).reshape(seq_count * weight_rows, 3 * own_width)
    from_x = from_axis(qkv_rows, "x", nx)
    out_moved = all_to_all(
        clock.hold(jnp.broadcast_to(w_out[None], (nz, weight_rows, width))), "z"
    )
    token_task.step()

    def tables(lengths, prefixes):
        position, low, high = group_layout(lengths[0], prefixes[0], count)
        return (*rotary_tables(position), low[:, None], high[:, None])

    cosine, sine, low, high = clock.run(tables, protein_lengths, prefix_lengths)
    arrived = [clock(value) for value, _ in from_x]
    qkv_pieces = [qkv_rows, *arrived]
    from_core = [other_core(value) for value in qkv_pieces]
    tokens_all = clock(token_task.finish())
    out_task = Task("w_out", grid.gather(clock(out_moved)))
    gate_up_moved = all_to_all(clock.hold(gate_up_blocks), TEAM)
    qkv_pieces += [clock(value) for value in from_core]
    qkv_bias = cut(b_qkv.reshape(3, width), (0, me * own_width), (3, own_width))

    def first_kernel(rows, whole, places_ref, outs, sums):
        tokens_ref, cos_ref, sin_ref = rows
        gain, bias, qkv_bias, *pieces = whole
        normed_ref, packed_ref = outs
        normed = layer_norm(tokens_ref[...].astype(f32), gain[...], bias[...])
        normed_ref[...] = normed.astype(bf16)
        raw = project_pieces(normed_ref, pieces, places_ref) + qkv_bias[...]
        for i in range(3 * own_heads):
            piece = raw[:, i * HEAD : (i + 1) * HEAD]
            if i < 2 * own_heads:
                piece = rotate(piece, cos_ref[...], sin_ref[...])
            packed_ref[:, i * HEAD : (i + 1) * HEAD] = piece.astype(bf16)

    normed, packed = clock.run(
        lambda tokens_all, *pieces: over_rows(
            "project",
            first_kernel,
            256,
            [tokens_all, cosine, sine],
            [row(ln1_gain), row(ln1_bias), row(qkv_bias), *pieces],
            [(width, bf16), (3 * own_width, bf16)],
            places=places,
        ),
        tokens_all,
        *qkv_pieces,
    )
    head_result, log_sums = clock.run(lambda values: attend_forward(values, low, high), packed)

    head_result = head_result.reshape(nz, ny, own_rows, own_width)
    moved_task = Task("to_y", exchange(head_result, "y", ny, 1, clock))
    moved = moved_task.finish().transpose(0, 2, 1, 3).reshape(line_rows, ny * own_width)
    attended_task = Task("attended", line.gather(clock(moved), 1))
    out_task.step()
    attended_task.step()
    gate_up_moved = clock(gate_up_moved)
    out_pieces = list(clock(*out_task.finish()))
    from_core = [other_core(piece) for piece in out_pieces]
    attended_task.step()
    gate_up_task = Task("gate_up", grid.gather(gate_up_moved))
    down_moved = all_to_all(clock.hold(down_blocks), TEAM)
    inputs_line, out_grad_turned = clock.run(
        lambda values, grads: (
            lax.dynamic_index_in_dim(
                values.reshape(nz, ny, own_rows, width), y, 1, False
            ).reshape(line_rows, width),
            grid.turn(grads),
        ),
        tokens_all,
        out_grad,
    )
    out_pieces = out_pieces + [clock(value) for value in from_core]
    attended = clock(attended_task.finish())
    grad_out_task = Task("out_grad", line.gather(out_grad_turned, 0))

    def second_kernel(rows, whole, places_ref, outs, more):
        tokens_ref, attended_ref = rows
        gain, bias, out_bias, *pieces = whole
        attn = project_pieces(attended_ref, pieces, places_ref) + out_bias[...]
        hidden = tokens_ref[...].astype(f32) + attn
        outs[1][...] = hidden
        (normed_ref,) = more
        normed_ref[...] = layer_norm(hidden, gain[...], bias[...]).astype(bf16)
        part = width // nx
        for k in range(nx):
            place = places_ref[2 * nx + k]
            outs[0][:, k * part : (k + 1) * part] = columns_of(normed_ref, place, part)[...]

    normed_two, hidden_in = clock.run(
        lambda tokens, attended, *pieces: over_rows(
            "second_norm",
            second_kernel,
            min(256, line_rows),
            [tokens, attended],
            [row(ln2_gain), row(ln2_bias), row(b_out), *pieces],
            [(width, bf16), (width, f32)],
            places=jnp.concatenate([places, half_places]),
            scratch=[(width, bf16)],
        ),
        inputs_line,
        attended,
        *out_pieces,
    )
    hidden_own = cut(hidden_in, (z * own_rows, 0), (own_rows, width))
    grad_out_task.step()
    normed_other = other_core(normed_two)
    gate_up_task.step()
    down_moved = clock(down_moved)
    grad_out_task.step()
    gate_up_own = clock(jnp.concatenate(gate_up_task.finish(), axis=0))
    down_task = Task("down", grid.gather(down_moved))
    normed_two = jnp.concatenate([normed_two, clock(normed_other)], axis=0)
    grad_out_line = clock(grad_out_task.finish())[:line_rows]
    grad_out_other = other_core(grad_out_line)

    def first_half(values, weight):
        gate_up = dot_nn(values, weight)
        gate = gate_up[:, :own_ffn] + ffn_bias(b_gate)
        upper = gate_up[:, own_ffn:] + ffn_bias(b_up)
        return gate, upper

    gate, upper = clock.run(first_half, normed_two, gate_up_own)
    down_task.step()
    grad_out_all = clock(jnp.concatenate([grad_out_line, clock(grad_out_other)], axis=0))
    down_own = clock(jnp.concatenate(down_task.finish(), axis=0))

    def first_half_back(grads, weight, gate, upper):
        grad_act = dot_nn(grads, weight)
        act, pull = jax.vjp(geglu, gate, upper)
        return jnp.concatenate([g.astype(bf16) for g in pull(grad_act)], axis=1), act.astype(bf16)

    grad_gate_up, act = clock.run(first_half_back, grad_out_all, down_own, gate, upper)

    def low_nt(left, right):
        return dot_nt(left, right).astype(bf16)

    def low_tn(left, right):
        return dot_tn(left, right).astype(bf16)

    def both_parts(grads, gate_up, act, down):
        return jnp.concatenate([low_nt(grads, gate_up), low_nt(act, down)], axis=1)

    other_parts = other_core(
        clock.run(both_parts, grad_gate_up[line_rows:], gate_up_own, act[line_rows:], down_own)
    )
    own_parts = clock.run(
        both_parts, grad_gate_up[:line_rows], gate_up_own, act[:line_rows], down_own
    )
    parts_task = Task("second_half", line.scatter(clock(add_up(own_parts, [clock(other_parts)]))))
    split = 3 * own_ffn // 2 // LANES * LANES
    first_share = clock.run(low_tn, normed_two, grad_gate_up[:, :split])
    second_share, third_share = clock.run(
        lambda a, b, c, d: (low_tn(a, b[:, split:]), low_tn(c, d)),
        normed_two,
        grad_gate_up,
        grad_out_all,
        act,
    )
    ffn_grad_task = Task(
        "ffn_grad", grid.scatter([first_share], [second_share, third_share], team_count)
    )
    parts_task.step()
    bias_gate_up = clock.run(
        lambda grads: jnp.sum(grads.astype(f32), axis=0), grad_gate_up
    )
    parts_task.step()
    ffn_grad_task.step()
    two_parts = parts_task.finish()

    def second_back_kernel(rows, whole, places_ref, outs, more):
        *sums, _ = more
        more = more[-1:]
        below, above, own, hidden, out_grad_ref = rows
        gain, *pieces = whole
        turned = below[:, :width].astype(f32) + above[:, :width].astype(f32) + own[:, :width]
        (grads_ref,) = more
        part = width // nx
        for k in range(nx):
            columns_of(grads_ref, places_ref[2 * nx + k], part)[...] = turned[:, k * part : (k + 1) * part]
        grads = grads_ref[...]
        unit, inverse = norm_parts(hidden[...])
        cotangent = out_grad_ref[...].astype(f32)
        total = cotangent + layer_norm_back(unit, inverse, gain[...], grads)
        low = total.astype(bf16)
        outs[0][...] = total
        outs[1][...] = low
        for i, piece in enumerate(pieces):
            part = dot_nt(low, piece[...]).astype(bf16)
            columns_of(outs[2], places_ref[i], piece.shape[0])[...] = part
        for ref, values in zip(sums, (grads * unit, grads, low.astype(f32), cotangent)):
            ref[...] += jnp.sum(values, axis=0, keepdims=True)

    grad_hidden, grad_attn, grad_attended, *second_sums = clock.run(
        lambda *values: over_rows(
            "second_norm_back",
            second_back_kernel,
            own_rows,
            values[:5],
            [row(ln2_gain), *values[5:]],
            [(width, f32), (width, bf16), (width, bf16)],
            [width] * 4,
            places=jnp.concatenate([places, half_places]),
            scratch=[(width, f32)],
        ),
        *two_parts,
        hidden_own,
        out_grad,
        *out_pieces,
    )

    grad_heads = all_to_all(
        grad_attended.reshape(own_rows, seq_count, own_width).transpose(1, 0, 2), GROUP
    )
    grad_heads = clock(grad_heads).reshape(count, own_width)
    ffn_share = clock(ffn_grad_task.finish())
    ffn_back = all_to_all(ffn_share, TEAM)
    grad_parts = clock.run(
        lambda *values: attend_backward(*values, low, high, log_sums, cosine, sine),
        packed,
        grad_heads,
    )

    def first_back_kernel(rows, whole, places_ref, outs, more):
        *sums, part_ref = more
        grads, tokens_ref = rows[:3], rows[3]
        unit, _ = norm_parts(tokens_ref[...].astype(f32))
        for i, piece in enumerate(whole):
            part = None
            for j, grad in enumerate(grads):
                term = dot_nt(grad[...], piece[:, j * own_width : (j + 1) * own_width])
                part = term if part is None else part + term
            depth = piece.shape[0]
            columns_of(outs[0], places_ref[i], depth)[...] = part.astype(bf16)
            columns_of(part_ref, places_ref[i], depth)[...] = part
        part = part_ref[...]
        sums[0][...] += jnp.sum(part * unit, axis=0, keepdims=True)
        sums[1][...] += jnp.sum(part, axis=0, keepdims=True)
        for j, grad in enumerate(grads):
            total = jnp.sum(grad[...].astype(f32), axis=0, keepdims=True)
            sums[2][:, j * own_width : (j + 1) * own_width] += total

    normed_part, *first_sums = clock.run(
        lambda *values: over_rows(
            "first_norm_back",
            first_back_kernel,
            256,
            values[:4],
            values[4:],
            [(width, bf16)],
            [width, width, 3 * own_width],
            places=places,
            scratch=[(width, f32)],
        ),
        *grad_parts,
        tokens_all,
        *qkv_pieces,
    )
    one_task = Task("grad_normed", ring.scatter(normed_part))

    def spread(values, start, size):
        return put(jnp.zeros((size,), f32), values, (start,))

    def gather_small(bias_gate_up, *sums):
        bias_qkv = sums[-1][0]
        small = [value[0] for value in sums[:-1]]
        small += [
            spread(bias_qkv[i * own_width : (i + 1) * own_width], me * own_width, width)
            for i in range(3)
        ]
        small += [
            spread(bias_gate_up[:own_ffn], first_tile, padded),
            spread(bias_gate_up[own_ffn:], first_tile, padded),
        ]
        return jnp.concatenate(small)

    small = clock.run(gather_small, bias_gate_up, *second_sums, *first_sums)
    small_task = Task("small", sum_everywhere(small, sizes_of, clock))
    qkv_share = clock.run(
        lambda a, b, c, d: low_tn(a, jnp.concatenate([b, c, d], axis=1)), normed, *grad_parts
    )
    qkv_share = qkv_share.reshape(nx, 2, seq_count * weight_rows, 3 * own_width)
    qkv_core = to_axis(qkv_share, "core", 2, 1)
    ffn_back = clock(ffn_back)
    one_task.step()
    grad_attn_task = Task(
        "grad_attn",
        exchange(grad_attn.reshape(own_rows, nz, width // nz).transpose(1, 0, 2), "z", nz, 0, clock),
    )
    qkv_share = clock(add_up(own_part(qkv_share, "core", 1), [clock(v) for v in qkv_core]))
    qkv_x = to_axis(qkv_share, "x", nx, 0)
    small_task.step()
    one_task.step()
    grad_attn_block = clock(grad_attn_task.finish()).reshape(line_rows, width // nz)
    out_share = clock.run(lambda a, b: low_tn(a[:, :width], b), attended, grad_attn_block)
    out_share = out_share.reshape(nx, 2, nz, ny, weight_rows, width // nz)
    out_core = to_axis(out_share, "core", 2, 1)
    small_task.step()
    qkv_share = clock(add_up(own_part(qkv_share, "x", 0), [clock(v) for v in qkv_x]))
    qkv_back = all_to_all(qkv_share.reshape(seq_count, weight_rows, 3 * own_width), GROUP)
    out_share = clock(add_up(own_part(out_share, "core", 1), [clock(v) for v in out_core]))
    out_x = to_axis(out_share, "x", nx, 0)
    one_task.step()
    small_task.step()
    output = clock.run(
        lambda below, above, own, hidden: (
            grid.turn_back(
                below[:, width:].astype(f32) + above[:, width:].astype(f32) + own[:, width:]
            )
            + hidden
            + b_down
        ).astype(bf16),
        *two_parts,
        hidden_own,
    )
    out_share = clock(add_up(own_part(out_share, "x", 0), [clock(v) for v in out_x]))
    out_y = to_axis(out_share, "y", ny, 1)
    one_parts = one_task.finish()
    small_task.step()
    out_share = clock(add_up(own_part(out_share, "y", 1), [clock(v) for v in out_y]))
    out_back = Task("out_grad", exchange(out_share, "z", nz, 0, clock))

    def last_kernel(rows, whole, places_ref, outs, sums):
        below, above, own, tokens_ref, hidden_grad = rows
        grads = below[...].astype(f32) + above[...].astype(f32) + own[...]
        unit, inverse = norm_parts(tokens_ref[...].astype(f32))
        total = hidden_grad[...] + layer_norm_back(unit, inverse, whole[0][...], grads)
        outs[0][...] = total.astype(bf16)

    tokens_grad = clock.run(
        lambda *values: over_rows(
            "first_norm_tokens",
            last_kernel,
            own_rows,
            values,
            [row(ln1_gain)],
            [(width, bf16)],
        )[0],
        *one_parts,
        tokens,
        grad_hidden,
    )
    small = small_task.finish()
    out_back = out_back.finish()

    def ffn_rows(moved, begin):
        pieces = [moved[i, :, begin : begin + sizes[i] * LANES] for i in range(team_count)]
        return jnp.concatenate(pieces, axis=1)[:, :ffn_width].astype(f32)

    out_weight_grad = (
        out_back.transpose(1, 0, 2).reshape(weight_rows, width).astype(f32)
    )
    qkv_weight_grad = (
        clock(qkv_back)
        .reshape(seq_count, weight_rows, 3, own_width)
        .transpose(1, 2, 0, 3)
        .reshape(weight_rows, 3 * width)
        .astype(f32)
    )
    gain_two, bias_two, b_out_grad, b_down_grad, gain_one, bias_one = (
        small[i * width : (i + 1) * width] for i in range(6)
    )
    b_qkv_grad = small[6 * width : 9 * width]
    b_gate_grad = small[9 * width : 9 * width + ffn_width]
    b_up_grad = small[9 * width + padded : 9 * width + padded + ffn_width]
    return (
        output,
        tokens_grad,
        gain_one,
        bias_one,
        qkv_weight_grad,
        b_qkv_grad,
        out_weight_grad,
        b_out_grad,
        gain_two,
        bias_two,
        ffn_rows(ffn_back, 0),
        b_gate_grad,
        ffn_rows(ffn_back, own_ffn),
        b_up_grad,
        ffn_rows(ffn_back, 2 * own_ffn),
        b_down_grad,
    )


def solution(mesh):
    nx, seq_count = mesh.shape["batch"] // 2, mesh.shape["seq"]
    nz = 4 if seq_count % 4 == 0 else seq_count
    grid = Mesh(mesh.devices.reshape(nx, 2, nz, seq_count // nz), EVERY)
    rows = P(EVERY, None)
    lengths = P(("x", "core"), None)
    in_specs = (
        rows, P(), P(), rows, P(), rows, P(), P(), P(), rows, P(), rows, P(), rows, P(),
        lengths, lengths, rows,
    )
    out_specs = (
        rows, rows, P(), P(), rows, P(), rows, P(), P(), P(), rows, P(), rows, P(), rows, P(),
    )
    return jax.shard_map(
        per_device, mesh=grid, in_specs=in_specs, out_specs=out_specs, check_vma=False
    )
```

```python
import math

import jax
import jax.numpy as jnp
from jax import lax
from jax.experimental import pallas as pl
from jax.experimental.pallas import tpu as pltpu
from jax.sharding import Mesh
from jax.sharding import PartitionSpec as P

HEADS = 16
HEAD = 128
LANES = 128
PIECES = 4

epsilon = 1e-05
masked_value = -1000000000.0
log2_e = math.log2(math.e)
bf16 = jnp.bfloat16
f32 = jnp.float32

EVERY = ("x", "core", "z", "y")
GROUP = ("z", "y")
TEAM = ("core", "z")


def norm_parts(values):
    average = jnp.mean(values, axis=-1, keepdims=True)
    centered = values - average
    spread = jnp.mean(centered * centered, axis=-1, keepdims=True)
    inverse = lax.rsqrt(spread + epsilon)
    return (centered * inverse, inverse)


def layer_norm(values, gain, bias):
    unit, _ = norm_parts(values)
    return unit * gain + bias


def layer_norm_back(unit, inverse, gain, grad):
    scaled = grad * gain
    first = jnp.mean(scaled, axis=-1, keepdims=True)
    second = jnp.mean(scaled * unit, axis=-1, keepdims=True)
    return inverse * (scaled - first - unit * second)


def gelu_tanh(values):
    return (
        0.5
        * values
        * (1.0 + jnp.tanh(0.7978845608028654 * (values + 0.044715 * values * values * values)))
    )


def geglu(gate, upper):
    return gelu_tanh(gate) * upper


def group_layout(lengths, prefixes, count):
    ends = jnp.cumsum(lengths)
    starts = ends - lengths
    places = jnp.arange(count, dtype=jnp.int32)
    member = ((places[:, None] >= starts[None, :]) & (places[:, None] < ends[None, :])).astype(
        jnp.int32
    )
    first = jnp.sum(member * starts[None, :], axis=1)
    limits = starts + jnp.minimum(prefixes, lengths)
    bound = jnp.sum(member * limits[None, :], axis=1)
    return (places - first, first, jnp.maximum(places + 1, bound))


def rotary_tables(position):
    half_size = HEAD // 2
    rates = jnp.exp(jnp.arange(half_size, dtype=f32) * (-2.0 * math.log(10000.0) / HEAD))
    angles = position.astype(f32)[:, None] * rates[None, :]
    cosine = jnp.cos(angles)
    sine = jnp.sin(angles)
    return (jnp.concatenate([cosine, cosine], axis=1), jnp.concatenate([-sine, sine], axis=1))


def swap_halves(values):
    half_size = HEAD // 2
    return jnp.concatenate([values[:, half_size:], values[:, :half_size]], axis=1)


def rotate(values, cosine, sine):
    return values * cosine + swap_halves(values) * sine


def rotate_back(values, cosine, sine):
    return values * cosine + swap_halves(values * sine)


def dot_nn(left, right):
    return lax.dot_general(left, right, (((1,), (0,)), ((), ())), preferred_element_type=f32)


def dot_nt(left, right):
    return lax.dot_general(left, right, (((1,), (1,)), ((), ())), preferred_element_type=f32)


def dot_tn(left, right):
    return lax.dot_general(left, right, (((0,), (0,)), ((), ())), preferred_element_type=f32)


def put(total, piece, where):
    return lax.dynamic_update_slice(total, piece, [jnp.int32(i) for i in where])


def cut(values, where, sizes):
    return lax.dynamic_slice(values, [jnp.int32(i) for i in where], sizes)


class Clock:
    def __init__(self):
        self.last = None

    def hold(self, *values):
        if self.last is None:
            return values if len(values) > 1 else values[0]
        held = lax.optimization_barrier((*values, self.last))[:-1]
        return held if len(values) > 1 else held[0]

    def run(self, step, *values):
        held = self.hold(*values)
        out = step(*held) if len(values) > 1 else step(held)
        return self(*out) if isinstance(out, (tuple, list)) else self(out)

    def __call__(self, *values):
        given = values if self.last is None else (*values, self.last)
        out = lax.optimization_barrier(given)
        self.last = out[0]
        out = out[: len(values)]
        return out if len(values) > 1 else out[0]


class Plan:
    def __init__(self):
        self.steps, self.transfers, self.running = {}, {}, {}

    def step(self, function):
        self.steps[function.__name__] = function
        return function

    def transfer(self, function):
        self.transfers[function.__name__] = function
        return function

    def run(self, order):
        for i, name in enumerate(order):
            with jax.named_scope(name):
                if name in self.steps:
                    self.steps[name]()
                    continue
                if name not in self.running:
                    self.running[name] = self.transfers[name]()
                if name in order[i + 1 :]:
                    next(self.running[name], None)
                    continue
                for _ in self.running[name]:
                    pass


class Ring:
    def __init__(self, rows, columns, clock):
        count = rows * columns
        self.count = count
        self.clock = clock
        if columns == 2:
            order = [2 * z for z in range(rows)] + [2 * z + 1 for z in reversed(range(rows))]
        else:
            order = list(range(count))
        self.forward = [(order[i], order[(i + 1) % count]) for i in range(count)]
        self.backward = [(b, a) for a, b in self.forward]
        me = lax.axis_index(GROUP)
        if columns == 2:
            place = jnp.where(me % 2 == 0, me // 2, count - 1 - me // 2)
        else:
            place = me
        self.me = me
        self.at = []
        for k in range(count):
            spot = lax.rem(place + k, count)
            if columns == 2:
                spot = jnp.where(spot < rows, 2 * spot, 2 * (count - 1 - spot) + 1)
            self.at.append(spot)

    def ahead(self, k):
        return self.at[k % self.count]

    def send(self, values, forward):
        return lax.ppermute(values, GROUP, self.forward if forward else self.backward)

    def gather(self, block):
        half_way = self.count // 2
        rows, width = block.shape
        half = rows // 2
        block = self.clock.hold(block)
        total = jnp.zeros((self.count * rows, width), block.dtype)
        total = put(total, block, (self.me * rows, 0))
        ahead = behind = block
        for k in range(1, half_way):
            behind, ahead = self.send(behind, True), self.send(ahead, False)
            yield
            behind, ahead = self.clock(behind, ahead)
            total = put(total, behind, (self.ahead(-k) * rows, 0))
            total = put(total, ahead, (self.ahead(k) * rows, 0))
        behind, ahead = self.send(behind[:half], True), self.send(ahead[half:], False)
        yield
        behind, ahead = self.clock(behind, ahead)
        total = put(total, behind, (self.ahead(half_way) * rows, 0))
        return put(total, ahead, (self.ahead(half_way) * rows + half, 0))

    def scatter(self, parts):
        half_way = self.count // 2
        rows, width = parts.shape[0] // self.count, parts.shape[1]
        half = rows // 2
        parts = self.clock.hold(parts)

        def piece(owner, start=0, size=rows):
            return cut(parts, (owner * rows + start, 0), (size, width)).astype(f32)

        low, high = piece(self.ahead(half_way), 0, half), piece(self.ahead(half_way), half, half)
        low, high = self.clock(low.astype(bf16), high.astype(bf16))
        low, high = self.send(low, True), self.send(high, False)
        yield
        low, high = self.clock(low, high)
        nothing = jnp.zeros_like(low)
        forward = jnp.concatenate([low, nothing], axis=0)
        backward = jnp.concatenate([nothing, high], axis=0)
        for k in range(half_way - 1, 0, -1):
            forward = (forward.astype(f32) + piece(self.ahead(k))).astype(bf16)
            backward = (backward.astype(f32) + piece(self.ahead(-k))).astype(bf16)
            forward, backward = self.clock(forward, backward)
            forward, backward = self.send(forward, True), self.send(backward, False)
            yield
            forward, backward = self.clock(forward, backward)
        return forward, backward, piece(self.me)


class Line:
    def __init__(self, count, clock):
        self.count = count
        self.clock = clock
        self.me = lax.axis_index("z")
        order = list(range(0, count, 2)) + list(range(1, count, 2))[::-1]
        self.cycle = [(order[i], order[(i + 1) % count]) for i in range(count)]
        evens = (count + 1) // 2
        place = jnp.where(self.me % 2 == 0, self.me // 2, count - 1 - self.me // 2)
        self.at = []
        for k in range(count):
            spot = lax.rem(place + k, count)
            self.at.append(jnp.where(spot < evens, 2 * spot, 2 * (count - 1 - spot) + 1))

    def ahead(self, k):
        return self.at[k % self.count]

    def gather(self, block, axis):
        size = block.shape[axis]
        shape = list(block.shape)
        shape[axis] = size * self.count
        moved = self.clock.hold(block)
        pieces = [moved]
        for _ in range(1, self.count):
            moved = lax.ppermute(moved, "z", self.cycle)
            yield
            moved = self.clock(moved)
            pieces.append(moved)
        where = [
            [(i, size) if d == axis else None for d in range(2)] for i in range(len(pieces))
        ]
        return assemble(pieces, shape, where, [self.ahead(-k) for k in range(self.count)])

    def scatter(self, *parts):
        rows, width = parts[0].shape[0] // self.count, parts[0].shape[1]
        parts = self.clock.hold(*parts)

        def pieces(owner):
            return [cut(part, (owner * rows, 0), (rows, width)) for part in parts]

        moved = self.clock(add_up(*pieces(self.ahead(-1))))
        for k in range(self.count - 1, 0, -1):
            moved = lax.ppermute(moved, "z", self.cycle)
            yield
            moved = self.clock(moved)
            if k > 1:
                moved = self.clock(add_up(moved, *pieces(self.ahead(k - 1))))
        return moved, *pieces(self.me)


def shifts(count):
    return [[(i, (i + step) % count) for i in range(count)] for step in range(1, count)]


def from_axis(value, axis, count):
    me = lax.axis_index(axis)
    return [
        (lax.ppermute(value, axis, pairs), lax.rem(me - step + count, count))
        for step, pairs in enumerate(shifts(count), 1)
    ]


def to_axis(values, axis, count, dim):
    me = lax.axis_index(axis)
    return [
        lax.ppermute(
            lax.dynamic_index_in_dim(values, lax.rem(me + step, count), dim, False), axis, pairs
        )
        for step, pairs in enumerate(shifts(count), 1)
    ]


def in_order(found, axis, count, dim):
    me = lax.axis_index(axis)
    wide = jnp.stack((found[::-1] * 2)[:-1], axis=dim)
    where, sizes = [0] * wide.ndim, list(wide.shape)
    where[dim], sizes[dim] = count - 1 - me, count
    return cut(wide, where, sizes)


def exchange(values, axis, count, dim, clock):
    arrived = to_axis(values, axis, count, dim)
    yield
    found = [own_part(values, axis, dim)] + [clock(value) for value in arrived]
    return in_order(found, axis, count, dim)


def team_exchange(values, nz, clock):
    values = clock.hold(values).reshape(2, nz, *values.shape[1:])
    both = yield from exchange(values, "core", 2, 0, clock)
    out = yield from exchange(both, "z", nz, 1, clock)
    return out.reshape(2 * nz, *values.shape[2:])


def own_part(values, axis, dim):
    return lax.dynamic_index_in_dim(values, lax.axis_index(axis), dim, False)


def add_up(own, *others):
    total = own.astype(f32)
    for other in others:
        total = total + other.astype(f32)
    return total.astype(bf16)


class Grid:
    def __init__(self, nx, ny, clock):
        self.nx, self.ny, self.clock = nx, ny, clock
        self.x, self.y = lax.axis_index("x"), lax.axis_index("y")

    def gather(self, block, apart):
        rows, deep, width = block.shape
        half = rows // 2
        block = self.clock.hold(block)
        along_x, along_y = from_axis(block, "x", self.nx), from_axis(block, "y", self.ny)
        yield
        values = self.clock(*[v for v, _ in along_x + along_y])
        along_x, along_y = values[: self.nx - 1], values[self.nx - 1 :]
        left = [[w for w, _ in from_axis(v[:half], "y", self.ny)] for v in along_x]
        right = [[w for w, _ in from_axis(v[half:], "x", self.nx)] for v in along_y]
        yield
        owners = [lax.rem(self.y - k + self.ny, self.ny) for k in range(self.ny)]
        everything = slice(None)
        found = [([block, *along_y], [(everything, k) for k in range(self.ny)])]
        for i, value in enumerate(along_x):
            pieces, where = [value], [(everything, 0)]
            for j in range(self.ny - 1):
                pieces += self.clock(left[i][j], right[j][i])
                where += [(slice(0, half), j + 1), (slice(half, rows), j + 1)]
            found.append((pieces, where))
        size = rows * self.ny * deep
        if apart:
            return [
                assemble(
                    pieces,
                    (rows, self.ny, deep, width),
                    [[span, (k, None), None, None] for span, k in where],
                    owners,
                ).reshape(size, width)
                for pieces, where in found
            ]
        return assemble(
            [piece for pieces, _ in found for piece in pieces],
            (self.nx, rows, self.ny, deep, width),
            [
                [i, span, (k, None), None, None]
                for i, (_, where) in enumerate(found)
                for span, k in where
            ],
            owners,
        ).reshape(self.nx * size, width)

    def place(self, k):
        return lax.rem(self.x - k + self.nx, self.nx)

    def turn(self, values):
        half = values.shape[1] // self.nx
        wide = jnp.concatenate([values, values], axis=1)
        found = [
            cut(wide, (0, self.place(k) * half), (values.shape[0], half)) for k in range(self.nx)
        ]
        return jnp.concatenate(found, axis=1)

    def turn_back(self, values):
        return self.turn(values)

    def scatter(self, x_first, y_first, rows):
        nx, ny = self.nx, self.ny
        count = len(x_first)
        values = self.clock.hold(*x_first, *y_first)
        values = [v.reshape(nx, rows, ny, -1, v.shape[1]) for v in values]
        one, two = values[:count], values[count:]

        def send_x(values):
            return [
                lax.ppermute(values[k], "x", [(i, (i - k) % nx) for i in range(nx)])
                for k in range(1, nx)
            ]

        sent = [send_x(v) for v in one] + [to_axis(v, "y", ny, 2) for v in two]
        yield
        sent = [[self.clock(v) for v in group] for group in sent]
        one = [add_up(v[0], *group) for v, group in zip(one, sent)]
        two = [add_up(own_part(v, "y", 2), *group) for v, group in zip(two, sent[count:])]
        values = self.clock(*one, *two)
        one, two = values[:count], values[count:]
        sent = [to_axis(v, "y", ny, 1) for v in one] + [send_x(v) for v in two]
        yield
        sent = [[self.clock(v) for v in group] for group in sent]
        one = [add_up(own_part(v, "y", 1), *group) for v, group in zip(one, sent)]
        two = [add_up(v[0], *group) for v, group in zip(two, sent[count:])]
        return jnp.concatenate([*one, *two], axis=2)


def sum_everywhere(values, sizes, clock):
    values = clock.hold(values)
    for axis, count in sizes:
        if count & (count - 1):
            values = lax.psum(values, axis)
            continue
        step = 1
        while step < count:
            other = lax.ppermute(values, axis, [(i, i ^ step) for i in range(count)])
            yield
            values = values + clock(other)
            step *= 2
    return values


def allowed_keys(low_ref, high_ref, shape):
    places = lax.broadcasted_iota(jnp.int32, shape, 1)
    return (places >= low_ref[...]) & (places < high_ref[...])


def forward_kernel(q_ref, k_ref, v_ref, low_ref, high_ref, out_ref, lse_ref):
    scores = dot_nt(q_ref[...], k_ref[...]) * (HEAD**-0.5 * log2_e)
    allowed = allowed_keys(low_ref, high_ref, scores.shape)
    scores = jnp.where(allowed, scores, masked_value)
    largest = jnp.max(scores, axis=1, keepdims=True)
    powers = jnp.exp2(scores - largest)
    totals = jnp.sum(powers, axis=1, keepdims=True)
    probs = (powers * (1.0 / totals)).astype(bf16)
    out_ref[...] = dot_nn(probs, v_ref[...]).astype(bf16)
    lse_ref[0] = largest + jnp.log2(totals)


def backward_kernel(
    q_ref, k_ref, v_ref, g_ref, low_ref, high_ref, lse_ref, cos_ref, sin_ref, all_cos_ref, all_sin_ref,
    gq_ref, gk_ref, gv_ref, k_sum, v_sum,
):
    scale = HEAD**-0.5
    step = pl.program_id(1)

    @pl.when(step == 0)
    def _():
        k_sum[...] = jnp.zeros_like(k_sum)
        v_sum[...] = jnp.zeros_like(v_sum)

    scores = dot_nt(q_ref[...], k_ref[...]) * (scale * log2_e)
    allowed = allowed_keys(low_ref, high_ref, scores.shape)
    probs = jnp.where(allowed, jnp.exp2(scores - lse_ref[0]), 0.0)
    grad_probs = dot_nt(g_ref[...], v_ref[...])
    delta = jnp.sum(probs * grad_probs, axis=1, keepdims=True)
    grad_scores = (probs * (grad_probs - delta)).astype(bf16)
    grad_q = (dot_nn(grad_scores, k_ref[...]) * scale).astype(bf16).astype(f32)
    gq_ref[...] = rotate_back(grad_q, cos_ref[...], sin_ref[...]).astype(bf16)
    k_sum[...] += dot_tn(grad_scores, q_ref[...])
    v_sum[...] += dot_tn(probs.astype(bf16), g_ref[...])

    @pl.when(step == pl.num_programs(1) - 1)
    def _():
        grad_k = (k_sum[...] * scale).astype(bf16).astype(f32)
        gk_ref[...] = rotate_back(grad_k, all_cos_ref[...], all_sin_ref[...]).astype(bf16)
        gv_ref[...] = v_sum[...].astype(bf16)


params = pltpu.CompilerParams(vmem_limit_bytes=56 * 2**20)
cost = pl.CostEstimate(flops=0, bytes_accessed=0, transcendentals=0)


def assemble(pieces, shape, where, places):
    def kernel(places_ref, *refs):
        out, arrived = refs[len(pieces)], refs[-1]

        def index(part):
            if not isinstance(part, tuple):
                return slice(None) if part is None else part
            k, size = part
            if size is None:
                return places_ref[k]
            return pl.ds(pl.multiple_of(places_ref[k] * size, size), size)

        copies = [
            pltpu.make_async_copy(refs[i], out.at[tuple(map(index, parts))], arrived.at[i])
            for i, parts in enumerate(where)
        ]
        for copy in copies:
            copy.start()
        for copy in copies:
            copy.wait()

    return pl.pallas_call(
        kernel,
        grid_spec=pltpu.PrefetchScalarGridSpec(
            num_scalar_prefetch=1,
            grid=(1,),
            in_specs=[pl.BlockSpec(memory_space=pl.ANY)] * len(pieces),
            out_specs=pl.BlockSpec(tuple(shape), lambda i, places: (0,) * len(shape)),
            scratch_shapes=[pltpu.SemaphoreType.DMA((len(pieces),))],
        ),
        out_shape=jax.ShapeDtypeStruct(tuple(shape), pieces[0].dtype),
        compiler_params=params,
        cost_estimate=cost,
        name="assemble",
    )(jnp.stack(places).astype(jnp.int32), *pieces)


def lay_out(name, pieces, shape, kind, where, places=None):
    places = jnp.zeros((1,), jnp.int32) if places is None else places

    def kernel(places_ref, *refs):
        out = refs[-1]
        out[...] = jnp.zeros_like(out)
        for i, part, columns in where:
            value = refs[i][part].astype(kind)
            if isinstance(columns, list):
                place, start = columns
                size = value.shape[-1]
                begin = pl.multiple_of(places_ref[place] + start, LANES)
                out[:, pl.ds(begin, size)] = value
            else:
                out[:, columns : columns + value.shape[-1]] = value

    return pl.pallas_call(
        kernel,
        grid_spec=pltpu.PrefetchScalarGridSpec(
            num_scalar_prefetch=1,
            grid=(1,),
            in_specs=[
                pl.BlockSpec(a.shape, lambda i, places, n=a.ndim: (0,) * n) for a in pieces
            ],
            out_specs=pl.BlockSpec(shape, lambda i, places: (0, 0)),
        ),
        out_shape=jax.ShapeDtypeStruct(shape, kind),
        compiler_params=params,
        cost_estimate=cost,
        name=name,
    )(places, *pieces)


def attention_specs(count, heads, block):
    def one(column):
        return pl.BlockSpec((block, HEAD), lambda h, i: (i, column + h))

    def whole(column):
        return pl.BlockSpec((count, HEAD), lambda h, i: (0, column + h))

    edge = pl.BlockSpec((block, 1), lambda h, i: (i, 0))
    lse = pl.BlockSpec((1, block, 1), lambda h, i: (h, i, 0))
    return (one, whole, edge, lse)


def attend_forward(packed, low, high):
    count, heads = packed.shape[0], packed.shape[1] // (3 * HEAD)
    block = min(512, count)
    one, whole, edge, lse = attention_specs(count, heads, block)
    return pl.pallas_call(
        forward_kernel,
        grid=(heads, count // block),
        in_specs=[one(0), whole(heads), whole(2 * heads), edge, edge],
        out_specs=[one(0), lse],
        out_shape=[
            jax.ShapeDtypeStruct((count, heads * HEAD), bf16),
            jax.ShapeDtypeStruct((heads, count, 1), f32),
        ],
        compiler_params=params,
        cost_estimate=cost,
        name="attend_forward",
    )(packed, packed, packed, low, high)


def attend_backward(packed, grads, low, high, log_sums, cosine, sine):
    count, heads = packed.shape[0], packed.shape[1] // (3 * HEAD)
    block = min(512, count)
    one, whole, edge, lse = attention_specs(count, heads, block)
    shape = jax.ShapeDtypeStruct((count, heads * HEAD), bf16)
    turn = pl.BlockSpec((block, HEAD), lambda h, i: (i, 0))
    turn_all = pl.BlockSpec((count, HEAD), lambda h, i: (0, 0))
    return pl.pallas_call(
        backward_kernel,
        grid=(heads, count // block),
        in_specs=[one(0), whole(heads), whole(2 * heads), one(0), edge, edge, lse]
        + [turn, turn, turn_all, turn_all],
        out_specs=[one(0), whole(0), whole(0)],
        out_shape=[shape, shape, shape],
        scratch_shapes=[pltpu.VMEM((count, HEAD), f32), pltpu.VMEM((count, HEAD), f32)],
        compiler_params=params,
        cost_estimate=cost,
        name="attend_backward",
    )(packed, packed, packed, grads, low, high, log_sums, cosine, sine, cosine, sine)


def over_rows(
    name, body, block, rows, whole, outs, sums=(), places=None, scratch=(), first_map=None, count=None
):
    count = count or rows[-1].shape[0]
    places = jnp.zeros((1,), jnp.int32) if places is None else places

    def kernel(places_ref, *refs):
        n, m, k = len(rows), len(rows) + len(whole), len(rows) + len(whole) + len(outs)
        if sums:

            @pl.when(pl.program_id(0) == 0)
            def _():
                for ref in refs[k : k + len(sums)]:
                    ref[...] = jnp.zeros_like(ref)

        body(refs[:n], refs[n:m], places_ref, refs[m:k], refs[k:])

    room = [pltpu.VMEM((block, width), kind) for width, kind in scratch]

    def by_row(i, places):
        return (i, 0)

    def fixed(i, places):
        return (0, 0)

    return pl.pallas_call(
        kernel,
        grid_spec=pltpu.PrefetchScalarGridSpec(
            num_scalar_prefetch=1,
            grid=(count // block,),
            in_specs=[
                pl.BlockSpec((block, a.shape[1]), first_map if first_map and not i else by_row)
                for i, a in enumerate(rows)
            ]
            + [pl.BlockSpec(a.shape, fixed) for a in whole],
            out_specs=[pl.BlockSpec((block, width), by_row) for width, _ in outs]
            + [pl.BlockSpec((1, width), fixed) for width in sums],
            scratch_shapes=room,
        ),
        out_shape=[jax.ShapeDtypeStruct((count, width), kind) for width, kind in outs]
        + [jax.ShapeDtypeStruct((1, width), f32) for width in sums],
        compiler_params=params,
        cost_estimate=cost,
        name=name,
    )(places, *rows, *whole)


def columns_of(ref, place, width):
    return ref.at[:, pl.ds(pl.multiple_of(place * width, width), width)]


def project_pieces(left_ref, pieces, places_ref):
    total = None
    for i, piece in enumerate(pieces):
        depth = piece.shape[0]
        term = dot_nn(columns_of(left_ref, places_ref[i], depth)[...], piece[...])
        total = term if total is None else total + term
    return total


def transposed_sums(name, lefts, rights, block=256):
    rights = [r if isinstance(r, (tuple, list)) else [r] for r in rights]
    depth = lefts[0].shape[1]
    block = min(block, depth)
    width = sum(r.shape[1] for r in rights[0])
    flat = [r for group in rights for r in group]

    def kernel(*refs):
        left_refs, right_refs, out_ref = refs[: len(lefts)], refs[len(lefts) : -1], refs[-1]
        per = len(rights[0])
        start = 0
        for j in range(per):
            size = rights[0][j].shape[1]
            total = None
            for i, left in enumerate(left_refs):
                term = dot_tn(left[...], right_refs[i * per + j][...])
                total = term if total is None else total + term
            out_ref[:, start : start + size] = total.astype(bf16)
            start += size

    return pl.pallas_call(
        kernel,
        grid=(depth // block,),
        in_specs=[pl.BlockSpec((a.shape[0], block), lambda i: (0, i)) for a in lefts]
        + [pl.BlockSpec(a.shape, lambda i: (0, 0)) for a in flat],
        out_specs=pl.BlockSpec((block, width), lambda i: (i, 0)),
        out_shape=jax.ShapeDtypeStruct((depth, width), bf16),
        compiler_params=params,
        cost_estimate=cost,
        name=name,
    )(*lefts, *flat)


def times_transposed(name, left, pieces, places, width):
    def body(rows, whole, places_ref, outs, sums):
        for i, piece in enumerate(whole):
            part = dot_nt(rows[0][...], piece[...]).astype(bf16)
            columns_of(outs[0], places_ref[i], piece.shape[0])[...] = part

    (out,) = over_rows(
        name, body, min(256, left.shape[0]), [left], pieces, [(width, bf16)], places=places
    )
    return out


def tile_split(width, count):
    tiles = -(-width // LANES)
    least, extra = divmod(tiles, count)
    sizes = [least + (1 if i < extra else 0) for i in range(count)]
    starts = [sum(sizes[:i]) for i in range(count)]
    return (starts, sizes, max(sizes))


class Values:
    pass


ORDER = (
    "tokens_in", "qkv_in", "tokens_in", "gate_up_pack", "tokens_in", "down_pack", "qkv_in", "out_in",
    "tokens_in", "tables", "turn", "qkv_in", "tokens_in", "out_in", "gate_up_in", "qkv_in", "project",
    "out_grad_in", "attend", "to_y", "out_grad_in", "to_y", "attended_in", "out_in", "attended_in",
    "gate_up_in", "out_grad_in", "out_in", "attended_in", "out_in", "down_in", "attended_in", "out_grad_in",
    "gate_up_in", "second_norm", "normed_core", "gate_up_in", "down_in", "down_in", "normed_core",
    "out_grad_core", "gate_up", "down_in", "out_grad_core", "down_in", "act", "other_parts", "own_parts",
    "other_parts", "parts_out", "first_share", "second_share", "ffn_grad", "parts_out", "parts_out",
    "ffn_grad", "parts_out", "second_back", "heads_in", "ffn_grad", "heads_in", "ffn_back", "attend_back",
    "first_back", "normed_out", "small", "qkv_back", "ffn_back", "normed_out", "grad_attn_in", "qkv_back",
    "ffn_rows", "small", "normed_out", "grad_attn_in", "out_back", "small", "qkv_back", "out_back",
    "normed_out", "small", "output", "out_back", "normed_out", "small", "out_back", "first_norm_tokens",
    "qkv_back", "small", "out_back", "out_rows", "qkv_rows",
)


def per_device(
    tokens,
    ln1_gain,
    ln1_bias,
    w_qkv,
    b_qkv,
    w_out,
    b_out,
    ln2_gain,
    ln2_bias,
    w_gate,
    b_gate,
    w_up,
    b_up,
    w_down,
    b_down,
    protein_lengths,
    prefix_lengths,
    out_grad,
):
    nx, nz, ny = (lax.axis_size(axis) for axis in ("x", "z", "y"))
    x, core, z, y = (lax.axis_index(axis) for axis in EVERY)
    sizes_of = (("core", 2), ("x", nx), ("y", ny), ("z", nz))
    own_rows, width = tokens.shape
    weight_rows = w_qkv.shape[0]
    ffn_width = w_gate.shape[1]
    seq_count, team_count = nz * ny, 2 * nz
    count = own_rows * seq_count
    line_rows = nz * own_rows
    own_heads = HEADS // seq_count
    own_width = own_heads * HEAD
    clock = Clock()
    ring = Ring(nz, ny, clock)
    line = Line(nz, clock)
    grid = Grid(nx, ny, clock)
    me = ring.me

    def all_to_all(values, axes):
        return lax.all_to_all(values, axes, split_axis=0, concat_axis=0, tiled=True)

    def other_core(values):
        return lax.ppermute(values, "core", [(0, 1), (1, 0)])

    starts, sizes, most = tile_split(ffn_width, team_count)
    own_ffn = most * LANES
    padded = (starts[-1] + most) * LANES
    first_tile = jnp.asarray(starts, jnp.int32)[core * nz + z] * LANES
    split = 3 * own_ffn // 2 // LANES * LANES
    half_places = jnp.stack([lax.rem(x - k + nx, nx) for k in range(nx)])
    places = jnp.concatenate([half_places * 2 + core, half_places * 2 + 1 - core])
    cotangent = out_grad.astype(f32)
    pieces_of = PIECES if PIECES % nx == 0 else nx
    piece_width = width // pieces_of
    plan = Plan()
    v = Values()

    def ffn_blocks(weight, mask):
        whole = jnp.pad(weight, ((0, 0), (0, padded - ffn_width)))
        pieces = []
        for start, size in zip(starts, sizes):
            piece = whole[:, start * LANES : (start + most) * LANES]
            if mask and size < most:
                piece = jnp.pad(piece[:, : size * LANES], ((0, 0), (0, (most - size) * LANES)))
            pieces.append(piece)
        return jnp.stack(pieces)

    def ffn_bias(bias):
        return cut(jnp.pad(bias, (0, padded - ffn_width)), (first_tile,), (own_ffn,))

    def row(values):
        return values.reshape(1, -1)

    def low_nt(left, right):
        return dot_nt(left, right).astype(bf16)

    def low_tn(left, right):
        return dot_tn(left, right).astype(bf16)

    @plan.transfer
    def tokens_in():
        v.tokens_all = clock((yield from ring.gather(tokens)))

    @plan.transfer
    def qkv_in():
        blocks = (
            w_qkv.reshape(weight_rows, 3, seq_count, own_width)
            .transpose(2, 0, 1, 3)
            .reshape(seq_count, weight_rows, 3 * own_width)
        )
        moved = all_to_all(clock.hold(blocks), GROUP)
        yield
        rows = clock(moved).reshape(seq_count * weight_rows, 3 * own_width)
        from_x = from_axis(rows, "x", nx)
        yield
        pieces = [rows] + [clock(value) for value, _ in from_x]
        from_core = [other_core(value) for value in pieces]
        yield
        v.qkv_pieces = pieces + [clock(value) for value in from_core]

    @plan.transfer
    def out_in():
        block = jnp.broadcast_to(w_out[None], (nz, weight_rows, width))
        moved = all_to_all(clock.hold(block), "z")
        yield
        pieces = yield from grid.gather(clock(moved), True)
        pieces = list(clock(*pieces))
        from_core = [other_core(piece) for piece in pieces]
        yield
        v.out_pieces = pieces + [clock(value) for value in from_core]

    @plan.step
    def gate_up_pack():
        v.gate_up_blocks = clock.run(
            lambda gate, up: jnp.concatenate(
                [ffn_blocks(gate, False), ffn_blocks(up, False)], axis=2
            ),
            w_gate,
            w_up,
        )

    @plan.step
    def down_pack():
        v.down_blocks = clock.run(lambda down: ffn_blocks(down, True), w_down)

    @plan.transfer
    def gate_up_in():
        moved = all_to_all(clock.hold(v.gate_up_blocks), TEAM)
        yield
        v.gate_up_own = clock((yield from grid.gather(clock(moved), False)))

    @plan.transfer
    def down_in():
        moved = all_to_all(clock.hold(v.down_blocks), TEAM)
        yield
        v.down_moved = clock(moved)
        yield
        v.down_own = clock((yield from grid.gather(v.down_moved, False)))

    @plan.step
    def tables():
        def make(lengths, prefixes):
            position, low, high = group_layout(lengths[0], prefixes[0], count)
            return (*rotary_tables(position), low[:, None], high[:, None])

        v.cosine, v.sine, v.low, v.high = clock.run(make, protein_lengths, prefix_lengths)

    def project_kernel(rows, whole, places_ref, outs, sums):
        tokens_ref, cos_ref, sin_ref = rows
        gain, bias, qkv_bias, *pieces = whole
        normed_ref, packed_ref = outs
        normed = layer_norm(tokens_ref[...].astype(f32), gain[...], bias[...])
        normed_ref[...] = normed.astype(bf16)
        raw = project_pieces(normed_ref, pieces, places_ref) + qkv_bias[...]
        for i in range(3 * own_heads):
            piece = raw[:, i * HEAD : (i + 1) * HEAD]
            if i < 2 * own_heads:
                piece = rotate(piece, cos_ref[...], sin_ref[...])
            packed_ref[:, i * HEAD : (i + 1) * HEAD] = piece.astype(bf16)

    @plan.step
    def project():
        qkv_bias = cut(b_qkv.reshape(3, width), (0, me * own_width), (3, own_width))
        v.normed, v.packed = clock.run(
            lambda tokens_all, *pieces: over_rows(
                "project",
                project_kernel,
                256,
                [tokens_all, v.cosine, v.sine],
                [row(ln1_gain), row(ln1_bias), row(qkv_bias), *pieces],
                [(width, bf16), (3 * own_width, bf16)],
                places=places,
            ),
            v.tokens_all,
            *v.qkv_pieces,
        )

    @plan.step
    def attend():
        v.head_result, v.log_sums = clock.run(
            lambda values: attend_forward(values, v.low, v.high), v.packed
        )

    @plan.transfer
    def to_y():
        result = v.head_result.reshape(nz, ny, own_rows, own_width)
        moved = yield from exchange(result, "y", ny, 1, clock)
        moved = moved.transpose(0, 2, 1, 3).reshape(line_rows, ny * own_width)
        v.head_columns = clock(moved)

    @plan.transfer
    def attended_in():
        v.attended = clock((yield from line.gather(v.head_columns, 1)))

    @plan.step
    def turn():
        v.out_grad_turned = clock.run(grid.turn, out_grad)

    @plan.transfer
    def out_grad_in():
        found = yield from line.gather(v.out_grad_turned, 0)
        v.grad_out_line = clock(found)

    @plan.transfer
    def out_grad_core():
        moved = other_core(v.grad_out_line)
        yield
        both = [v.grad_out_line, clock(moved)]
        v.grad_out_all = clock(jnp.concatenate(both, axis=0))

    def second_kernel(rows, whole, places_ref, outs, more):
        tokens_ref, attended_ref = rows
        gain, bias, out_bias, *pieces = whole
        attn = project_pieces(attended_ref, pieces, places_ref) + out_bias[...]
        hidden = tokens_ref[...].astype(f32) + attn
        outs[0][...] = hidden
        (normed_ref,) = more
        normed_ref[...] = layer_norm(hidden, gain[...], bias[...]).astype(bf16)
        for k in range(nx):
            place = places_ref[2 * nx + k]
            whole = columns_of(normed_ref, place, width // nx)
            for j in range(pieces_of // nx):
                out = outs[1 + k * (pieces_of // nx) + j]
                out[...] = whole[:, j * piece_width : (j + 1) * piece_width]

    @plan.step
    def second_norm():
        hidden_in, *v.normed_line = clock.run(
            lambda tokens, attended, *pieces: over_rows(
                "second_norm",
                second_kernel,
                own_rows,
                [tokens, attended],
                [row(ln2_gain), row(ln2_bias), row(b_out), *pieces],
                [(width, f32)] + [(piece_width, bf16)] * pieces_of,
                places=jnp.concatenate([places, half_places, row(y)[0]]),
                scratch=[(width, bf16)],
                first_map=lambda i, places: (i * ny + places[3 * nx], 0),
                count=line_rows,
            ),
            v.tokens_all,
            v.attended,
            *v.out_pieces,
        )
        v.hidden_own = cut(hidden_in, (z * own_rows, 0), (own_rows, width))

    @plan.transfer
    def normed_core():
        moved = [other_core(piece) for piece in v.normed_line]
        yield
        moved = clock(*moved)
        where = [
            [slice(j * line_rows, (j + 1) * line_rows), slice(i * piece_width, (i + 1) * piece_width)]
            for j in range(2)
            for i in range(pieces_of)
        ]
        v.normed_two = clock(
            assemble([*v.normed_line, *moved], (2 * line_rows, width), where, [me])
        )

    @plan.step
    def gate_up():
        bias = jnp.concatenate([ffn_bias(b_gate), ffn_bias(b_up)])
        v.gate_up = clock.run(lambda a, b: dot_nn(a, b) + bias, v.normed_two, v.gate_up_own)

    @plan.step
    def act():
        def make(grads, weight, gate_up):
            grad_act = dot_nn(grads, weight)
            values, pull = jax.vjp(geglu, gate_up[:, :own_ffn], gate_up[:, own_ffn:])
            grads = [g.astype(bf16) for g in pull(grad_act)]
            return jnp.concatenate(grads, axis=1), values.astype(bf16)

        v.grad_gate_up, v.act = clock.run(make, v.grad_out_all, v.down_own, v.gate_up)

    def both_parts(grads, gate_up, act, down):
        return jnp.concatenate([low_nt(grads, gate_up), low_nt(act, down)], axis=1)

    @plan.transfer
    def other_parts():
        found = clock.run(
            both_parts, v.grad_gate_up[line_rows:], v.gate_up_own, v.act[line_rows:], v.down_own
        )
        moved = other_core(found)
        yield
        v.other_parts = clock(moved)

    @plan.step
    def own_parts():
        v.own_parts = clock.run(
            both_parts, v.grad_gate_up[:line_rows], v.gate_up_own, v.act[:line_rows], v.down_own
        )

    @plan.transfer
    def parts_out():
        v.two_parts = yield from line.scatter(v.own_parts, v.other_parts)

    @plan.step
    def first_share():
        v.first_share = clock.run(low_tn, v.normed_two, v.grad_gate_up[:, :split])

    @plan.step
    def second_share():
        v.second_share, v.third_share = clock.run(
            lambda a, b, c, d: (low_tn(a, b[:, split:]), low_tn(c, d)),
            v.normed_two,
            v.grad_gate_up,
            v.grad_out_all,
            v.act,
        )

    @plan.transfer
    def ffn_grad():
        found = yield from grid.scatter(
            [v.first_share], [v.second_share, v.third_share], team_count
        )
        v.ffn_share = clock(found)

    @plan.transfer
    def ffn_back():
        moved = all_to_all(clock.hold(v.ffn_share), TEAM)
        yield
        v.ffn_back = clock(moved)

    def second_back_kernel(rows, whole, places_ref, outs, more):
        *sums, grads_ref = more
        *terms, hidden, out_grad_ref = rows
        gain, *pieces = whole
        turned = sum(term[:, :width].astype(f32) for term in terms)
        part = width // nx
        for k in range(nx):
            place = places_ref[2 * nx + k]
            columns_of(grads_ref, place, part)[...] = turned[:, k * part : (k + 1) * part]
        grads = grads_ref[...]
        unit, inverse = norm_parts(hidden[...])
        cotangent = out_grad_ref[...].astype(f32)
        total = cotangent + layer_norm_back(unit, inverse, gain[...], grads)
        low = total.astype(bf16)
        outs[0][...] = total
        outs[1][...] = low
        for i, piece in enumerate(pieces):
            part = dot_nt(low, piece[...]).astype(bf16)
            columns_of(outs[2], places_ref[i], piece.shape[0])[...] = part
        for ref, values in zip(sums, (grads * unit, grads, low.astype(f32), cotangent)):
            ref[...] += jnp.sum(values, axis=0, keepdims=True)

    @plan.step
    def second_back():
        v.grad_hidden, v.grad_attn, v.grad_attended, *v.second_sums = clock.run(
            lambda *values: over_rows(
                "second_norm_back",
                second_back_kernel,
                own_rows,
                values[:5],
                [row(ln2_gain), *values[5:]],
                [(width, f32), (width, bf16), (width, bf16)],
                [width] * 4,
                places=jnp.concatenate([places, half_places]),
                scratch=[(width, f32)],
            ),
            *v.two_parts,
            v.hidden_own,
            out_grad,
            *v.out_pieces,
        )

    @plan.transfer
    def heads_in():
        blocks = v.grad_attended.reshape(own_rows, seq_count, own_width).transpose(1, 0, 2)
        moved = all_to_all(clock.hold(blocks), GROUP)
        yield
        v.grad_heads = clock(moved).reshape(count, own_width)

    @plan.step
    def attend_back():
        v.grad_parts = clock.run(
            lambda *values: attend_backward(*values, v.low, v.high, v.log_sums, v.cosine, v.sine),
            v.packed,
            v.grad_heads,
        )

    def first_back_kernel(rows, whole, places_ref, outs, more):
        *sums, part_ref = more
        grads, tokens_ref = rows[:3], rows[3]
        unit, _ = norm_parts(tokens_ref[...].astype(f32))
        for i, piece in enumerate(whole):
            part = None
            for j, grad in enumerate(grads):
                term = dot_nt(grad[...], piece[:, j * own_width : (j + 1) * own_width])
                part = term if part is None else part + term
            depth = piece.shape[0]
            columns_of(outs[0], places_ref[i], depth)[...] = part.astype(bf16)
            columns_of(part_ref, places_ref[i], depth)[...] = part
        part = part_ref[...]
        sums[0][...] += jnp.sum(part * unit, axis=0, keepdims=True)
        sums[1][...] += jnp.sum(part, axis=0, keepdims=True)
        for j, grad in enumerate(grads):
            total = jnp.sum(grad[...].astype(f32), axis=0, keepdims=True)
            sums[2][:, j * own_width : (j + 1) * own_width] += total

    @plan.step
    def first_back():
        v.normed_part, *v.first_sums = clock.run(
            lambda *values: over_rows(
                "first_norm_back",
                first_back_kernel,
                256,
                values[:4],
                values[4:],
                [(width, bf16)],
                [width, width, 3 * own_width],
                places=places,
                scratch=[(width, f32)],
            ),
            *v.grad_parts,
            v.tokens_all,
            *v.qkv_pieces,
        )

    @plan.transfer
    def normed_out():
        v.one_parts = yield from ring.scatter(v.normed_part)

    @plan.transfer
    def small():
        sums = [*v.second_sums, *v.first_sums[:2]]
        bias_gate_up = jnp.sum(v.grad_gate_up.astype(f32), axis=0, keepdims=True)
        where = [(i, (slice(None), slice(None)), i * width) for i in range(len(sums))]
        start = len(sums) * width
        for i in range(3):
            part = (slice(None), slice(i * own_width, (i + 1) * own_width))
            where.append((len(sums), part, [0, start + i * width]))
        start += 3 * width
        for i in range(2):
            part = (slice(None), slice(i * own_ffn, (i + 1) * own_ffn))
            where.append((len(sums) + 1, part, [1, start + i * padded]))
        values = clock.run(
            lambda *values: lay_out(
                "small",
                values,
                (1, start + 2 * padded),
                f32,
                where,
                jnp.stack([me * own_width, first_tile]).astype(jnp.int32),
            ),
            *sums,
            v.first_sums[2],
            bias_gate_up,
        )
        v.small = (yield from sum_everywhere(values, sizes_of, clock))[0]

    @plan.transfer
    def qkv_back():
        share = clock.run(
            lambda a, *b: low_tn(a, jnp.concatenate(b, axis=1)), v.normed, *v.grad_parts
        )
        share = share.reshape(nx, 2, seq_count * weight_rows, 3 * own_width)
        for axis, size, dim in (("core", 2, 1), ("x", nx, 0)):
            arrived = to_axis(share, axis, size, dim)
            yield
            share = clock(add_up(own_part(share, axis, dim), *[clock(a) for a in arrived]))
        moved = all_to_all(share.reshape(seq_count, weight_rows, 3 * own_width), GROUP)
        yield
        v.qkv_back = clock(moved)

    @plan.transfer
    def grad_attn_in():
        blocks = clock.hold(v.grad_attn).reshape(own_rows, nz, width // nz).transpose(1, 0, 2)
        found = yield from exchange(blocks, "z", nz, 0, clock)
        v.grad_attn_block = clock(found).reshape(line_rows, width // nz)

    @plan.transfer
    def out_back():
        share = clock.run(low_tn, v.attended, v.grad_attn_block)
        share = share.reshape(nx, 2, nz, ny, weight_rows, width // nz)
        for axis, size, dim in (("core", 2, 1), ("x", nx, 0), ("y", ny, 1)):
            arrived = to_axis(share, axis, size, dim)
            yield
            share = clock(add_up(own_part(share, axis, dim), *[clock(a) for a in arrived]))
        v.out_back = yield from exchange(share, "z", nz, 0, clock)

    @plan.step
    def output():
        v.output = clock.run(
            lambda hidden, *terms: (
                grid.turn_back(sum(term[:, width:].astype(f32) for term in terms))
                + hidden
                + b_down
            ).astype(bf16),
            v.hidden_own,
            *v.two_parts,
        )

    def last_kernel(rows, whole, places_ref, outs, sums):
        below, above, own, tokens_ref, hidden_grad = rows
        grads = below[...].astype(f32) + above[...].astype(f32) + own[...]
        unit, inverse = norm_parts(tokens_ref[...].astype(f32))
        total = hidden_grad[...] + layer_norm_back(unit, inverse, whole[0][...], grads)
        outs[0][...] = total.astype(bf16)

    @plan.step
    def first_norm_tokens():
        v.tokens_grad = clock.run(
            lambda *values: over_rows(
                "first_norm_tokens",
                last_kernel,
                own_rows,
                values,
                [row(ln1_gain)],
                [(width, bf16)],
            )[0],
            *v.one_parts,
            tokens,
            v.grad_hidden,
        )

    @plan.step
    def ffn_rows():
        def rows_of(moved, which):
            everything = slice(None)
            where = []
            for i in range(team_count):
                size = min(sizes[i] * LANES, ffn_width - starts[i] * LANES)
                span = slice(which * own_ffn, which * own_ffn + size)
                where.append((0, (i, everything, span), starts[i] * LANES))
            return lay_out("ffn_rows", [moved], (weight_rows, ffn_width), f32, where)

        v.ffn_rows = clock.run(lambda moved: [rows_of(moved, i) for i in range(3)], v.ffn_back)

    @plan.step
    def qkv_rows():
        everything = slice(None)
        where = [
            (0, (i, everything, slice(j * own_width, (j + 1) * own_width)), j * width + i * own_width)
            for i in range(seq_count)
            for j in range(3)
        ]
        v.qkv_rows = clock.run(
            lambda moved: lay_out("qkv_rows", [moved], (weight_rows, 3 * width), f32, where),
            v.qkv_back,
        )

    @plan.step
    def out_rows():
        everything = slice(None)
        where = [(0, (i, everything, everything), i * (width // nz)) for i in range(nz)]
        v.out_rows = clock.run(
            lambda moved: lay_out("out_rows", [moved], (weight_rows, width), f32, where),
            v.out_back,
        )

    plan.run(ORDER)


    gain_two, bias_two, b_out_grad, b_down_grad, gain_one, bias_one = (
        v.small[i * width : (i + 1) * width] for i in range(6)
    )
    b_qkv_grad = v.small[6 * width : 9 * width]
    b_gate_grad = v.small[9 * width : 9 * width + ffn_width]
    b_up_grad = v.small[9 * width + padded : 9 * width + padded + ffn_width]
    return (
        v.output,
        v.tokens_grad,
        gain_one,
        bias_one,
        v.qkv_rows,
        b_qkv_grad,
        v.out_rows,
        b_out_grad,
        gain_two,
        bias_two,
        v.ffn_rows[0],
        b_gate_grad,
        v.ffn_rows[1],
        b_up_grad,
        v.ffn_rows[2],
        b_down_grad,
    )


def solution(mesh):
    nx, seq_count = mesh.shape["batch"] // 2, mesh.shape["seq"]
    nz = 4 if seq_count % 4 == 0 else seq_count
    grid = Mesh(mesh.devices.reshape(nx, 2, nz, seq_count // nz), EVERY)
    rows = P(EVERY, None)
    lengths = P(("x", "core"), None)
    in_specs = (
        rows, P(), P(), rows, P(), rows, P(), P(), P(), rows, P(), rows, P(), rows, P(),
        lengths, lengths, rows,
    )
    out_specs = (
        rows, rows, P(), P(), rows, P(), rows, P(), P(), P(), rows, P(), rows, P(), rows, P(),
    )
    return jax.shard_map(
        per_device, mesh=grid, in_specs=in_specs, out_specs=out_specs, check_vma=False
    )
```

```python
import math

import jax
import jax.numpy as jnp
from jax import lax
from jax.experimental import pallas as pl
from jax.experimental.pallas import tpu as pltpu
from jax.sharding import Mesh
from jax.sharding import PartitionSpec as P

HEADS = 16
HEAD = 128
LANES = 128
PIECES = 4

epsilon = 1e-05
masked_value = -1000000000.0
log2_e = math.log2(math.e)
bf16 = jnp.bfloat16
f32 = jnp.float32

EVERY = ("x", "core", "z", "y")
GROUP = ("z", "y")
TEAM = ("core", "z")


def norm_parts(values):
    average = jnp.mean(values, axis=-1, keepdims=True)
    centered = values - average
    spread = jnp.mean(centered * centered, axis=-1, keepdims=True)
    inverse = lax.rsqrt(spread + epsilon)
    return (centered * inverse, inverse)


def layer_norm(values, gain, bias):
    unit, _ = norm_parts(values)
    return unit * gain + bias


def layer_norm_back(unit, inverse, gain, grad):
    scaled = grad * gain
    first = jnp.mean(scaled, axis=-1, keepdims=True)
    second = jnp.mean(scaled * unit, axis=-1, keepdims=True)
    return inverse * (scaled - first - unit * second)


def gelu_tanh(values):
    return (
        0.5
        * values
        * (1.0 + jnp.tanh(0.7978845608028654 * (values + 0.044715 * values * values * values)))
    )


def geglu(gate, upper):
    return gelu_tanh(gate) * upper


def group_layout(lengths, prefixes, count):
    ends = jnp.cumsum(lengths)
    starts = ends - lengths
    places = jnp.arange(count, dtype=jnp.int32)
    member = ((places[:, None] >= starts[None, :]) & (places[:, None] < ends[None, :])).astype(
        jnp.int32
    )
    first = jnp.sum(member * starts[None, :], axis=1)
    limits = starts + jnp.minimum(prefixes, lengths)
    bound = jnp.sum(member * limits[None, :], axis=1)
    return (places - first, first, jnp.maximum(places + 1, bound))


def rotary_tables(position):
    half_size = HEAD // 2
    rates = jnp.exp(jnp.arange(half_size, dtype=f32) * (-2.0 * math.log(10000.0) / HEAD))
    angles = position.astype(f32)[:, None] * rates[None, :]
    cosine = jnp.cos(angles)
    sine = jnp.sin(angles)
    return (jnp.concatenate([cosine, cosine], axis=1), jnp.concatenate([-sine, sine], axis=1))


def swap_halves(values):
    half_size = HEAD // 2
    return jnp.concatenate([values[:, half_size:], values[:, :half_size]], axis=1)


def rotate(values, cosine, sine):
    return values * cosine + swap_halves(values) * sine


def rotate_back(values, cosine, sine):
    return values * cosine + swap_halves(values * sine)


def dot_nn(left, right):
    return lax.dot_general(left, right, (((1,), (0,)), ((), ())), preferred_element_type=f32)


def dot_nt(left, right):
    return lax.dot_general(left, right, (((1,), (1,)), ((), ())), preferred_element_type=f32)


def dot_tn(left, right):
    return lax.dot_general(left, right, (((0,), (0,)), ((), ())), preferred_element_type=f32)


def put(total, piece, where):
    return lax.dynamic_update_slice(total, piece, [jnp.int32(i) for i in where])


def cut(values, where, sizes):
    return lax.dynamic_slice(values, [jnp.int32(i) for i in where], sizes)


class Clock:
    def __init__(self):
        self.last = None

    def hold(self, *values):
        if self.last is None:
            return values if len(values) > 1 else values[0]
        held = lax.optimization_barrier((*values, self.last))[:-1]
        return held if len(values) > 1 else held[0]

    def run(self, step, *values):
        held = self.hold(*values)
        out = step(*held) if len(values) > 1 else step(held)
        return self(*out) if isinstance(out, (tuple, list)) else self(out)

    def __call__(self, *values):
        given = values if self.last is None else (*values, self.last)
        out = lax.optimization_barrier(given)
        self.last = out[0]
        out = out[: len(values)]
        return out if len(values) > 1 else out[0]


class Plan:
    def __init__(self):
        self.steps, self.transfers, self.running = {}, {}, {}

    def step(self, function):
        self.steps[function.__name__] = function
        return function

    def transfer(self, function):
        self.transfers[function.__name__] = function
        return function

    def run(self, order):
        for i, name in enumerate(order):
            with jax.named_scope(name):
                if name in self.steps:
                    self.steps[name]()
                    continue
                if name not in self.running:
                    self.running[name] = self.transfers[name]()
                if name in order[i + 1 :]:
                    next(self.running[name], None)
                    continue
                for _ in self.running[name]:
                    pass


class Ring:
    def __init__(self, rows, columns, clock):
        count = rows * columns
        self.count = count
        self.clock = clock
        if columns == 2:
            order = [2 * z for z in range(rows)] + [2 * z + 1 for z in reversed(range(rows))]
        else:
            order = list(range(count))
        self.forward = [(order[i], order[(i + 1) % count]) for i in range(count)]
        self.backward = [(b, a) for a, b in self.forward]
        me = lax.axis_index(GROUP)
        if columns == 2:
            place = jnp.where(me % 2 == 0, me // 2, count - 1 - me // 2)
        else:
            place = me
        self.me = me
        self.at = []
        for k in range(count):
            spot = lax.rem(place + k, count)
            if columns == 2:
                spot = jnp.where(spot < rows, 2 * spot, 2 * (count - 1 - spot) + 1)
            self.at.append(spot)

    def ahead(self, k):
        return self.at[k % self.count]

    def send(self, values, forward):
        return lax.ppermute(values, GROUP, self.forward if forward else self.backward)

    def gather(self, block):
        half_way = self.count // 2
        rows, width = block.shape
        half = rows // 2
        block = self.clock.hold(block)
        total = jnp.zeros((self.count * rows, width), block.dtype)
        total = put(total, block, (self.me * rows, 0))
        ahead = behind = block
        for k in range(1, half_way):
            behind, ahead = self.send(behind, True), self.send(ahead, False)
            yield
            behind, ahead = self.clock(behind, ahead)
            total = put(total, behind, (self.ahead(-k) * rows, 0))
            total = put(total, ahead, (self.ahead(k) * rows, 0))
        behind, ahead = self.send(behind[:half], True), self.send(ahead[half:], False)
        yield
        behind, ahead = self.clock(behind, ahead)
        total = put(total, behind, (self.ahead(half_way) * rows, 0))
        return put(total, ahead, (self.ahead(half_way) * rows + half, 0))

    def scatter(self, parts):
        half_way = self.count // 2
        rows, width = parts.shape[0] // self.count, parts.shape[1]
        half = rows // 2
        parts = self.clock.hold(parts)

        def piece(owner, start=0, size=rows):
            return cut(parts, (owner * rows + start, 0), (size, width)).astype(f32)

        low, high = piece(self.ahead(half_way), 0, half), piece(self.ahead(half_way), half, half)
        low, high = self.clock(low.astype(bf16), high.astype(bf16))
        low, high = self.send(low, True), self.send(high, False)
        yield
        low, high = self.clock(low, high)
        nothing = jnp.zeros_like(low)
        forward = jnp.concatenate([low, nothing], axis=0)
        backward = jnp.concatenate([nothing, high], axis=0)
        for k in range(half_way - 1, 0, -1):
            forward = (forward.astype(f32) + piece(self.ahead(k))).astype(bf16)
            backward = (backward.astype(f32) + piece(self.ahead(-k))).astype(bf16)
            forward, backward = self.clock(forward, backward)
            forward, backward = self.send(forward, True), self.send(backward, False)
            yield
            forward, backward = self.clock(forward, backward)
        return forward, backward, piece(self.me)


class Line:
    def __init__(self, count, clock):
        self.count = count
        self.clock = clock
        self.me = lax.axis_index("z")
        order = list(range(0, count, 2)) + list(range(1, count, 2))[::-1]
        self.cycle = [(order[i], order[(i + 1) % count]) for i in range(count)]
        evens = (count + 1) // 2
        place = jnp.where(self.me % 2 == 0, self.me // 2, count - 1 - self.me // 2)
        self.at = []
        for k in range(count):
            spot = lax.rem(place + k, count)
            self.at.append(jnp.where(spot < evens, 2 * spot, 2 * (count - 1 - spot) + 1))

    def ahead(self, k):
        return self.at[k % self.count]

    def gather(self, block, axis):
        size = block.shape[axis]
        shape = list(block.shape)
        shape[axis] = size * self.count
        moved = self.clock.hold(block)
        pieces = [moved]
        for _ in range(1, self.count):
            moved = lax.ppermute(moved, "z", self.cycle)
            yield
            moved = self.clock(moved)
            pieces.append(moved)
        where = [
            [(i, size) if d == axis else None for d in range(2)] for i in range(len(pieces))
        ]
        return assemble(pieces, shape, where, [self.ahead(-k) for k in range(self.count)])

    def scatter(self, *parts):
        rows, width = parts[0].shape[0] // self.count, parts[0].shape[1]
        parts = self.clock.hold(*parts)

        def pieces(owner):
            return [cut(part, (owner * rows, 0), (rows, width)) for part in parts]

        moved = self.clock(add_up(*pieces(self.ahead(-1))))
        for k in range(self.count - 1, 0, -1):
            moved = lax.ppermute(moved, "z", self.cycle)
            yield
            moved = self.clock(moved)
            if k > 1:
                moved = self.clock(add_up(moved, *pieces(self.ahead(k - 1))))
        return moved, *pieces(self.me)


def shifts(count):
    return [[(i, (i + step) % count) for i in range(count)] for step in range(1, count)]


def from_axis(value, axis, count):
    me = lax.axis_index(axis)
    return [
        (lax.ppermute(value, axis, pairs), lax.rem(me - step + count, count))
        for step, pairs in enumerate(shifts(count), 1)
    ]


def to_axis(values, axis, count, dim):
    me = lax.axis_index(axis)
    return [
        lax.ppermute(
            lax.dynamic_index_in_dim(values, lax.rem(me + step, count), dim, False), axis, pairs
        )
        for step, pairs in enumerate(shifts(count), 1)
    ]


def in_order(found, axis, count, dim):
    me = lax.axis_index(axis)
    wide = jnp.stack((found[::-1] * 2)[:-1], axis=dim)
    where, sizes = [0] * wide.ndim, list(wide.shape)
    where[dim], sizes[dim] = count - 1 - me, count
    return cut(wide, where, sizes)


def exchange(values, axis, count, dim, clock):
    arrived = to_axis(values, axis, count, dim)
    yield
    found = [own_part(values, axis, dim)] + [clock(value) for value in arrived]
    return in_order(found, axis, count, dim)


def own_part(values, axis, dim):
    return lax.dynamic_index_in_dim(values, lax.axis_index(axis), dim, False)


def add_up(own, *others):
    total = own.astype(f32)
    for other in others:
        total = total + other.astype(f32)
    return total.astype(bf16)


class Grid:
    def __init__(self, nx, ny, clock):
        self.nx, self.ny, self.clock = nx, ny, clock
        self.x, self.y = lax.axis_index("x"), lax.axis_index("y")

    def gather(self, block, apart):
        rows, deep, width = block.shape
        half = rows // 2
        block = self.clock.hold(block)
        along_x, along_y = from_axis(block, "x", self.nx), from_axis(block, "y", self.ny)
        yield
        values = self.clock(*[v for v, _ in along_x + along_y])
        along_x, along_y = values[: self.nx - 1], values[self.nx - 1 :]
        left = [[w for w, _ in from_axis(v[:half], "y", self.ny)] for v in along_x]
        right = [[w for w, _ in from_axis(v[half:], "x", self.nx)] for v in along_y]
        yield
        owners = [lax.rem(self.y - k + self.ny, self.ny) for k in range(self.ny)]
        everything = slice(None)
        found = [([block, *along_y], [(everything, k) for k in range(self.ny)])]
        for i, value in enumerate(along_x):
            pieces, where = [value], [(everything, 0)]
            for j in range(self.ny - 1):
                pieces += self.clock(left[i][j], right[j][i])
                where += [(slice(0, half), j + 1), (slice(half, rows), j + 1)]
            found.append((pieces, where))
        size = rows * self.ny * deep
        if apart:
            return [
                assemble(
                    pieces,
                    (rows, self.ny, deep, width),
                    [[span, (k, None), None, None] for span, k in where],
                    owners,
                ).reshape(size, width)
                for pieces, where in found
            ]
        return assemble(
            [piece for pieces, _ in found for piece in pieces],
            (self.nx, rows, self.ny, deep, width),
            [
                [i, span, (k, None), None, None]
                for i, (_, where) in enumerate(found)
                for span, k in where
            ],
            owners,
        ).reshape(self.nx * size, width)

    def send(self, values, i, j):
        nx, ny = self.nx, self.ny
        pairs = [
            (x * ny + y, (x + i) % nx * ny + (y + j) % ny) for x in range(nx) for y in range(ny)
        ]
        return lax.ppermute(values, ("x", "y"), pairs)

    def place(self, k):
        return lax.rem(self.x - k + self.nx, self.nx)

    def turn(self, values):
        half = values.shape[1] // self.nx
        wide = jnp.concatenate([values, values], axis=1)
        found = [
            cut(wide, (0, self.place(k) * half), (values.shape[0], half)) for k in range(self.nx)
        ]
        return jnp.concatenate(found, axis=1)

    def turn_back(self, values):
        return self.turn(values)

    def scatter(self, x_first, y_first, rows):
        nx, ny = self.nx, self.ny
        count = len(x_first)
        values = self.clock.hold(*x_first, *y_first)
        values = [v.reshape(nx, rows, ny, -1, v.shape[1]) for v in values]
        one, two = values[:count], values[count:]

        def x_blocks(values):
            return [values[k] for k in range(1, nx)]

        def send_x(blocks):
            return [
                lax.ppermute(block, "x", [(i, (i - k) % nx) for i in range(nx)])
                for k, block in enumerate(blocks, 1)
            ]

        def y_blocks(values, dim):
            return [
                lax.dynamic_index_in_dim(values, lax.rem(self.y + step, ny), dim, False)
                for step in range(1, ny)
            ]

        def send_y(blocks):
            return [lax.ppermute(block, "y", pairs) for block, pairs in zip(blocks, shifts(ny))]

        def exchange_all(x_arrays, y_arrays, dim):
            groups = [x_blocks(v) for v in x_arrays] + [y_blocks(v, dim) for v in y_arrays]
            flat = self.clock(*[block for group in groups for block in group])
            flat = list(flat) if isinstance(flat, (tuple, list)) else [flat]
            groups = [[flat.pop(0) for _ in group] for group in groups]
            count = len(x_arrays)
            return [send_x(g) for g in groups[:count]] + [send_y(g) for g in groups[count:]]

        sent = exchange_all(one, two, 2)
        yield
        sent = [[self.clock(v) for v in group] for group in sent]
        one = [add_up(v[0], *group) for v, group in zip(one, sent)]
        two = [add_up(own_part(v, "y", 2), *group) for v, group in zip(two, sent[count:])]
        values = self.clock(*one, *two)
        one, two = values[:count], values[count:]
        sent = exchange_all(two, one, 1)
        yield
        sent = [[self.clock(v) for v in group] for group in sent]
        back = len(two)
        one = [add_up(own_part(v, "y", 1), *group) for v, group in zip(one, sent[back:])]
        two = [add_up(v[0], *group) for v, group in zip(two, sent[:back])]
        return jnp.concatenate([*one, *two], axis=2)


def sum_everywhere(values, sizes, clock):
    values = clock.hold(values)
    for axis, count in sizes:
        if count & (count - 1):
            values = lax.psum(values, axis)
            continue
        step = 1
        while step < count:
            other = lax.ppermute(values, axis, [(i, i ^ step) for i in range(count)])
            yield
            values = values + clock(other)
            step *= 2
    return values


def allowed_keys(low_ref, high_ref, shape):
    places = lax.broadcasted_iota(jnp.int32, shape, 1)
    return (places >= low_ref[...]) & (places < high_ref[...])


def forward_kernel(q_ref, k_ref, v_ref, low_ref, high_ref, out_ref, lse_ref):
    scores = dot_nt(q_ref[...], k_ref[...]) * (HEAD**-0.5 * log2_e)
    allowed = allowed_keys(low_ref, high_ref, scores.shape)
    scores = jnp.where(allowed, scores, masked_value)
    largest = jnp.max(scores, axis=1, keepdims=True)
    powers = jnp.exp2(scores - largest)
    totals = jnp.sum(powers, axis=1, keepdims=True)
    probs = (powers * (1.0 / totals)).astype(bf16)
    out_ref[...] = dot_nn(probs, v_ref[...]).astype(bf16)
    lse_ref[0] = largest + jnp.log2(totals)


def backward_kernel(
    q_ref, k_ref, v_ref, g_ref, low_ref, high_ref, lse_ref, cos_ref, sin_ref, all_cos_ref, all_sin_ref,
    gq_ref, gk_ref, gv_ref, k_sum, v_sum,
):
    scale = HEAD**-0.5
    step = pl.program_id(1)

    @pl.when(step == 0)
    def _():
        k_sum[...] = jnp.zeros_like(k_sum)
        v_sum[...] = jnp.zeros_like(v_sum)

    scores = dot_nt(q_ref[...], k_ref[...]) * (scale * log2_e)
    allowed = allowed_keys(low_ref, high_ref, scores.shape)
    probs = jnp.where(allowed, jnp.exp2(scores - lse_ref[0]), 0.0)
    grad_probs = dot_nt(g_ref[...], v_ref[...])
    delta = jnp.sum(probs * grad_probs, axis=1, keepdims=True)
    grad_scores = (probs * (grad_probs - delta)).astype(bf16)
    grad_q = (dot_nn(grad_scores, k_ref[...]) * scale).astype(bf16).astype(f32)
    gq_ref[...] = rotate_back(grad_q, cos_ref[...], sin_ref[...]).astype(bf16)
    k_sum[...] += dot_tn(grad_scores, q_ref[...])
    v_sum[...] += dot_tn(probs.astype(bf16), g_ref[...])

    @pl.when(step == pl.num_programs(1) - 1)
    def _():
        grad_k = (k_sum[...] * scale).astype(bf16).astype(f32)
        gk_ref[...] = rotate_back(grad_k, all_cos_ref[...], all_sin_ref[...]).astype(bf16)
        gv_ref[...] = v_sum[...].astype(bf16)


params = pltpu.CompilerParams(vmem_limit_bytes=56 * 2**20)
cost = pl.CostEstimate(flops=0, bytes_accessed=0, transcendentals=0)


def assemble(pieces, shape, where, places):
    def kernel(places_ref, *refs):
        out, arrived = refs[len(pieces)], refs[-1]

        def index(part):
            if not isinstance(part, tuple):
                return slice(None) if part is None else part
            k, size = part
            if size is None:
                return places_ref[k]
            return pl.ds(pl.multiple_of(places_ref[k] * size, size), size)

        copies = [
            pltpu.make_async_copy(refs[i], out.at[tuple(map(index, parts))], arrived.at[i])
            for i, parts in enumerate(where)
        ]
        for copy in copies:
            copy.start()
        for copy in copies:
            copy.wait()

    return pl.pallas_call(
        kernel,
        grid_spec=pltpu.PrefetchScalarGridSpec(
            num_scalar_prefetch=1,
            grid=(1,),
            in_specs=[pl.BlockSpec(memory_space=pl.ANY)] * len(pieces),
            out_specs=pl.BlockSpec(tuple(shape), lambda i, places: (0,) * len(shape)),
            scratch_shapes=[pltpu.SemaphoreType.DMA((len(pieces),))],
        ),
        out_shape=jax.ShapeDtypeStruct(tuple(shape), pieces[0].dtype),
        compiler_params=params,
        cost_estimate=cost,
        name="assemble",
    )(jnp.stack(places).astype(jnp.int32), *pieces)


def lay_out(name, pieces, shape, kind, where, places=None):
    places = jnp.zeros((1,), jnp.int32) if places is None else places

    def kernel(places_ref, *refs):
        out = refs[-1]
        out[...] = jnp.zeros_like(out)
        for i, part, columns in where:
            value = refs[i][part].astype(kind)
            if isinstance(columns, list):
                place, start = columns
                size = value.shape[-1]
                begin = pl.multiple_of(places_ref[place] + start, LANES)
                out[:, pl.ds(begin, size)] = value
            else:
                out[:, columns : columns + value.shape[-1]] = value

    return pl.pallas_call(
        kernel,
        grid_spec=pltpu.PrefetchScalarGridSpec(
            num_scalar_prefetch=1,
            grid=(1,),
            in_specs=[
                pl.BlockSpec(a.shape, lambda i, places, n=a.ndim: (0,) * n) for a in pieces
            ],
            out_specs=pl.BlockSpec(shape, lambda i, places: (0, 0)),
        ),
        out_shape=jax.ShapeDtypeStruct(shape, kind),
        compiler_params=params,
        cost_estimate=cost,
        name=name,
    )(places, *pieces)


def attention_specs(count, heads, block):
    def one(column):
        return pl.BlockSpec((block, HEAD), lambda h, i: (i, column + h))

    def whole(column):
        return pl.BlockSpec((count, HEAD), lambda h, i: (0, column + h))

    edge = pl.BlockSpec((block, 1), lambda h, i: (i, 0))
    lse = pl.BlockSpec((1, block, 1), lambda h, i: (h, i, 0))
    return (one, whole, edge, lse)


def attend_forward(packed, low, high):
    count, heads = packed.shape[0], packed.shape[1] // (3 * HEAD)
    block = min(512, count)
    one, whole, edge, lse = attention_specs(count, heads, block)
    return pl.pallas_call(
        forward_kernel,
        grid=(heads, count // block),
        in_specs=[one(0), whole(heads), whole(2 * heads), edge, edge],
        out_specs=[one(0), lse],
        out_shape=[
            jax.ShapeDtypeStruct((count, heads * HEAD), bf16),
            jax.ShapeDtypeStruct((heads, count, 1), f32),
        ],
        compiler_params=params,
        cost_estimate=cost,
        name="attend_forward",
    )(packed, packed, packed, low, high)


def attend_backward(packed, grads, low, high, log_sums, cosine, sine):
    count, heads = packed.shape[0], packed.shape[1] // (3 * HEAD)
    block = min(512, count)
    one, whole, edge, lse = attention_specs(count, heads, block)
    shape = jax.ShapeDtypeStruct((count, heads * HEAD), bf16)
    turn = pl.BlockSpec((block, HEAD), lambda h, i: (i, 0))
    turn_all = pl.BlockSpec((count, HEAD), lambda h, i: (0, 0))
    return pl.pallas_call(
        backward_kernel,
        grid=(heads, count // block),
        in_specs=[one(0), whole(heads), whole(2 * heads), one(0), edge, edge, lse]
        + [turn, turn, turn_all, turn_all],
        out_specs=[one(0), whole(0), whole(0)],
        out_shape=[shape, shape, shape],
        scratch_shapes=[pltpu.VMEM((count, HEAD), f32), pltpu.VMEM((count, HEAD), f32)],
        compiler_params=params,
        cost_estimate=cost,
        name="attend_backward",
    )(packed, packed, packed, grads, low, high, log_sums, cosine, sine, cosine, sine)


def over_rows(
    name, body, block, rows, whole, outs, sums=(), places=None, scratch=(), first_map=None, count=None
):
    count = count or rows[-1].shape[0]
    places = jnp.zeros((1,), jnp.int32) if places is None else places

    def kernel(places_ref, *refs):
        n, m, k = len(rows), len(rows) + len(whole), len(rows) + len(whole) + len(outs)
        if sums:

            @pl.when(pl.program_id(0) == 0)
            def _():
                for ref in refs[k : k + len(sums)]:
                    ref[...] = jnp.zeros_like(ref)

        body(refs[:n], refs[n:m], places_ref, refs[m:k], refs[k:])

    room = [pltpu.VMEM((block, width), kind) for width, kind in scratch]

    def by_row(i, places):
        return (i, 0)

    def fixed(i, places):
        return (0, 0)

    return pl.pallas_call(
        kernel,
        grid_spec=pltpu.PrefetchScalarGridSpec(
            num_scalar_prefetch=1,
            grid=(count // block,),
            in_specs=[
                pl.BlockSpec((block, a.shape[1]), first_map if first_map and not i else by_row)
                for i, a in enumerate(rows)
            ]
            + [pl.BlockSpec(a.shape, fixed) for a in whole],
            out_specs=[pl.BlockSpec((block, width), by_row) for width, _ in outs]
            + [pl.BlockSpec((1, width), fixed) for width in sums],
            scratch_shapes=room,
        ),
        out_shape=[jax.ShapeDtypeStruct((count, width), kind) for width, kind in outs]
        + [jax.ShapeDtypeStruct((1, width), f32) for width in sums],
        compiler_params=params,
        cost_estimate=cost,
        name=name,
    )(places, *rows, *whole)


def columns_of(ref, place, width):
    return ref.at[:, pl.ds(pl.multiple_of(place * width, width), width)]


def project_pieces(left_ref, pieces, places_ref):
    total = None
    for i, piece in enumerate(pieces):
        depth = piece.shape[0]
        term = dot_nn(columns_of(left_ref, places_ref[i], depth)[...], piece[...])
        total = term if total is None else total + term
    return total


def tile_split(width, count):
    tiles = -(-width // LANES)
    least, extra = divmod(tiles, count)
    sizes = [least + (1 if i < extra else 0) for i in range(count)]
    starts = [sum(sizes[:i]) for i in range(count)]
    return (starts, sizes, max(sizes))


class Values:
    pass


ORDER = (
    "tokens_in", "qkv_in", "tokens_in", "gate_up_pack", "tokens_in", "down_pack", "qkv_in", "out_in",
    "tokens_in", "tables", "turn", "qkv_in", "tokens_in", "out_in", "gate_up_in", "qkv_in", "project",
    "out_grad_in", "attend", "to_y", "out_grad_in", "to_y", "attended_in", "out_in", "attended_in",
    "gate_up_in", "out_grad_in", "out_in", "attended_in", "out_in", "down_in", "attended_in", "out_grad_in",
    "gate_up_in", "second_norm", "normed_core", "gate_up_in", "down_in", "down_in", "normed_core",
    "out_grad_core", "gate_up", "down_in", "out_grad_core", "down_in", "act", "other_parts", "own_parts",
    "other_parts", "parts_out", "first_share", "second_share", "ffn_grad", "parts_out", "parts_out",
    "ffn_grad", "parts_out", "second_back", "heads_in", "ffn_grad", "heads_in", "ffn_back", "attend_back",
    "qkv_back", "first_back", "normed_out", "qkv_back", "small", "grad_attn_in", "ffn_back", "normed_out",
    "qkv_back", "small", "ffn_rows", "normed_out", "grad_attn_in", "out_back", "small", "normed_out",
    "out_back", "small", "qkv_back", "qkv_rows", "normed_out", "out_back", "small", "output",
    "first_norm_tokens", "small", "out_back", "out_rows",
)


def per_device(
    tokens,
    ln1_gain,
    ln1_bias,
    w_qkv,
    b_qkv,
    w_out,
    b_out,
    ln2_gain,
    ln2_bias,
    w_gate,
    b_gate,
    w_up,
    b_up,
    w_down,
    b_down,
    protein_lengths,
    prefix_lengths,
    out_grad,
):
    nx, nz, ny = (lax.axis_size(axis) for axis in ("x", "z", "y"))
    x, core, z, y = (lax.axis_index(axis) for axis in EVERY)
    sizes_of = (("core", 2), ("x", nx), ("y", ny), ("z", nz))
    own_rows, width = tokens.shape
    weight_rows = w_qkv.shape[0]
    ffn_width = w_gate.shape[1]
    seq_count, team_count = nz * ny, 2 * nz
    count = own_rows * seq_count
    line_rows = nz * own_rows
    own_heads = HEADS // seq_count
    own_width = own_heads * HEAD
    clock = Clock()
    ring = Ring(nz, ny, clock)
    line = Line(nz, clock)
    grid = Grid(nx, ny, clock)
    me = ring.me

    def all_to_all(values, axes):
        return lax.all_to_all(values, axes, split_axis=0, concat_axis=0, tiled=True)

    def other_core(values):
        return lax.ppermute(values, "core", [(0, 1), (1, 0)])

    starts, sizes, most = tile_split(ffn_width, team_count)
    own_ffn = most * LANES
    padded = (starts[-1] + most) * LANES
    first_tile = jnp.asarray(starts, jnp.int32)[core * nz + z] * LANES
    split = 3 * own_ffn // 2 // LANES * LANES
    half_places = jnp.stack([lax.rem(x - k + nx, nx) for k in range(nx)])
    places = jnp.concatenate([half_places * 2 + core, half_places * 2 + 1 - core])
    cotangent = out_grad.astype(f32)
    pieces_of = PIECES if PIECES % nx == 0 else nx
    piece_width = width // pieces_of
    plan = Plan()
    v = Values()

    def ffn_blocks(weight, mask):
        whole = jnp.pad(weight, ((0, 0), (0, padded - ffn_width)))
        pieces = []
        for start, size in zip(starts, sizes):
            piece = whole[:, start * LANES : (start + most) * LANES]
            if mask and size < most:
                piece = jnp.pad(piece[:, : size * LANES], ((0, 0), (0, (most - size) * LANES)))
            pieces.append(piece)
        return jnp.stack(pieces)

    def ffn_bias(bias):
        return cut(jnp.pad(bias, (0, padded - ffn_width)), (first_tile,), (own_ffn,))

    def row(values):
        return values.reshape(1, -1)

    def low_nt(left, right):
        return dot_nt(left, right).astype(bf16)

    def low_tn(left, right):
        return dot_tn(left, right).astype(bf16)

    @plan.transfer
    def tokens_in():
        v.tokens_all = clock((yield from ring.gather(tokens)))

    @plan.transfer
    def qkv_in():
        blocks = (
            w_qkv.reshape(weight_rows, 3, seq_count, own_width)
            .transpose(2, 0, 1, 3)
            .reshape(seq_count, weight_rows, 3 * own_width)
        )
        moved = all_to_all(clock.hold(blocks), GROUP)
        yield
        rows = clock(moved).reshape(seq_count * weight_rows, 3 * own_width)
        from_x = from_axis(rows, "x", nx)
        yield
        pieces = [rows] + [clock(value) for value, _ in from_x]
        from_core = [other_core(value) for value in pieces]
        yield
        v.qkv_pieces = pieces + [clock(value) for value in from_core]

    @plan.transfer
    def out_in():
        block = jnp.broadcast_to(w_out[None], (nz, weight_rows, width))
        moved = all_to_all(clock.hold(block), "z")
        yield
        pieces = yield from grid.gather(clock(moved), True)
        pieces = list(clock(*pieces))
        from_core = [other_core(piece) for piece in pieces]
        yield
        v.out_pieces = pieces + [clock(value) for value in from_core]

    @plan.step
    def gate_up_pack():
        v.gate_up_blocks = clock.run(
            lambda gate, up: jnp.concatenate(
                [ffn_blocks(gate, False), ffn_blocks(up, False)], axis=2
            ),
            w_gate,
            w_up,
        )

    @plan.step
    def down_pack():
        v.down_blocks = clock.run(lambda down: ffn_blocks(down, True), w_down)

    @plan.transfer
    def gate_up_in():
        moved = all_to_all(clock.hold(v.gate_up_blocks), TEAM)
        yield
        v.gate_up_own = clock((yield from grid.gather(clock(moved), False)))

    @plan.transfer
    def down_in():
        moved = all_to_all(clock.hold(v.down_blocks), TEAM)
        yield
        v.down_moved = clock(moved)
        yield
        v.down_own = clock((yield from grid.gather(v.down_moved, False)))

    @plan.step
    def tables():
        def make(lengths, prefixes):
            position, low, high = group_layout(lengths[0], prefixes[0], count)
            return (*rotary_tables(position), low[:, None], high[:, None])

        v.cosine, v.sine, v.low, v.high = clock.run(make, protein_lengths, prefix_lengths)

    def project_kernel(rows, whole, places_ref, outs, sums):
        tokens_ref, cos_ref, sin_ref = rows
        gain, bias, qkv_bias, *pieces = whole
        normed_ref, packed_ref = outs
        normed = layer_norm(tokens_ref[...].astype(f32), gain[...], bias[...])
        normed_ref[...] = normed.astype(bf16)
        raw = project_pieces(normed_ref, pieces, places_ref) + qkv_bias[...]
        for i in range(3 * own_heads):
            piece = raw[:, i * HEAD : (i + 1) * HEAD]
            if i < 2 * own_heads:
                piece = rotate(piece, cos_ref[...], sin_ref[...])
            packed_ref[:, i * HEAD : (i + 1) * HEAD] = piece.astype(bf16)

    @plan.step
    def project():
        qkv_bias = cut(b_qkv.reshape(3, width), (0, me * own_width), (3, own_width))
        v.normed, v.packed = clock.run(
            lambda tokens_all, *pieces: over_rows(
                "project",
                project_kernel,
                256,
                [tokens_all, v.cosine, v.sine],
                [row(ln1_gain), row(ln1_bias), row(qkv_bias), *pieces],
                [(width, bf16), (3 * own_width, bf16)],
                places=places,
            ),
            v.tokens_all,
            *v.qkv_pieces,
        )

    @plan.step
    def attend():
        v.head_result, v.log_sums = clock.run(
            lambda values: attend_forward(values, v.low, v.high), v.packed
        )

    @plan.transfer
    def to_y():
        result = v.head_result.reshape(nz, ny, own_rows, own_width)
        moved = yield from exchange(result, "y", ny, 1, clock)
        moved = moved.transpose(0, 2, 1, 3).reshape(line_rows, ny * own_width)
        v.head_columns = clock(moved)

    @plan.transfer
    def attended_in():
        v.attended = clock((yield from line.gather(v.head_columns, 1)))

    @plan.step
    def turn():
        v.out_grad_turned = clock.run(grid.turn, out_grad)

    @plan.transfer
    def out_grad_in():
        found = yield from line.gather(v.out_grad_turned, 0)
        v.grad_out_line = clock(found)

    @plan.transfer
    def out_grad_core():
        moved = other_core(v.grad_out_line)
        yield
        both = [v.grad_out_line, clock(moved)]
        v.grad_out_all = clock(jnp.concatenate(both, axis=0))

    def second_kernel(rows, whole, places_ref, outs, more):
        tokens_ref, attended_ref = rows
        gain, bias, out_bias, *pieces = whole
        attn = project_pieces(attended_ref, pieces, places_ref) + out_bias[...]
        hidden = tokens_ref[...].astype(f32) + attn
        outs[0][...] = hidden
        (normed_ref,) = more
        normed_ref[...] = layer_norm(hidden, gain[...], bias[...]).astype(bf16)
        for k in range(nx):
            place = places_ref[2 * nx + k]
            whole = columns_of(normed_ref, place, width // nx)
            for j in range(pieces_of // nx):
                out = outs[1 + k * (pieces_of // nx) + j]
                out[...] = whole[:, j * piece_width : (j + 1) * piece_width]

    @plan.step
    def second_norm():
        hidden_in, *v.normed_line = clock.run(
            lambda tokens, attended, *pieces: over_rows(
                "second_norm",
                second_kernel,
                own_rows,
                [tokens, attended],
                [row(ln2_gain), row(ln2_bias), row(b_out), *pieces],
                [(width, f32)] + [(piece_width, bf16)] * pieces_of,
                places=jnp.concatenate([places, half_places, row(y)[0]]),
                scratch=[(width, bf16)],
                first_map=lambda i, places: (i * ny + places[3 * nx], 0),
                count=line_rows,
            ),
            v.tokens_all,
            v.attended,
            *v.out_pieces,
        )
        v.hidden_own = cut(hidden_in, (z * own_rows, 0), (own_rows, width))

    @plan.transfer
    def normed_core():
        moved = [other_core(piece) for piece in v.normed_line]
        yield
        moved = clock(*moved)
        where = [
            [slice(j * line_rows, (j + 1) * line_rows), slice(i * piece_width, (i + 1) * piece_width)]
            for j in range(2)
            for i in range(pieces_of)
        ]
        v.normed_two = clock(
            assemble([*v.normed_line, *moved], (2 * line_rows, width), where, [me])
        )

    @plan.step
    def gate_up():
        bias = jnp.concatenate([ffn_bias(b_gate), ffn_bias(b_up)])
        v.gate_up = clock.run(lambda a, b: dot_nn(a, b) + bias, v.normed_two, v.gate_up_own)

    @plan.step
    def act():
        def make(grads, weight, gate_up):
            grad_act = dot_nn(grads, weight)
            values, pull = jax.vjp(geglu, gate_up[:, :own_ffn], gate_up[:, own_ffn:])
            grads = [g.astype(bf16) for g in pull(grad_act)]
            return jnp.concatenate(grads, axis=1), values.astype(bf16)

        v.grad_gate_up, v.act = clock.run(make, v.grad_out_all, v.down_own, v.gate_up)

    def both_parts(grads, gate_up, act, down):
        return jnp.concatenate([low_nt(grads, gate_up), low_nt(act, down)], axis=1)

    @plan.transfer
    def other_parts():
        found = clock.run(
            both_parts, v.grad_gate_up[line_rows:], v.gate_up_own, v.act[line_rows:], v.down_own
        )
        moved = other_core(found)
        yield
        v.other_parts = clock(moved)

    @plan.step
    def own_parts():
        v.own_parts = clock.run(
            both_parts, v.grad_gate_up[:line_rows], v.gate_up_own, v.act[:line_rows], v.down_own
        )

    @plan.transfer
    def parts_out():
        v.two_parts = yield from line.scatter(v.own_parts, v.other_parts)

    @plan.step
    def first_share():
        v.first_share = clock.run(low_tn, v.normed_two, v.grad_gate_up[:, :split])

    @plan.step
    def second_share():
        v.second_share, v.third_share = clock.run(
            lambda a, b, c, d: (low_tn(a, b[:, split:]), low_tn(c, d)),
            v.normed_two,
            v.grad_gate_up,
            v.grad_out_all,
            v.act,
        )

    @plan.transfer
    def ffn_grad():
        found = yield from grid.scatter(
            [v.first_share], [v.second_share, v.third_share], team_count
        )
        v.ffn_share = clock(found)

    @plan.transfer
    def ffn_back():
        moved = all_to_all(clock.hold(v.ffn_share), TEAM)
        yield
        v.ffn_back = clock(moved)

    def second_back_kernel(rows, whole, places_ref, outs, more):
        *sums, grads_ref = more
        *terms, hidden, out_grad_ref = rows
        gain, *pieces = whole
        turned = sum(term[:, :width].astype(f32) for term in terms)
        part = width // nx
        for k in range(nx):
            place = places_ref[2 * nx + k]
            columns_of(grads_ref, place, part)[...] = turned[:, k * part : (k + 1) * part]
        grads = grads_ref[...]
        unit, inverse = norm_parts(hidden[...])
        cotangent = out_grad_ref[...].astype(f32)
        total = cotangent + layer_norm_back(unit, inverse, gain[...], grads)
        low = total.astype(bf16)
        outs[0][...] = total
        outs[1][...] = low
        for i, piece in enumerate(pieces):
            part = dot_nt(low, piece[...]).astype(bf16)
            columns_of(outs[2], places_ref[i], piece.shape[0])[...] = part
        for ref, values in zip(sums, (grads * unit, grads, low.astype(f32), cotangent)):
            ref[...] += jnp.sum(values, axis=0, keepdims=True)

    @plan.step
    def second_back():
        v.grad_hidden, v.grad_attn, v.grad_attended, *v.second_sums = clock.run(
            lambda *values: over_rows(
                "second_norm_back",
                second_back_kernel,
                own_rows,
                values[:5],
                [row(ln2_gain), *values[5:]],
                [(width, f32), (width, bf16), (width, bf16)],
                [width] * 4,
                places=jnp.concatenate([places, half_places]),
                scratch=[(width, f32)],
            ),
            *v.two_parts,
            v.hidden_own,
            out_grad,
            *v.out_pieces,
        )

    @plan.transfer
    def heads_in():
        blocks = v.grad_attended.reshape(own_rows, seq_count, own_width).transpose(1, 0, 2)
        moved = all_to_all(clock.hold(blocks), GROUP)
        yield
        v.grad_heads = clock(moved).reshape(count, own_width)

    @plan.step
    def attend_back():
        v.grad_parts = clock.run(
            lambda *values: attend_backward(*values, v.low, v.high, v.log_sums, v.cosine, v.sine),
            v.packed,
            v.grad_heads,
        )

    def first_back_kernel(rows, whole, places_ref, outs, more):
        *sums, part_ref = more
        grads, tokens_ref = rows[:3], rows[3]
        unit, _ = norm_parts(tokens_ref[...].astype(f32))
        for i, piece in enumerate(whole):
            part = None
            for j, grad in enumerate(grads):
                term = dot_nt(grad[...], piece[:, j * own_width : (j + 1) * own_width])
                part = term if part is None else part + term
            depth = piece.shape[0]
            columns_of(outs[0], places_ref[i], depth)[...] = part.astype(bf16)
            columns_of(part_ref, places_ref[i], depth)[...] = part
        part = part_ref[...]
        sums[0][...] += jnp.sum(part * unit, axis=0, keepdims=True)
        sums[1][...] += jnp.sum(part, axis=0, keepdims=True)
        for j, grad in enumerate(grads):
            total = jnp.sum(grad[...].astype(f32), axis=0, keepdims=True)
            sums[2][:, j * own_width : (j + 1) * own_width] += total

    @plan.step
    def first_back():
        v.normed_part, *v.first_sums = clock.run(
            lambda *values: over_rows(
                "first_norm_back",
                first_back_kernel,
                256,
                values[:4],
                values[4:],
                [(width, bf16)],
                [width, width, 3 * own_width],
                places=places,
                scratch=[(width, f32)],
            ),
            *v.grad_parts,
            v.tokens_all,
            *v.qkv_pieces,
        )

    @plan.transfer
    def normed_out():
        v.one_parts = yield from ring.scatter(v.normed_part)

    @plan.transfer
    def small():
        sums = [*v.second_sums, *v.first_sums[:2]]
        bias_gate_up = jnp.sum(v.grad_gate_up.astype(f32), axis=0, keepdims=True)
        where = [(i, (slice(None), slice(None)), i * width) for i in range(len(sums))]
        start = len(sums) * width
        for i in range(3):
            part = (slice(None), slice(i * own_width, (i + 1) * own_width))
            where.append((len(sums), part, [0, start + i * width]))
        start += 3 * width
        for i in range(2):
            part = (slice(None), slice(i * own_ffn, (i + 1) * own_ffn))
            where.append((len(sums) + 1, part, [1, start + i * padded]))
        values = clock.run(
            lambda *values: lay_out(
                "small",
                values,
                (1, start + 2 * padded),
                f32,
                where,
                jnp.stack([me * own_width, first_tile]).astype(jnp.int32),
            ),
            *sums,
            v.first_sums[2],
            bias_gate_up,
        )
        v.small = (yield from sum_everywhere(values, sizes_of, clock))[0]

    @plan.transfer
    def qkv_back():
        share = clock.run(
            lambda a, *b: low_tn(a, jnp.concatenate(b, axis=1)), v.normed, *v.grad_parts
        )
        share = share.reshape(nx, 2, seq_count * weight_rows, 3 * own_width)
        for axis, size, dim in (("core", 2, 1), ("x", nx, 0)):
            arrived = to_axis(share, axis, size, dim)
            yield
            share = clock(add_up(own_part(share, axis, dim), *[clock(a) for a in arrived]))
        moved = all_to_all(share.reshape(seq_count, weight_rows, 3 * own_width), GROUP)
        yield
        v.qkv_back = clock(moved)

    @plan.transfer
    def grad_attn_in():
        blocks = clock.hold(v.grad_attn).reshape(own_rows, nz, width // nz).transpose(1, 0, 2)
        found = yield from exchange(blocks, "z", nz, 0, clock)
        v.grad_attn_block = clock(found).reshape(line_rows, width // nz)

    @plan.transfer
    def out_back():
        share = clock.run(low_tn, v.attended, v.grad_attn_block)
        share = share.reshape(nx, 2, nz, ny, weight_rows, width // nz)
        arrived = to_axis(share, "core", 2, 1)
        yield
        share = clock(add_up(own_part(share, "core", 1), *[clock(a) for a in arrived]))

        def part_of(i, j):
            where = (lax.rem(x + i, nx), 0, lax.rem(y + j, ny), 0, 0)
            found = cut(share, where, (1, nz, 1, weight_rows, width // nz))
            return found.reshape(nz, weight_rows, width // nz)

        others = [(i, j) for i in range(nx) for j in range(ny) if i or j]
        arrived = [grid.send(part_of(i, j), i, j) for i, j in others]
        yield
        share = clock(add_up(part_of(0, 0), *[clock(a) for a in arrived]))
        v.out_back = yield from exchange(share, "z", nz, 0, clock)

    @plan.step
    def output():
        v.output = clock.run(
            lambda hidden, *terms: (
                grid.turn_back(sum(term[:, width:].astype(f32) for term in terms))
                + hidden
                + b_down
            ).astype(bf16),
            v.hidden_own,
            *v.two_parts,
        )

    def last_kernel(rows, whole, places_ref, outs, sums):
        below, above, own, tokens_ref, hidden_grad = rows
        grads = below[...].astype(f32) + above[...].astype(f32) + own[...]
        unit, inverse = norm_parts(tokens_ref[...].astype(f32))
        total = hidden_grad[...] + layer_norm_back(unit, inverse, whole[0][...], grads)
        outs[0][...] = total.astype(bf16)

    @plan.step
    def first_norm_tokens():
        v.tokens_grad = clock.run(
            lambda *values: over_rows(
                "first_norm_tokens",
                last_kernel,
                own_rows,
                values,
                [row(ln1_gain)],
                [(width, bf16)],
            )[0],
            *v.one_parts,
            tokens,
            v.grad_hidden,
        )

    @plan.step
    def ffn_rows():
        def rows_of(moved, which):
            everything = slice(None)
            where = []
            for i in range(team_count):
                size = min(sizes[i] * LANES, ffn_width - starts[i] * LANES)
                span = slice(which * own_ffn, which * own_ffn + size)
                where.append((0, (i, everything, span), starts[i] * LANES))
            return lay_out("ffn_rows", [moved], (weight_rows, ffn_width), f32, where)

        v.ffn_rows = clock.run(lambda moved: [rows_of(moved, i) for i in range(3)], v.ffn_back)

    @plan.step
    def qkv_rows():
        everything = slice(None)
        where = [
            (0, (i, everything, slice(j * own_width, (j + 1) * own_width)), j * width + i * own_width)
            for i in range(seq_count)
            for j in range(3)
        ]
        v.qkv_rows = clock.run(
            lambda moved: lay_out("qkv_rows", [moved], (weight_rows, 3 * width), f32, where),
            v.qkv_back,
        )

    @plan.step
    def out_rows():
        everything = slice(None)
        where = [(0, (i, everything, everything), i * (width // nz)) for i in range(nz)]
        v.out_rows = clock.run(
            lambda moved: lay_out("out_rows", [moved], (weight_rows, width), f32, where),
            v.out_back,
        )

    plan.run(ORDER)


    gain_two, bias_two, b_out_grad, b_down_grad, gain_one, bias_one = (
        v.small[i * width : (i + 1) * width] for i in range(6)
    )
    b_qkv_grad = v.small[6 * width : 9 * width]
    b_gate_grad = v.small[9 * width : 9 * width + ffn_width]
    b_up_grad = v.small[9 * width + padded : 9 * width + padded + ffn_width]
    return (
        v.output,
        v.tokens_grad,
        gain_one,
        bias_one,
        v.qkv_rows,
        b_qkv_grad,
        v.out_rows,
        b_out_grad,
        gain_two,
        bias_two,
        v.ffn_rows[0],
        b_gate_grad,
        v.ffn_rows[1],
        b_up_grad,
        v.ffn_rows[2],
        b_down_grad,
    )


def solution(mesh):
    nx, seq_count = mesh.shape["batch"] // 2, mesh.shape["seq"]
    nz = 4 if seq_count % 4 == 0 else seq_count
    grid = Mesh(mesh.devices.reshape(nx, 2, nz, seq_count // nz), EVERY)
    rows = P(EVERY, None)
    lengths = P(("x", "core"), None)
    in_specs = (
        rows, P(), P(), rows, P(), rows, P(), P(), P(), rows, P(), rows, P(), rows, P(),
        lengths, lengths, rows,
    )
    out_specs = (
        rows, rows, P(), P(), rows, P(), rows, P(), P(), P(), rows, P(), rows, P(), rows, P(),
    )
    return jax.shard_map(
        per_device, mesh=grid, in_specs=in_specs, out_specs=out_specs, check_vma=False
    )
```

```python
import math

import jax
import jax.numpy as jnp
from jax import lax
from jax.experimental import pallas as pl
from jax.experimental.pallas import tpu as pltpu
from jax.sharding import Mesh
from jax.sharding import PartitionSpec as P

HEADS = 16
HEAD = 128
LANES = 128
PIECES = 4

epsilon = 1e-05
masked_value = -1000000000.0
log2_e = math.log2(math.e)
bf16 = jnp.bfloat16
f32 = jnp.float32

EVERY = ("x", "core", "z", "y")
GROUP = ("z", "y")
TEAM = ("core", "z")


def norm_parts(values):
    average = jnp.mean(values, axis=-1, keepdims=True)
    centered = values - average
    spread = jnp.mean(centered * centered, axis=-1, keepdims=True)
    inverse = lax.rsqrt(spread + epsilon)
    return (centered * inverse, inverse)


def layer_norm(values, gain, bias):
    unit, _ = norm_parts(values)
    return unit * gain + bias


def layer_norm_back(unit, inverse, gain, grad):
    scaled = grad * gain
    first = jnp.mean(scaled, axis=-1, keepdims=True)
    second = jnp.mean(scaled * unit, axis=-1, keepdims=True)
    return inverse * (scaled - first - unit * second)


def gelu_tanh(values):
    return (
        0.5
        * values
        * (1.0 + jnp.tanh(0.7978845608028654 * (values + 0.044715 * values * values * values)))
    )


def geglu(gate, upper):
    return gelu_tanh(gate) * upper


def group_layout(lengths, prefixes, count):
    ends = jnp.cumsum(lengths)
    starts = ends - lengths
    places = jnp.arange(count, dtype=jnp.int32)
    member = ((places[:, None] >= starts[None, :]) & (places[:, None] < ends[None, :])).astype(
        jnp.int32
    )
    first = jnp.sum(member * starts[None, :], axis=1)
    limits = starts + jnp.minimum(prefixes, lengths)
    bound = jnp.sum(member * limits[None, :], axis=1)
    return (places - first, first, jnp.maximum(places + 1, bound))


def rotary_tables(position):
    half_size = HEAD // 2
    rates = jnp.exp(jnp.arange(half_size, dtype=f32) * (-2.0 * math.log(10000.0) / HEAD))
    angles = position.astype(f32)[:, None] * rates[None, :]
    cosine = jnp.cos(angles)
    sine = jnp.sin(angles)
    return (jnp.concatenate([cosine, cosine], axis=1), jnp.concatenate([-sine, sine], axis=1))


def swap_halves(values):
    half_size = HEAD // 2
    return jnp.concatenate([values[:, half_size:], values[:, :half_size]], axis=1)


def rotate(values, cosine, sine):
    return values * cosine + swap_halves(values) * sine


def rotate_back(values, cosine, sine):
    return values * cosine + swap_halves(values * sine)


def dot_nn(left, right):
    return lax.dot_general(left, right, (((1,), (0,)), ((), ())), preferred_element_type=f32)


def dot_nt(left, right):
    return lax.dot_general(left, right, (((1,), (1,)), ((), ())), preferred_element_type=f32)


def dot_tn(left, right):
    return lax.dot_general(left, right, (((0,), (0,)), ((), ())), preferred_element_type=f32)


def put(total, piece, where):
    return lax.dynamic_update_slice(total, piece, [jnp.int32(i) for i in where])


def cut(values, where, sizes):
    return lax.dynamic_slice(values, [jnp.int32(i) for i in where], sizes)


class Clock:
    def __init__(self):
        self.last = None

    def hold(self, *values):
        if self.last is None:
            return values if len(values) > 1 else values[0]
        held = lax.optimization_barrier((*values, self.last))[:-1]
        return held if len(values) > 1 else held[0]

    def run(self, step, *values):
        held = self.hold(*values)
        out = step(*held) if len(values) > 1 else step(held)
        return self(*out) if isinstance(out, (tuple, list)) else self(out)

    def __call__(self, *values):
        given = values if self.last is None else (*values, self.last)
        out = lax.optimization_barrier(given)
        self.last = out[0]
        out = out[: len(values)]
        return out if len(values) > 1 else out[0]


class Plan:
    def __init__(self):
        self.steps, self.transfers, self.running = {}, {}, {}

    def step(self, function):
        self.steps[function.__name__] = function
        return function

    def transfer(self, function):
        self.transfers[function.__name__] = function
        return function

    def run(self, order):
        for i, name in enumerate(order):
            with jax.named_scope(name):
                if name in self.steps:
                    self.steps[name]()
                    continue
                if name not in self.running:
                    self.running[name] = self.transfers[name]()
                if name in order[i + 1 :]:
                    next(self.running[name], None)
                    continue
                for _ in self.running[name]:
                    pass


class Ring:
    def __init__(self, rows, columns, clock):
        count = rows * columns
        self.count = count
        self.clock = clock
        if columns == 2:
            order = [2 * z for z in range(rows)] + [2 * z + 1 for z in reversed(range(rows))]
        else:
            order = list(range(count))
        self.forward = [(order[i], order[(i + 1) % count]) for i in range(count)]
        self.backward = [(b, a) for a, b in self.forward]
        me = lax.axis_index(GROUP)
        if columns == 2:
            place = jnp.where(me % 2 == 0, me // 2, count - 1 - me // 2)
        else:
            place = me
        self.me = me
        self.at = []
        for k in range(count):
            spot = lax.rem(place + k, count)
            if columns == 2:
                spot = jnp.where(spot < rows, 2 * spot, 2 * (count - 1 - spot) + 1)
            self.at.append(spot)

    def ahead(self, k):
        return self.at[k % self.count]

    def send(self, values, forward):
        return lax.ppermute(values, GROUP, self.forward if forward else self.backward)

    def gather(self, block):
        half_way = self.count // 2
        rows, width = block.shape
        half = rows // 2
        block = self.clock.hold(block)
        total = jnp.zeros((self.count * rows, width), block.dtype)
        total = put(total, block, (self.me * rows, 0))
        ahead = behind = block
        for k in range(1, half_way):
            behind, ahead = self.send(behind, True), self.send(ahead, False)
            yield
            behind, ahead = self.clock(behind, ahead)
            total = put(total, behind, (self.ahead(-k) * rows, 0))
            total = put(total, ahead, (self.ahead(k) * rows, 0))
        behind, ahead = self.send(behind[:half], True), self.send(ahead[half:], False)
        yield
        behind, ahead = self.clock(behind, ahead)
        total = put(total, behind, (self.ahead(half_way) * rows, 0))
        return put(total, ahead, (self.ahead(half_way) * rows + half, 0))

    def scatter(self, parts):
        half_way = self.count // 2
        rows, width = parts.shape[0] // self.count, parts.shape[1]
        half = rows // 2
        parts = self.clock.hold(parts)

        def piece(owner, start=0, size=rows):
            return cut(parts, (owner * rows + start, 0), (size, width)).astype(f32)

        low, high = piece(self.ahead(half_way), 0, half), piece(self.ahead(half_way), half, half)
        low, high = self.clock(low.astype(bf16), high.astype(bf16))
        low, high = self.send(low, True), self.send(high, False)
        yield
        low, high = self.clock(low, high)
        nothing = jnp.zeros_like(low)
        forward = jnp.concatenate([low, nothing], axis=0)
        backward = jnp.concatenate([nothing, high], axis=0)
        for k in range(half_way - 1, 0, -1):
            forward = (forward.astype(f32) + piece(self.ahead(k))).astype(bf16)
            backward = (backward.astype(f32) + piece(self.ahead(-k))).astype(bf16)
            forward, backward = self.clock(forward, backward)
            forward, backward = self.send(forward, True), self.send(backward, False)
            yield
            forward, backward = self.clock(forward, backward)
        return forward, backward, piece(self.me)


class Line:
    def __init__(self, count, clock):
        self.count = count
        self.clock = clock
        self.me = lax.axis_index("z")
        order = list(range(0, count, 2)) + list(range(1, count, 2))[::-1]
        self.cycle = [(order[i], order[(i + 1) % count]) for i in range(count)]
        evens = (count + 1) // 2
        place = jnp.where(self.me % 2 == 0, self.me // 2, count - 1 - self.me // 2)
        self.at = []
        for k in range(count):
            spot = lax.rem(place + k, count)
            self.at.append(jnp.where(spot < evens, 2 * spot, 2 * (count - 1 - spot) + 1))

    def ahead(self, k):
        return self.at[k % self.count]

    def gather(self, block, axis):
        size = block.shape[axis]
        shape = list(block.shape)
        shape[axis] = size * self.count
        moved = self.clock.hold(block)
        pieces = [moved]
        for _ in range(1, self.count):
            moved = lax.ppermute(moved, "z", self.cycle)
            yield
            moved = self.clock(moved)
            pieces.append(moved)
        where = [
            [(i, size) if d == axis else None for d in range(2)] for i in range(len(pieces))
        ]
        return assemble(pieces, shape, where, [self.ahead(-k) for k in range(self.count)])

    def scatter(self, *parts):
        rows, width = parts[0].shape[0] // self.count, parts[0].shape[1]
        parts = self.clock.hold(*parts)

        def pieces(owner):
            return [cut(part, (owner * rows, 0), (rows, width)) for part in parts]

        moved = self.clock(add_up(*pieces(self.ahead(-1))))
        for k in range(self.count - 1, 0, -1):
            moved = lax.ppermute(moved, "z", self.cycle)
            yield
            moved = self.clock(moved)
            if k > 1:
                moved = self.clock(add_up(moved, *pieces(self.ahead(k - 1))))
        return moved, *pieces(self.me)


def shifts(count):
    return [[(i, (i + step) % count) for i in range(count)] for step in range(1, count)]


def from_axis(value, axis, count):
    me = lax.axis_index(axis)
    return [
        (lax.ppermute(value, axis, pairs), lax.rem(me - step + count, count))
        for step, pairs in enumerate(shifts(count), 1)
    ]


def to_axis(values, axis, count, dim):
    me = lax.axis_index(axis)
    return [
        lax.ppermute(
            lax.dynamic_index_in_dim(values, lax.rem(me + step, count), dim, False), axis, pairs
        )
        for step, pairs in enumerate(shifts(count), 1)
    ]


def in_order(found, axis, count, dim):
    me = lax.axis_index(axis)
    wide = jnp.stack((found[::-1] * 2)[:-1], axis=dim)
    where, sizes = [0] * wide.ndim, list(wide.shape)
    where[dim], sizes[dim] = count - 1 - me, count
    return cut(wide, where, sizes)


def exchange(values, axis, count, dim, clock):
    arrived = to_axis(values, axis, count, dim)
    yield
    found = [own_part(values, axis, dim)] + [clock(value) for value in arrived]
    return in_order(found, axis, count, dim)


def own_part(values, axis, dim):
    return lax.dynamic_index_in_dim(values, lax.axis_index(axis), dim, False)


def add_up(own, *others):
    total = own.astype(f32)
    for other in others:
        total = total + other.astype(f32)
    return total.astype(bf16)


class Grid:
    def __init__(self, nx, ny, clock):
        self.nx, self.ny, self.clock = nx, ny, clock
        self.x, self.y = lax.axis_index("x"), lax.axis_index("y")

    def gather(self, block, apart):
        rows, deep, width = block.shape
        half = rows // 2
        block = self.clock.hold(block)
        along_x, along_y = from_axis(block, "x", self.nx), from_axis(block, "y", self.ny)
        yield
        values = self.clock(*[v for v, _ in along_x + along_y])
        along_x, along_y = values[: self.nx - 1], values[self.nx - 1 :]
        left = [[w for w, _ in from_axis(v[:half], "y", self.ny)] for v in along_x]
        right = [[w for w, _ in from_axis(v[half:], "x", self.nx)] for v in along_y]
        yield
        owners = [lax.rem(self.y - k + self.ny, self.ny) for k in range(self.ny)]
        everything = slice(None)
        found = [([block, *along_y], [(everything, k) for k in range(self.ny)])]
        for i, value in enumerate(along_x):
            pieces, where = [value], [(everything, 0)]
            for j in range(self.ny - 1):
                pieces += self.clock(left[i][j], right[j][i])
                where += [(slice(0, half), j + 1), (slice(half, rows), j + 1)]
            found.append((pieces, where))
        size = rows * self.ny * deep
        if apart:
            return [
                assemble(
                    pieces,
                    (rows, self.ny, deep, width),
                    [[span, (k, None), None, None] for span, k in where],
                    owners,
                ).reshape(size, width)
                for pieces, where in found
            ]
        return assemble(
            [piece for pieces, _ in found for piece in pieces],
            (self.nx, rows, self.ny, deep, width),
            [
                [i, span, (k, None), None, None]
                for i, (_, where) in enumerate(found)
                for span, k in where
            ],
            owners,
        ).reshape(self.nx * size, width)

    def send(self, values, i, j):
        nx, ny = self.nx, self.ny
        pairs = [
            (x * ny + y, (x + i) % nx * ny + (y + j) % ny) for x in range(nx) for y in range(ny)
        ]
        return lax.ppermute(values, ("x", "y"), pairs)

    def place(self, k):
        return lax.rem(self.x - k + self.nx, self.nx)

    def turn(self, values):
        half = values.shape[1] // self.nx
        wide = jnp.concatenate([values, values], axis=1)
        found = [
            cut(wide, (0, self.place(k) * half), (values.shape[0], half)) for k in range(self.nx)
        ]
        return jnp.concatenate(found, axis=1)

    def turn_back(self, values):
        return self.turn(values)

    def scatter(self, x_first, y_first, rows):
        nx, ny = self.nx, self.ny
        count = len(x_first)
        values = self.clock.hold(*x_first, *y_first)
        values = [v.reshape(nx, rows, ny, -1, v.shape[1]) for v in values]
        one, two = values[:count], values[count:]

        def x_blocks(values):
            return [values[k] for k in range(1, nx)]

        def send_x(blocks):
            return [
                lax.ppermute(block, "x", [(i, (i - k) % nx) for i in range(nx)])
                for k, block in enumerate(blocks, 1)
            ]

        def y_blocks(values, dim):
            return [
                lax.dynamic_index_in_dim(values, lax.rem(self.y + step, ny), dim, False)
                for step in range(1, ny)
            ]

        def send_y(blocks):
            return [lax.ppermute(block, "y", pairs) for block, pairs in zip(blocks, shifts(ny))]

        def exchange_all(x_arrays, y_arrays, dim):
            groups = [x_blocks(v) for v in x_arrays] + [y_blocks(v, dim) for v in y_arrays]
            flat = self.clock(*[block for group in groups for block in group])
            flat = list(flat) if isinstance(flat, (tuple, list)) else [flat]
            groups = [[flat.pop(0) for _ in group] for group in groups]
            count = len(x_arrays)
            return [send_x(g) for g in groups[:count]] + [send_y(g) for g in groups[count:]]

        sent = exchange_all(one, two, 2)
        yield
        sent = [[self.clock(v) for v in group] for group in sent]
        one = [add_up(v[0], *group) for v, group in zip(one, sent)]
        two = [add_up(own_part(v, "y", 2), *group) for v, group in zip(two, sent[count:])]
        values = self.clock(*one, *two)
        one, two = values[:count], values[count:]
        sent = exchange_all(two, one, 1)
        yield
        sent = [[self.clock(v) for v in group] for group in sent]
        back = len(two)
        one = [add_up(own_part(v, "y", 1), *group) for v, group in zip(one, sent[back:])]
        two = [add_up(v[0], *group) for v, group in zip(two, sent[:back])]
        return jnp.concatenate([*one, *two], axis=2)


def sum_everywhere(values, sizes, clock):
    values = clock.hold(values)
    for axis, count in sizes:
        if count & (count - 1):
            values = lax.psum(values, axis)
            continue
        step = 1
        while step < count:
            other = lax.ppermute(values, axis, [(i, i ^ step) for i in range(count)])
            yield
            values = values + clock(other)
            step *= 2
    return values


def allowed_keys(low_ref, high_ref, shape):
    places = lax.broadcasted_iota(jnp.int32, shape, 1)
    return (places >= low_ref[...]) & (places < high_ref[...])


def forward_kernel(q_ref, k_ref, v_ref, low_ref, high_ref, out_ref, lse_ref):
    scores = dot_nt(q_ref[...], k_ref[...]) * (HEAD**-0.5 * log2_e)
    allowed = allowed_keys(low_ref, high_ref, scores.shape)
    scores = jnp.where(allowed, scores, masked_value)
    largest = jnp.max(scores, axis=1, keepdims=True)
    powers = jnp.exp2(scores - largest)
    totals = jnp.sum(powers, axis=1, keepdims=True)
    probs = (powers * (1.0 / totals)).astype(bf16)
    out_ref[...] = dot_nn(probs, v_ref[...]).astype(bf16)
    lse_ref[0] = largest + jnp.log2(totals)


def backward_kernel(
    q_ref, k_ref, v_ref, g_ref, low_ref, high_ref, lse_ref, cos_ref, sin_ref, all_cos_ref, all_sin_ref,
    gq_ref, gk_ref, gv_ref, k_sum, v_sum,
):
    scale = HEAD**-0.5
    step = pl.program_id(1)

    @pl.when(step == 0)
    def _():
        k_sum[...] = jnp.zeros_like(k_sum)
        v_sum[...] = jnp.zeros_like(v_sum)

    scores = dot_nt(q_ref[...], k_ref[...]) * (scale * log2_e)
    allowed = allowed_keys(low_ref, high_ref, scores.shape)
    probs = jnp.where(allowed, jnp.exp2(scores - lse_ref[0]), 0.0)
    grad_probs = dot_nt(g_ref[...], v_ref[...])
    delta = jnp.sum(probs * grad_probs, axis=1, keepdims=True)
    grad_scores = (probs * (grad_probs - delta)).astype(bf16)
    grad_q = (dot_nn(grad_scores, k_ref[...]) * scale).astype(bf16).astype(f32)
    gq_ref[...] = rotate_back(grad_q, cos_ref[...], sin_ref[...]).astype(bf16)
    k_sum[...] += dot_tn(grad_scores, q_ref[...])
    v_sum[...] += dot_tn(probs.astype(bf16), g_ref[...])

    @pl.when(step == pl.num_programs(1) - 1)
    def _():
        grad_k = (k_sum[...] * scale).astype(bf16).astype(f32)
        gk_ref[...] = rotate_back(grad_k, all_cos_ref[...], all_sin_ref[...]).astype(bf16)
        gv_ref[...] = v_sum[...].astype(bf16)


params = pltpu.CompilerParams(vmem_limit_bytes=56 * 2**20)
cost = pl.CostEstimate(flops=0, bytes_accessed=0, transcendentals=0)


def assemble(pieces, shape, where, places):
    def kernel(places_ref, *refs):
        out, arrived = refs[len(pieces)], refs[-1]

        def index(part):
            if not isinstance(part, tuple):
                return slice(None) if part is None else part
            k, size = part
            if size is None:
                return places_ref[k]
            return pl.ds(pl.multiple_of(places_ref[k] * size, size), size)

        copies = [
            pltpu.make_async_copy(refs[i], out.at[tuple(map(index, parts))], arrived.at[i])
            for i, parts in enumerate(where)
        ]
        for copy in copies:
            copy.start()
        for copy in copies:
            copy.wait()

    return pl.pallas_call(
        kernel,
        grid_spec=pltpu.PrefetchScalarGridSpec(
            num_scalar_prefetch=1,
            grid=(1,),
            in_specs=[pl.BlockSpec(memory_space=pl.ANY)] * len(pieces),
            out_specs=pl.BlockSpec(tuple(shape), lambda i, places: (0,) * len(shape)),
            scratch_shapes=[pltpu.SemaphoreType.DMA((len(pieces),))],
        ),
        out_shape=jax.ShapeDtypeStruct(tuple(shape), pieces[0].dtype),
        compiler_params=params,
        cost_estimate=cost,
        name="assemble",
    )(jnp.stack(places).astype(jnp.int32), *pieces)


def lay_out(name, pieces, shape, kind, where, places=None):
    places = jnp.zeros((1,), jnp.int32) if places is None else places

    def kernel(places_ref, *refs):
        out = refs[-1]
        out[...] = jnp.zeros_like(out)
        for i, part, columns in where:
            value = refs[i][part].astype(kind)
            if isinstance(columns, list):
                place, start = columns
                size = value.shape[-1]
                begin = pl.multiple_of(places_ref[place] + start, LANES)
                out[:, pl.ds(begin, size)] = value
            else:
                out[:, columns : columns + value.shape[-1]] = value

    return pl.pallas_call(
        kernel,
        grid_spec=pltpu.PrefetchScalarGridSpec(
            num_scalar_prefetch=1,
            grid=(1,),
            in_specs=[
                pl.BlockSpec(a.shape, lambda i, places, n=a.ndim: (0,) * n) for a in pieces
            ],
            out_specs=pl.BlockSpec(shape, lambda i, places: (0, 0)),
        ),
        out_shape=jax.ShapeDtypeStruct(shape, kind),
        compiler_params=params,
        cost_estimate=cost,
        name=name,
    )(places, *pieces)


def attention_specs(count, heads, block):
    def one(column):
        return pl.BlockSpec((block, HEAD), lambda h, i: (i, column + h))

    def whole(column):
        return pl.BlockSpec((count, HEAD), lambda h, i: (0, column + h))

    edge = pl.BlockSpec((block, 1), lambda h, i: (i, 0))
    lse = pl.BlockSpec((1, block, 1), lambda h, i: (h, i, 0))
    return (one, whole, edge, lse)


def attend_forward(packed, low, high):
    count, heads = packed.shape[0], packed.shape[1] // (3 * HEAD)
    block = min(512, count)
    one, whole, edge, lse = attention_specs(count, heads, block)
    return pl.pallas_call(
        forward_kernel,
        grid=(heads, count // block),
        in_specs=[one(0), whole(heads), whole(2 * heads), edge, edge],
        out_specs=[one(0), lse],
        out_shape=[
            jax.ShapeDtypeStruct((count, heads * HEAD), bf16),
            jax.ShapeDtypeStruct((heads, count, 1), f32),
        ],
        compiler_params=params,
        cost_estimate=cost,
        name="attend_forward",
    )(packed, packed, packed, low, high)


def attend_backward(packed, grads, low, high, log_sums, cosine, sine):
    count, heads = packed.shape[0], packed.shape[1] // (3 * HEAD)
    block = min(512, count)
    one, whole, edge, lse = attention_specs(count, heads, block)
    shape = jax.ShapeDtypeStruct((count, heads * HEAD), bf16)
    turn = pl.BlockSpec((block, HEAD), lambda h, i: (i, 0))
    turn_all = pl.BlockSpec((count, HEAD), lambda h, i: (0, 0))
    return pl.pallas_call(
        backward_kernel,
        grid=(heads, count // block),
        in_specs=[one(0), whole(heads), whole(2 * heads), one(0), edge, edge, lse]
        + [turn, turn, turn_all, turn_all],
        out_specs=[one(0), whole(0), whole(0)],
        out_shape=[shape, shape, shape],
        scratch_shapes=[pltpu.VMEM((count, HEAD), f32), pltpu.VMEM((count, HEAD), f32)],
        compiler_params=params,
        cost_estimate=cost,
        name="attend_backward",
    )(packed, packed, packed, grads, low, high, log_sums, cosine, sine, cosine, sine)


def over_rows(
    name, body, block, rows, whole, outs, sums=(), places=None, scratch=(), first_map=None, count=None
):
    count = count or rows[-1].shape[0]
    places = jnp.zeros((1,), jnp.int32) if places is None else places

    def kernel(places_ref, *refs):
        n, m, k = len(rows), len(rows) + len(whole), len(rows) + len(whole) + len(outs)
        if sums:

            @pl.when(pl.program_id(0) == 0)
            def _():
                for ref in refs[k : k + len(sums)]:
                    ref[...] = jnp.zeros_like(ref)

        body(refs[:n], refs[n:m], places_ref, refs[m:k], refs[k:])

    room = [pltpu.VMEM((block, width), kind) for width, kind in scratch]

    def by_row(i, places):
        return (i, 0)

    def fixed(i, places):
        return (0, 0)

    return pl.pallas_call(
        kernel,
        grid_spec=pltpu.PrefetchScalarGridSpec(
            num_scalar_prefetch=1,
            grid=(count // block,),
            in_specs=[
                pl.BlockSpec((block, a.shape[1]), first_map if first_map and not i else by_row)
                for i, a in enumerate(rows)
            ]
            + [pl.BlockSpec(a.shape, fixed) for a in whole],
            out_specs=[pl.BlockSpec((block, width), by_row) for width, _ in outs]
            + [pl.BlockSpec((1, width), fixed) for width in sums],
            scratch_shapes=room,
        ),
        out_shape=[jax.ShapeDtypeStruct((count, width), kind) for width, kind in outs]
        + [jax.ShapeDtypeStruct((1, width), f32) for width in sums],
        compiler_params=params,
        cost_estimate=cost,
        name=name,
    )(places, *rows, *whole)


def columns_of(ref, place, width):
    return ref.at[:, pl.ds(pl.multiple_of(place * width, width), width)]


def project_pieces(left_ref, pieces, places_ref):
    total = None
    for i, piece in enumerate(pieces):
        depth = piece.shape[0]
        term = dot_nn(columns_of(left_ref, places_ref[i], depth)[...], piece[...])
        total = term if total is None else total + term
    return total


def tile_split(width, count):
    tiles = -(-width // LANES)
    least, extra = divmod(tiles, count)
    sizes = [least + (1 if i < extra else 0) for i in range(count)]
    starts = [sum(sizes[:i]) for i in range(count)]
    return (starts, sizes, max(sizes))


class Values:
    pass


ORDER = (
    "tokens_in", "qkv_in", "tokens_in", "gate_up_pack", "tokens_in", "down_pack", "qkv_in", "out_in",
    "tokens_in", "tables", "turn", "qkv_in", "tokens_in", "out_in", "gate_up_in", "qkv_in", "project",
    "out_grad_in", "attend", "to_y", "out_grad_in", "to_y", "attended_in", "out_in", "attended_in",
    "gate_up_in", "out_grad_in", "out_in", "attended_in", "out_in", "down_in", "attended_in", "out_grad_in",
    "gate_up_in", "second_norm", "normed_core", "gate_up_in", "down_in", "down_in", "normed_core",
    "out_grad_core", "gate_up", "down_in", "out_grad_core", "down_in", "act", "other_parts", "own_parts",
    "other_parts", "parts_out", "first_share", "second_share", "ffn_grad", "parts_out", "parts_out",
    "ffn_grad", "parts_out", "second_back", "heads_in", "ffn_grad", "heads_in", "ffn_back", "grad_attn_in",
    "attend_back", "qkv_back", "first_back", "normed_out", "qkv_back", "small", "ffn_back", "normed_out",
    "qkv_back", "small", "ffn_rows", "normed_out", "grad_attn_in", "out_back", "small", "normed_out",
    "out_back", "small", "qkv_back", "qkv_rows", "normed_out", "out_back", "small", "output",
    "first_norm_tokens", "small", "out_back", "out_rows",
)


def per_device(
    tokens,
    ln1_gain,
    ln1_bias,
    w_qkv,
    b_qkv,
    w_out,
    b_out,
    ln2_gain,
    ln2_bias,
    w_gate,
    b_gate,
    w_up,
    b_up,
    w_down,
    b_down,
    protein_lengths,
    prefix_lengths,
    out_grad,
):
    nx, nz, ny = (lax.axis_size(axis) for axis in ("x", "z", "y"))
    x, core, z, y = (lax.axis_index(axis) for axis in EVERY)
    sizes_of = (("core", 2), ("x", nx), ("y", ny), ("z", nz))
    own_rows, width = tokens.shape
    weight_rows = w_qkv.shape[0]
    ffn_width = w_gate.shape[1]
    seq_count, team_count = nz * ny, 2 * nz
    count = own_rows * seq_count
    line_rows = nz * own_rows
    own_heads = HEADS // seq_count
    own_width = own_heads * HEAD
    clock = Clock()
    ring = Ring(nz, ny, clock)
    line = Line(nz, clock)
    grid = Grid(nx, ny, clock)
    me = ring.me

    def all_to_all(values, axes):
        return lax.all_to_all(values, axes, split_axis=0, concat_axis=0, tiled=True)

    def other_core(values):
        return lax.ppermute(values, "core", [(0, 1), (1, 0)])

    starts, sizes, most = tile_split(ffn_width, team_count)
    own_ffn = most * LANES
    padded = (starts[-1] + most) * LANES
    first_tile = jnp.asarray(starts, jnp.int32)[core * nz + z] * LANES
    split = 3 * own_ffn // 2 // LANES * LANES
    half_places = jnp.stack([lax.rem(x - k + nx, nx) for k in range(nx)])
    places = jnp.concatenate([half_places * 2 + core, half_places * 2 + 1 - core])
    cotangent = out_grad.astype(f32)
    pieces_of = PIECES if PIECES % nx == 0 else nx
    piece_width = width // pieces_of
    plan = Plan()
    v = Values()

    def ffn_blocks(weight, mask):
        whole = jnp.pad(weight, ((0, 0), (0, padded - ffn_width)))
        pieces = []
        for start, size in zip(starts, sizes):
            piece = whole[:, start * LANES : (start + most) * LANES]
            if mask and size < most:
                piece = jnp.pad(piece[:, : size * LANES], ((0, 0), (0, (most - size) * LANES)))
            pieces.append(piece)
        return jnp.stack(pieces)

    def ffn_bias(bias):
        return cut(jnp.pad(bias, (0, padded - ffn_width)), (first_tile,), (own_ffn,))

    def row(values):
        return values.reshape(1, -1)

    def low_nt(left, right):
        return dot_nt(left, right).astype(bf16)

    def low_tn(left, right):
        return dot_tn(left, right).astype(bf16)

    @plan.transfer
    def tokens_in():
        v.tokens_all = clock((yield from ring.gather(tokens)))

    @plan.transfer
    def qkv_in():
        blocks = (
            w_qkv.reshape(weight_rows, 3, seq_count, own_width)
            .transpose(2, 0, 1, 3)
            .reshape(seq_count, weight_rows, 3 * own_width)
        )
        moved = all_to_all(clock.hold(blocks), GROUP)
        yield
        rows = clock(moved).reshape(seq_count * weight_rows, 3 * own_width)
        from_x = from_axis(rows, "x", nx)
        yield
        pieces = [rows] + [clock(value) for value, _ in from_x]
        from_core = [other_core(value) for value in pieces]
        yield
        v.qkv_pieces = pieces + [clock(value) for value in from_core]

    @plan.transfer
    def out_in():
        block = jnp.broadcast_to(w_out[None], (nz, weight_rows, width))
        moved = all_to_all(clock.hold(block), "z")
        yield
        pieces = yield from grid.gather(clock(moved), True)
        pieces = list(clock(*pieces))
        from_core = [other_core(piece) for piece in pieces]
        yield
        v.out_pieces = pieces + [clock(value) for value in from_core]

    @plan.step
    def gate_up_pack():
        v.gate_up_blocks = clock.run(
            lambda gate, up: jnp.concatenate(
                [ffn_blocks(gate, False), ffn_blocks(up, False)], axis=2
            ),
            w_gate,
            w_up,
        )

    @plan.step
    def down_pack():
        v.down_blocks = clock.run(lambda down: ffn_blocks(down, True), w_down)

    @plan.transfer
    def gate_up_in():
        moved = all_to_all(clock.hold(v.gate_up_blocks), TEAM)
        yield
        v.gate_up_own = clock((yield from grid.gather(clock(moved), False)))

    @plan.transfer
    def down_in():
        moved = all_to_all(clock.hold(v.down_blocks), TEAM)
        yield
        v.down_moved = clock(moved)
        yield
        v.down_own = clock((yield from grid.gather(v.down_moved, False)))

    @plan.step
    def tables():
        def make(lengths, prefixes):
            position, low, high = group_layout(lengths[0], prefixes[0], count)
            return (*rotary_tables(position), low[:, None], high[:, None])

        v.cosine, v.sine, v.low, v.high = clock.run(make, protein_lengths, prefix_lengths)

    def project_kernel(rows, whole, places_ref, outs, sums):
        tokens_ref, cos_ref, sin_ref = rows
        gain, bias, qkv_bias, *pieces = whole
        normed_ref, packed_ref = outs
        normed = layer_norm(tokens_ref[...].astype(f32), gain[...], bias[...])
        normed_ref[...] = normed.astype(bf16)
        raw = project_pieces(normed_ref, pieces, places_ref) + qkv_bias[...]
        for i in range(3 * own_heads):
            piece = raw[:, i * HEAD : (i + 1) * HEAD]
            if i < 2 * own_heads:
                piece = rotate(piece, cos_ref[...], sin_ref[...])
            packed_ref[:, i * HEAD : (i + 1) * HEAD] = piece.astype(bf16)

    @plan.step
    def project():
        qkv_bias = cut(b_qkv.reshape(3, width), (0, me * own_width), (3, own_width))
        v.normed, v.packed = clock.run(
            lambda tokens_all, *pieces: over_rows(
                "project",
                project_kernel,
                256,
                [tokens_all, v.cosine, v.sine],
                [row(ln1_gain), row(ln1_bias), row(qkv_bias), *pieces],
                [(width, bf16), (3 * own_width, bf16)],
                places=places,
            ),
            v.tokens_all,
            *v.qkv_pieces,
        )

    @plan.step
    def attend():
        v.head_result, v.log_sums = clock.run(
            lambda values: attend_forward(values, v.low, v.high), v.packed
        )

    @plan.transfer
    def to_y():
        result = v.head_result.reshape(nz, ny, own_rows, own_width)
        moved = yield from exchange(result, "y", ny, 1, clock)
        moved = moved.transpose(0, 2, 1, 3).reshape(line_rows, ny * own_width)
        v.head_columns = clock(moved)

    @plan.transfer
    def attended_in():
        v.attended = clock((yield from line.gather(v.head_columns, 1)))

    @plan.step
    def turn():
        v.out_grad_turned = clock.run(grid.turn, out_grad)

    @plan.transfer
    def out_grad_in():
        found = yield from line.gather(v.out_grad_turned, 0)
        v.grad_out_line = clock(found)

    @plan.transfer
    def out_grad_core():
        moved = other_core(v.grad_out_line)
        yield
        both = [v.grad_out_line, clock(moved)]
        v.grad_out_all = clock(jnp.concatenate(both, axis=0))

    def second_kernel(rows, whole, places_ref, outs, more):
        tokens_ref, attended_ref = rows
        gain, bias, out_bias, *pieces = whole
        attn = project_pieces(attended_ref, pieces, places_ref) + out_bias[...]
        hidden = tokens_ref[...].astype(f32) + attn
        outs[0][...] = hidden
        (normed_ref,) = more
        normed_ref[...] = layer_norm(hidden, gain[...], bias[...]).astype(bf16)
        for k in range(nx):
            place = places_ref[2 * nx + k]
            whole = columns_of(normed_ref, place, width // nx)
            for j in range(pieces_of // nx):
                out = outs[1 + k * (pieces_of // nx) + j]
                out[...] = whole[:, j * piece_width : (j + 1) * piece_width]

    @plan.step
    def second_norm():
        hidden_in, *v.normed_line = clock.run(
            lambda tokens, attended, *pieces: over_rows(
                "second_norm",
                second_kernel,
                own_rows,
                [tokens, attended],
                [row(ln2_gain), row(ln2_bias), row(b_out), *pieces],
                [(width, f32)] + [(piece_width, bf16)] * pieces_of,
                places=jnp.concatenate([places, half_places, row(y)[0]]),
                scratch=[(width, bf16)],
                first_map=lambda i, places: (i * ny + places[3 * nx], 0),
                count=line_rows,
            ),
            v.tokens_all,
            v.attended,
            *v.out_pieces,
        )
        v.hidden_own = cut(hidden_in, (z * own_rows, 0), (own_rows, width))

    @plan.transfer
    def normed_core():
        moved = [other_core(piece) for piece in v.normed_line]
        yield
        moved = clock(*moved)
        where = [
            [slice(j * line_rows, (j + 1) * line_rows), slice(i * piece_width, (i + 1) * piece_width)]
            for j in range(2)
            for i in range(pieces_of)
        ]
        v.normed_two = clock(
            assemble([*v.normed_line, *moved], (2 * line_rows, width), where, [me])
        )

    @plan.step
    def gate_up():
        bias = jnp.concatenate([ffn_bias(b_gate), ffn_bias(b_up)])
        v.gate_up = clock.run(lambda a, b: dot_nn(a, b) + bias, v.normed_two, v.gate_up_own)

    @plan.step
    def act():
        def make(grads, weight, gate_up):
            grad_act = dot_nn(grads, weight)
            values, pull = jax.vjp(geglu, gate_up[:, :own_ffn], gate_up[:, own_ffn:])
            grads = [g.astype(bf16) for g in pull(grad_act)]
            return jnp.concatenate(grads, axis=1), values.astype(bf16)

        v.grad_gate_up, v.act = clock.run(make, v.grad_out_all, v.down_own, v.gate_up)

    def both_parts(grads, gate_up, act, down):
        return jnp.concatenate([low_nt(grads, gate_up), low_nt(act, down)], axis=1)

    @plan.transfer
    def other_parts():
        found = clock.run(
            both_parts, v.grad_gate_up[line_rows:], v.gate_up_own, v.act[line_rows:], v.down_own
        )
        moved = other_core(found)
        yield
        v.other_parts = clock(moved)

    @plan.step
    def own_parts():
        v.own_parts = clock.run(
            both_parts, v.grad_gate_up[:line_rows], v.gate_up_own, v.act[:line_rows], v.down_own
        )

    @plan.transfer
    def parts_out():
        v.two_parts = yield from line.scatter(v.own_parts, v.other_parts)

    @plan.step
    def first_share():
        v.first_share = clock.run(low_tn, v.normed_two, v.grad_gate_up[:, :split])

    @plan.step
    def second_share():
        v.second_share, v.third_share = clock.run(
            lambda a, b, c, d: (low_tn(a, b[:, split:]), low_tn(c, d)),
            v.normed_two,
            v.grad_gate_up,
            v.grad_out_all,
            v.act,
        )

    @plan.transfer
    def ffn_grad():
        found = yield from grid.scatter(
            [v.first_share], [v.second_share, v.third_share], team_count
        )
        v.ffn_share = clock(found)

    @plan.transfer
    def ffn_back():
        moved = all_to_all(clock.hold(v.ffn_share), TEAM)
        yield
        v.ffn_back = clock(moved)

    def second_back_kernel(rows, whole, places_ref, outs, more):
        *sums, grads_ref = more
        *terms, hidden, out_grad_ref = rows
        gain, *pieces = whole
        turned = sum(term[:, :width].astype(f32) for term in terms)
        part = width // nx
        for k in range(nx):
            place = places_ref[2 * nx + k]
            columns_of(grads_ref, place, part)[...] = turned[:, k * part : (k + 1) * part]
        grads = grads_ref[...]
        unit, inverse = norm_parts(hidden[...])
        cotangent = out_grad_ref[...].astype(f32)
        total = cotangent + layer_norm_back(unit, inverse, gain[...], grads)
        low = total.astype(bf16)
        outs[0][...] = total
        outs[1][...] = low
        for i, piece in enumerate(pieces):
            part = dot_nt(low, piece[...]).astype(bf16)
            columns_of(outs[2], places_ref[i], piece.shape[0])[...] = part
        for ref, values in zip(sums, (grads * unit, grads, low.astype(f32), cotangent)):
            ref[...] += jnp.sum(values, axis=0, keepdims=True)

    @plan.step
    def second_back():
        v.grad_hidden, v.grad_attn, v.grad_attended, *v.second_sums = clock.run(
            lambda *values: over_rows(
                "second_norm_back",
                second_back_kernel,
                own_rows,
                values[:5],
                [row(ln2_gain), *values[5:]],
                [(width, f32), (width, bf16), (width, bf16)],
                [width] * 4,
                places=jnp.concatenate([places, half_places]),
                scratch=[(width, f32)],
            ),
            *v.two_parts,
            v.hidden_own,
            out_grad,
            *v.out_pieces,
        )

    @plan.transfer
    def heads_in():
        blocks = v.grad_attended.reshape(own_rows, seq_count, own_width).transpose(1, 0, 2)
        moved = all_to_all(clock.hold(blocks), GROUP)
        yield
        v.grad_heads = clock(moved).reshape(count, own_width)

    @plan.step
    def attend_back():
        v.grad_parts = clock.run(
            lambda *values: attend_backward(*values, v.low, v.high, v.log_sums, v.cosine, v.sine),
            v.packed,
            v.grad_heads,
        )

    def first_back_kernel(rows, whole, places_ref, outs, more):
        *sums, part_ref = more
        grads, tokens_ref = rows[:3], rows[3]
        unit, _ = norm_parts(tokens_ref[...].astype(f32))
        for i, piece in enumerate(whole):
            part = None
            for j, grad in enumerate(grads):
                term = dot_nt(grad[...], piece[:, j * own_width : (j + 1) * own_width])
                part = term if part is None else part + term
            depth = piece.shape[0]
            columns_of(outs[0], places_ref[i], depth)[...] = part.astype(bf16)
            columns_of(part_ref, places_ref[i], depth)[...] = part
        part = part_ref[...]
        sums[0][...] += jnp.sum(part * unit, axis=0, keepdims=True)
        sums[1][...] += jnp.sum(part, axis=0, keepdims=True)
        for j, grad in enumerate(grads):
            total = jnp.sum(grad[...].astype(f32), axis=0, keepdims=True)
            sums[2][:, j * own_width : (j + 1) * own_width] += total

    @plan.step
    def first_back():
        v.normed_part, *v.first_sums = clock.run(
            lambda *values: over_rows(
                "first_norm_back",
                first_back_kernel,
                256,
                values[:4],
                values[4:],
                [(width, bf16)],
                [width, width, 3 * own_width],
                places=places,
                scratch=[(width, f32)],
            ),
            *v.grad_parts,
            v.tokens_all,
            *v.qkv_pieces,
        )

    @plan.transfer
    def normed_out():
        v.one_parts = yield from ring.scatter(v.normed_part)

    @plan.transfer
    def small():
        sums = [*v.second_sums, *v.first_sums[:2]]
        bias_gate_up = jnp.sum(v.grad_gate_up.astype(f32), axis=0, keepdims=True)
        where = [(i, (slice(None), slice(None)), i * width) for i in range(len(sums))]
        start = len(sums) * width
        for i in range(3):
            part = (slice(None), slice(i * own_width, (i + 1) * own_width))
            where.append((len(sums), part, [0, start + i * width]))
        start += 3 * width
        for i in range(2):
            part = (slice(None), slice(i * own_ffn, (i + 1) * own_ffn))
            where.append((len(sums) + 1, part, [1, start + i * padded]))
        values = clock.run(
            lambda *values: lay_out(
                "small",
                values,
                (1, start + 2 * padded),
                f32,
                where,
                jnp.stack([me * own_width, first_tile]).astype(jnp.int32),
            ),
            *sums,
            v.first_sums[2],
            bias_gate_up,
        )
        v.small = (yield from sum_everywhere(values, sizes_of, clock))[0]

    @plan.transfer
    def qkv_back():
        share = clock.run(
            lambda a, *b: low_tn(a, jnp.concatenate(b, axis=1)), v.normed, *v.grad_parts
        )
        share = share.reshape(nx, 2, seq_count * weight_rows, 3 * own_width)
        for axis, size, dim in (("core", 2, 1), ("x", nx, 0)):
            arrived = to_axis(share, axis, size, dim)
            yield
            share = clock(add_up(own_part(share, axis, dim), *[clock(a) for a in arrived]))
        moved = all_to_all(share.reshape(seq_count, weight_rows, 3 * own_width), GROUP)
        yield
        v.qkv_back = clock(moved)

    @plan.transfer
    def grad_attn_in():
        blocks = clock.hold(v.grad_attn).reshape(own_rows, nz, width // nz).transpose(1, 0, 2)
        found = yield from exchange(blocks, "z", nz, 0, clock)
        v.grad_attn_block = clock(found).reshape(line_rows, width // nz)

    @plan.transfer
    def out_back():
        share = clock.run(low_tn, v.attended, v.grad_attn_block)
        share = share.reshape(nx, 2, nz, ny, weight_rows, width // nz)
        arrived = to_axis(share, "core", 2, 1)
        yield
        share = clock(add_up(own_part(share, "core", 1), *[clock(a) for a in arrived]))

        def part_of(i, j):
            where = (lax.rem(x + i, nx), 0, lax.rem(y + j, ny), 0, 0)
            found = cut(share, where, (1, nz, 1, weight_rows, width // nz))
            return found.reshape(nz, weight_rows, width // nz)

        others = [(i, j) for i in range(nx) for j in range(ny) if i or j]
        arrived = [grid.send(part_of(i, j), i, j) for i, j in others]
        yield
        share = clock(add_up(part_of(0, 0), *[clock(a) for a in arrived]))
        v.out_back = yield from exchange(share, "z", nz, 0, clock)

    @plan.step
    def output():
        v.output = clock.run(
            lambda hidden, *terms: (
                grid.turn_back(sum(term[:, width:].astype(f32) for term in terms))
                + hidden
                + b_down
            ).astype(bf16),
            v.hidden_own,
            *v.two_parts,
        )

    def last_kernel(rows, whole, places_ref, outs, sums):
        below, above, own, tokens_ref, hidden_grad = rows
        grads = below[...].astype(f32) + above[...].astype(f32) + own[...]
        unit, inverse = norm_parts(tokens_ref[...].astype(f32))
        total = hidden_grad[...] + layer_norm_back(unit, inverse, whole[0][...], grads)
        outs[0][...] = total.astype(bf16)

    @plan.step
    def first_norm_tokens():
        v.tokens_grad = clock.run(
            lambda *values: over_rows(
                "first_norm_tokens",
                last_kernel,
                own_rows,
                values,
                [row(ln1_gain)],
                [(width, bf16)],
            )[0],
            *v.one_parts,
            tokens,
            v.grad_hidden,
        )

    @plan.step
    def ffn_rows():
        def rows_of(moved, which):
            everything = slice(None)
            where = []
            for i in range(team_count):
                size = min(sizes[i] * LANES, ffn_width - starts[i] * LANES)
                span = slice(which * own_ffn, which * own_ffn + size)
                where.append((0, (i, everything, span), starts[i] * LANES))
            return lay_out("ffn_rows", [moved], (weight_rows, ffn_width), f32, where)

        v.ffn_rows = clock.run(lambda moved: [rows_of(moved, i) for i in range(3)], v.ffn_back)

    @plan.step
    def qkv_rows():
        everything = slice(None)
        where = [
            (0, (i, everything, slice(j * own_width, (j + 1) * own_width)), j * width + i * own_width)
            for i in range(seq_count)
            for j in range(3)
        ]
        v.qkv_rows = clock.run(
            lambda moved: lay_out("qkv_rows", [moved], (weight_rows, 3 * width), f32, where),
            v.qkv_back,
        )

    @plan.step
    def out_rows():
        everything = slice(None)
        where = [(0, (i, everything, everything), i * (width // nz)) for i in range(nz)]
        v.out_rows = clock.run(
            lambda moved: lay_out("out_rows", [moved], (weight_rows, width), f32, where),
            v.out_back,
        )

    plan.run(ORDER)


    gain_two, bias_two, b_out_grad, b_down_grad, gain_one, bias_one = (
        v.small[i * width : (i + 1) * width] for i in range(6)
    )
    b_qkv_grad = v.small[6 * width : 9 * width]
    b_gate_grad = v.small[9 * width : 9 * width + ffn_width]
    b_up_grad = v.small[9 * width + padded : 9 * width + padded + ffn_width]
    return (
        v.output,
        v.tokens_grad,
        gain_one,
        bias_one,
        v.qkv_rows,
        b_qkv_grad,
        v.out_rows,
        b_out_grad,
        gain_two,
        bias_two,
        v.ffn_rows[0],
        b_gate_grad,
        v.ffn_rows[1],
        b_up_grad,
        v.ffn_rows[2],
        b_down_grad,
    )


def solution(mesh):
    nx, seq_count = mesh.shape["batch"] // 2, mesh.shape["seq"]
    nz = 4 if seq_count % 4 == 0 else seq_count
    grid = Mesh(mesh.devices.reshape(nx, 2, nz, seq_count // nz), EVERY)
    rows = P(EVERY, None)
    lengths = P(("x", "core"), None)
    in_specs = (
        rows, P(), P(), rows, P(), rows, P(), P(), P(), rows, P(), rows, P(), rows, P(),
        lengths, lengths, rows,
    )
    out_specs = (
        rows, rows, P(), P(), rows, P(), rows, P(), P(), P(), rows, P(), rows, P(), rows, P(),
    )
    return jax.shard_map(
        per_device, mesh=grid, in_specs=in_specs, out_specs=out_specs, check_vma=False
    )
```
